32 devices in a mesh: group: 2 (over x), tp: 16 (over z, y, core).
Axes of the slice: x: 2, y: 2, z: 4, core: 2. Of those that a mesh axis runs over, the one named last changes fastest.
Arguments:
- hidden_states: bfloat16 [16, 2, 8192], P('group'), parts along dimension 0, may hold values from -6 to 6
- qkv_weight: bfloat16 [10240, 8192], P('tp'), may hold values from -0.0625 to 0.0625
- out_weight: bfloat16 [8192, 8192], P('tp'), may hold values from -0.0625 to 0.0625
- cache_pages: bfloat16 [2048, 128, 256], P(('group', 'tp')), parts along dimension 0, may hold values from -6 to 6
- context_lengths: int32 [16], P('group'), parts along dimension 0, may hold values from 1 to 2046, 8184 in all
- new_units: int32 [128], P('group'), parts along dimension 0, may hold values from 0 to 63, as said below
- old_pages: int32 [2048], P('group'), parts along dimension 0, may hold values from 0 to 1023, as said below
Outputs:
- mixed_out: bfloat16 [16, 2, 8192], P('group', None, 'tp'), parts along dimension 0
- cache_out: bfloat16 [2048, 128, 256], P(('group', 'tp')), parts along dimension 0
The draws below stay inside these ranges and needn't reach their ends.
There are 2 independent parts, one for each index of `group`. The reference program is written for one: setup_inputs(seed, part) draws one part's arguments, and reference() takes and returns one part's arrays. A program takes and returns all parts, laid end to end along the dimension named above; an argument that names none is the same for every part. Nothing has to cross between parts.
Inputs may be any that keep to these rules, and one draw needn't show every extreme that they name: `new_units`: A permutation of all request head groups; slot q of the new layout is on device q // 4. `old_pages`: A permutation of all logical pages (page u * 16 + i is page i of unit u); position p is on device p // 64. The pages that one device holds go to exactly 16 devices of the new layout, exactly 4 to each.
All inputs are finite; a program needn't handle non-finite values.
Results may differ from the reference program's by a relative error of at most 0.013.
Values may be sent and summed in bfloat16 or wider, within the bound.
No kernel may reach another device: no remote copies, remote signals or barrier semaphores. Data moves between devices by JAX's collectives and lax.ppermute only.
A program may use at most 128 MiB of HBM per device.

```python
import math
import jax
import jax.numpy as jnp
import numpy as np
from jax import lax

D = 8192
HEADS = 64
KVH = 8
HD = 128
GROUP = 8
U_DEV = 4
MAXCTX = 2048
PAGE = 128
PAGES_DEV = 64
CAP = 4
REQ = 8
PAGES = 1024
N_TP = 16


def layout_tables(key):
    unit_total = U_DEV * N_TP
    page_total = PAGES_DEV * N_TP
    per_unit = MAXCTX // PAGE
    capacity = CAP
    new_units = jax.random.permutation(jax.random.fold_in(key, 101), unit_total).astype(jnp.int32)
    offsets = jax.random.permutation(jax.random.fold_in(key, 102), N_TP).astype(jnp.int32)[:PAGES_DEV // capacity]
    first_perm = jax.random.permutation(jax.random.fold_in(key, 103), N_TP).astype(jnp.int32)
    second_perm = jax.random.permutation(jax.random.fold_in(key, 104), N_TP).astype(jnp.int32)
    within = jax.vmap(lambda sub: jax.random.permutation(sub, PAGES_DEV))(jax.random.split(jax.random.fold_in(key, 105), N_TP)).astype(jnp.int32)
    shuffle = jax.vmap(lambda sub: jax.random.permutation(sub, PAGES_DEV))(jax.random.split(jax.random.fold_in(key, 106), N_TP)).astype(jnp.int32)
    new_position = jnp.arange(page_total, dtype=jnp.int32)
    new_device = new_position // PAGES_DEV
    new_slot = new_position % PAGES_DEV
    page_id = new_units[new_position // per_unit] * per_unit + new_position % per_unit
    drawn_rank = within[new_device, new_slot]
    group_index = drawn_rank // capacity
    member = drawn_rank % capacity
    old_device = second_perm[(first_perm[new_device] + offsets[group_index]) % N_TP]
    old_slot = shuffle[old_device, group_index * capacity + member]
    old_position = old_device * PAGES_DEV + old_slot
    old_pages = jnp.zeros((page_total,), jnp.int32).at[old_position].set(page_id)
    return (new_units, old_pages)


def draw_new_units(key, part):
    return layout_tables(key)[0]


def draw_old_pages(key, part):
    return layout_tables(key)[1]


def block_levels(rng, extent, pieces, smallest, high):
    gain = 1.0
    for axis_at, blocks in pieces:
        heights = jax.random.uniform(jax.random.fold_in(jax.random.fold_in(rng, 6), axis_at), (blocks,), jnp.float32, smallest / len(pieces), high / len(pieces))
        gain = gain * jnp.repeat(jnp.exp(heights), extent[axis_at] // blocks).reshape((-1,) + (1,) * (len(extent) - 1 - axis_at))
    return gain


def split_up(number_of, total, most, lean):
    weights = [(1 << 20) // math.isqrt(rank ** lean) + 1 for rank in range(2, number_of + 1)]
    spare, given = total - most - (number_of - 1), [1] * (number_of - 1)
    while spare > 0:
        candidates = [i for i in range(number_of - 1) if given[i] < most]
        pool, left = sum([weights[i] for i in candidates]), spare
        for i in candidates:
            more = min(most - given[i], max(1, left * weights[i] // pool), spare)
            given[i] = given[i] + more
            spare = spare - more
    return np.array([most] + given)


def ragged(stream_key, count, total, most, lean):
    if count == 2:
        one = jax.random.randint(stream_key, (), max(1, total - most), min(most, total - 1) + 1)
        return jnp.stack([one, total - one])
    sizes = jnp.asarray(split_up(count, total, most, lean), jnp.int32)
    couples = (count - 1) // 2
    giver, sink = sizes[1:1 + 2 * couples:2], sizes[2:2 + 2 * couples:2]
    slack = jnp.minimum(giver - 1, most - sink)
    shifted = jax.random.randint(jax.random.fold_in(stream_key, 1), (couples,), 0, 1 << 20) % (slack + 1)
    sizes = sizes.at[1:1 + 2 * couples:2].set(giver - shifted).at[2:2 + 2 * couples:2].set(sink + shifted)
    return sizes[jax.random.permutation(jax.random.fold_in(stream_key, 2), count)]


def normal_values(own_key, extent, width, limit, cuts=(), kind=jnp.bfloat16):
    array = width * jax.random.normal(own_key, extent, jnp.float32)
    if cuts:
        array = array * block_levels(own_key, extent, cuts, -0.22, 0.18)
    return jnp.clip(array, -limit, limit).astype(kind)


def setup_inputs(seed: int = 0, part: int = 0) -> dict:
    splits = jax.random.split(jax.random.key(seed), 8)
    part_splits = jax.random.split(jax.random.fold_in(splits[7], part), 8)
    hidden_states = normal_values(part_splits[0], (REQ, 2, D), 1.0, 6.0)
    qkv_weight = normal_values(splits[1], (KVH * (GROUP + 2) * HD, D), D ** -0.5, 0.0625, ((0, 16),))
    out_weight = normal_values(splits[2], (D, HEADS * HD), (HEADS * HD) ** -0.5, 0.0625, ((0, 16),))
    cache_pages = normal_values(part_splits[3], (PAGES, PAGE, 2 * HD), 1.0, 6.0, ((0, 16),))
    context_lengths = ragged(part_splits[4], REQ, REQ * (MAXCTX - 2) // 2, MAXCTX - 2, 2).astype(jnp.int32)
    new_units = draw_new_units(jax.random.fold_in(jax.random.fold_in(splits[7], part), 71), part)
    old_pages = draw_old_pages(jax.random.fold_in(jax.random.fold_in(splits[7], part), 71), part)
    return {"hidden_states": hidden_states, "qkv_weight": qkv_weight, "out_weight": out_weight, "cache_pages": cache_pages, "context_lengths": context_lengths, "new_units": new_units, "old_pages": old_pages}


rope_base = 10000.0

def rotate_positions(values, positions):
    half_dim = values.shape[-1] // 2
    frequency = rope_base ** (-(jnp.arange(half_dim, dtype=jnp.float32) * 2.0 / values.shape[-1]))
    angles = positions.astype(jnp.float32)[..., None] * frequency
    cosine = jnp.concatenate([jnp.cos(angles), jnp.cos(angles)], axis=-1)
    sine_table = jnp.concatenate([jnp.sin(angles), jnp.sin(angles)], axis=-1)
    turned = jnp.concatenate([-values[..., half_dim:], values[..., :half_dim]], axis=-1)
    return values * cosine + turned * sine_table

def prepare(unit_qkv, base_lengths):
    group_count = HEADS // KVH
    count_units = unit_qkv.shape[0]
    positions = base_lengths[:, None] + jnp.arange(2, dtype=jnp.int32)[None, :]
    widened = unit_qkv.astype(jnp.float32)
    queries = widened[..., :group_count * HD].reshape(count_units, 2, group_count, HD)
    queries = rotate_positions(queries, positions[:, :, None]).astype(jnp.bfloat16)
    new_keys = rotate_positions(widened[..., group_count * HD:(group_count + 1) * HD], positions).astype(jnp.bfloat16)
    new_values = unit_qkv[..., (group_count + 1) * HD:]
    return (queries, new_keys, new_values)

def reference(hidden_states, qkv_weight, out_weight, cache_pages, context_lengths, new_units, old_pages):
    group_count = HEADS // KVH
    unit_rows = (group_count + 2) * HD
    requests = hidden_states.shape[0]
    total_units = requests * KVH
    per_unit = MAXCTX // PAGE
    page_width = cache_pages.shape[2]
    total_pages = old_pages.shape[0]
    score_scale = 1.0 / math.sqrt(HD)
    flat_rows = hidden_states.reshape(requests * 2, D)
    projected = jnp.dot(flat_rows, qkv_weight.T, preferred_element_type=jnp.float32).astype(jnp.bfloat16)
    unit_qkv = projected.reshape(requests, 2, KVH, unit_rows).transpose(0, 2, 1, 3).reshape(total_units, 2, unit_rows)
    unit_lengths = jnp.repeat(context_lengths, KVH)
    queries, new_keys, new_values = prepare(unit_qkv, unit_lengths)
    stored_position = jnp.zeros((total_pages,), jnp.int32).at[old_pages].set(jnp.arange(total_pages, dtype=jnp.int32))
    contexts = cache_pages[stored_position].reshape(total_units, MAXCTX, page_width)

    def one_unit(packed):
        context, unit_query, keys_new, values_new, valid_count = packed
        cached_keys = jnp.concatenate([context[:, :HD], keys_new], axis=0).astype(jnp.float32)
        cached_values = jnp.concatenate([context[:, HD:], values_new], axis=0).astype(jnp.float32)
        scores = jnp.einsum('sgd,td->sgt', unit_query.astype(jnp.float32), cached_keys) * score_scale
        cached = jnp.arange(MAXCTX, dtype=jnp.int32) < valid_count
        recent = jnp.arange(2, dtype=jnp.int32)[None, :] <= jnp.arange(2, dtype=jnp.int32)[:, None]
        visible = jnp.concatenate([jnp.broadcast_to(cached[None, :], (2, MAXCTX)), recent], axis=1)
        weights = jnp.where(visible[:, None, :], jnp.exp(scores), 0.0)
        totals = lax.optimization_barrier(jnp.sum(weights, axis=-1))
        rounded = lax.optimization_barrier(weights.astype(jnp.bfloat16)).astype(jnp.float32)
        weighted = jnp.einsum('sgt,td->sgd', rounded, cached_values)
        return (weighted / totals[..., None]).astype(jnp.bfloat16)
    attended = lax.map(one_unit, (contexts, queries, new_keys, new_values, unit_lengths))
    heads_out = attended.reshape(requests, KVH, 2, group_count * HD).transpose(0, 2, 1, 3).reshape(requests * 2, HEADS * HD)
    mixed_rows = jnp.dot(heads_out, out_weight.T, preferred_element_type=jnp.float32).astype(jnp.bfloat16).reshape(requests, 2, D)
    slot_contexts = contexts[new_units]
    slot_lengths = unit_lengths[new_units]
    fresh_rows = jnp.concatenate([new_keys, new_values], axis=-1)[new_units]
    positions = jnp.arange(MAXCTX, dtype=jnp.int32)[None, :]
    slot_contexts = jnp.where((positions == slot_lengths[:, None])[..., None], fresh_rows[:, 0:1], slot_contexts)
    slot_contexts = jnp.where((positions == slot_lengths[:, None] + 1)[..., None], fresh_rows[:, 1:2], slot_contexts)
    new_cache = slot_contexts.reshape(total_units * per_unit, PAGE, page_width)
    return (mixed_rows, new_cache)
```

```python
import functools
import math

import jax
import jax.numpy as jnp
from jax import lax
from jax.experimental import pallas as pl
from jax.experimental.pallas import tpu as pltpu
from jax.sharding import PartitionSpec as P

D = 8192
HEADS = 64
KVH = 8
HD = 128
U_DEV = 4
MAXCTX = 2048
PAGE = 128
GROUP = HEADS // KVH
QROWS = 2 * GROUP
PER_UNIT = MAXCTX // PAGE
VMEM_LIMIT = 32 * 1024 * 1024
FIRST = 3
LATE = 0
GROUPS = (5, 4, 4, 2)

rope_base = 10000.0


def rope_tables(positions):
    half_dim = HD // 2
    frequency = rope_base ** (-(jnp.arange(half_dim, dtype=jnp.float32) * 2.0 / HD))
    angles = positions.astype(jnp.float32)[..., None] * frequency
    cosine = jnp.concatenate([jnp.cos(angles), jnp.cos(angles)], axis=-1)
    sine = jnp.concatenate([-jnp.sin(angles), jnp.sin(angles)], axis=-1)
    return cosine, sine


def rotate(values, cosine, sine):
    half_dim = HD // 2
    turned = jnp.concatenate([values[..., half_dim:], values[..., :half_dim]], axis=-1)
    return values * cosine + turned * sine


def any_spec():
    return pl.BlockSpec(memory_space=pl.ANY)


def smem_spec():
    return pl.BlockSpec(memory_space=pltpu.SMEM)


def vmem_spec():
    return pl.BlockSpec(memory_space=pltpu.VMEM)


def load_order(devices, capacity, relative, units_ref, old_ref, order_ref, slots, count):
    device = lax.axis_index("tp")
    total_units = units_ref.shape[0]
    pages_dev = old_ref.shape[0] // devices

    def clear(t, carry):
        count[t] = 0
        return carry

    def empty(t, carry):
        order_ref[t] = 0
        return carry

    def invert(q, carry):
        slots[units_ref[q]] = q
        return carry

    def assign(i, carry):
        unit = old_ref[device * pages_dev + i] // PER_UNIT
        target = slots[unit] // U_DEV
        if relative:
            target = target ^ device
        rank = count[target]
        count[target] = rank + 1
        order_ref[target * capacity + rank] = i
        return carry

    lax.fori_loop(0, devices, clear, 0, unroll=8)
    if devices * capacity > pages_dev:
        lax.fori_loop(0, devices * capacity, empty, 0, unroll=8)
    lax.fori_loop(0, total_units, invert, 0, unroll=8)
    lax.fori_loop(0, pages_dev, assign, 0, unroll=8)


def move_pages(capacity, keys, order_ref, pages_ref, outs, stage, load_sem, store_sem):
    loads, stores = [], []
    for n, key in enumerate(keys):
        for r in range(capacity):
            copy = pltpu.make_async_copy(
                pages_ref.at[order_ref[key * capacity + r]],
                stage.at[n * capacity + r],
                load_sem.at[n * capacity + r],
            )
            copy.start()
            loads.append(copy)
    for n, key in enumerate(keys):
        for r in range(capacity):
            loads[n * capacity + r].wait()
        target = outs[n] if len(outs) > 1 else outs[0].at[pl.ds(n * capacity, capacity)]
        copy = pltpu.make_async_copy(
            stage.at[pl.ds(n * capacity, capacity)], target, store_sem.at[n]
        )
        copy.start()
        stores.append(copy)
    for copy in stores:
        copy.wait()


def first_pack_kernel(devices, capacity, keys, relative, units_ref, old_ref, pages_ref, *rest):
    outs = rest[:-6]
    order_ref, slots, count, stage, load_sem, store_sem = rest[-6:]
    load_order(devices, capacity, relative, units_ref, old_ref, order_ref, slots, count)
    move_pages(capacity, keys, order_ref, pages_ref, outs, stage, load_sem, store_sem)


def next_pack_kernel(capacity, keys, order_ref, pages_ref, *rest):
    outs = rest[:-3]
    stage, load_sem, store_sem = rest[-3:]
    move_pages(capacity, keys, order_ref, pages_ref, outs, stage, load_sem, store_sem)


def pack_scratch(count, pages):
    return [
        pltpu.VMEM((count,) + pages.shape[1:], pages.dtype),
        pltpu.SemaphoreType.DMA((count,)),
        pltpu.SemaphoreType.DMA((count,)),
    ]


def first_pack(new_units, old_pages, pages, devices, capacity, keys, relative):
    chunk = (capacity,) + pages.shape[1:]
    if relative:
        outs = [jax.ShapeDtypeStruct(chunk, pages.dtype) for _ in keys]
    else:
        outs = [jax.ShapeDtypeStruct((len(keys) * capacity,) + chunk[1:], pages.dtype)]
    result = pl.pallas_call(
        functools.partial(first_pack_kernel, devices, capacity, keys, relative),
        out_shape=tuple(outs) + (jax.ShapeDtypeStruct((devices * capacity,), jnp.int32),),
        in_specs=[smem_spec(), smem_spec(), any_spec()],
        out_specs=tuple(any_spec() for _ in outs) + (smem_spec(),),
        scratch_shapes=[
            pltpu.SMEM(new_units.shape, jnp.int32),
            pltpu.SMEM((devices,), jnp.int32),
        ]
        + pack_scratch(len(keys) * capacity, pages),
        compiler_params=pltpu.CompilerParams(vmem_limit_bytes=VMEM_LIMIT),
        name="first_pack",
    )(new_units, old_pages, pages)
    return result[:-1], result[-1]


def next_pack(order, pages, capacity, keys):
    chunk = (capacity,) + pages.shape[1:]
    return pl.pallas_call(
        functools.partial(next_pack_kernel, capacity, keys),
        out_shape=tuple(jax.ShapeDtypeStruct(chunk, pages.dtype) for _ in keys),
        in_specs=[smem_spec(), any_spec()],
        out_specs=tuple(any_spec() for _ in keys),
        scratch_shapes=pack_scratch(len(keys) * capacity, pages),
        compiler_params=pltpu.CompilerParams(vmem_limit_bytes=VMEM_LIMIT),
        name="next_pack",
    )(order, pages)


def attend(query, keys, values, limit):
    scale = 1.0 / math.sqrt(HD)
    scores = (
        lax.dot_general(query, keys, (((1,), (1,)), ((), ())), preferred_element_type=jnp.float32)
        * scale
    )
    lane = lax.broadcasted_iota(jnp.int32, scores.shape, 1)
    weights = jnp.where(lane < limit, jnp.exp(scores), 0.0)
    total = jnp.sum(weights, axis=1, keepdims=True)
    weighted = jnp.dot(weights.astype(jnp.bfloat16), values, preferred_element_type=jnp.float32)
    return weighted, total


def partial_kernel(
    capacity, keys, order_ref, old_ref, lengths_ref, queries_ref, pages_ref, *rest
):
    outs = rest[: len(keys)]
    stage, load_sem = rest[len(keys) :]
    device = lax.axis_index("tp")
    pages_dev = pages_ref.shape[0]
    lane = lax.broadcasted_iota(jnp.int32, (QROWS, HD), 1)
    loads = []
    for n, key in enumerate(keys):
        for r in range(capacity):
            copy = pltpu.make_async_copy(
                pages_ref.at[order_ref[key * capacity + r]],
                stage.at[n * capacity + r],
                load_sem.at[n * capacity + r],
            )
            copy.start()
            loads.append(copy)
    for n, key in enumerate(keys):
        sums = jnp.zeros((QROWS, HD), jnp.float32)
        for r in range(capacity):
            page = old_ref[device * pages_dev + order_ref[key * capacity + r]]
            unit = page // PER_UNIT
            limit = lengths_ref[unit // KVH] - (page % PER_UNIT) * PAGE
            slot = n * capacity + r
            loads[slot].wait()
            weighted, total = attend(
                queries_ref[unit], stage[slot, :, :HD], stage[slot, :, HD:], limit
            )
            outs[n][r * QROWS : (r + 1) * QROWS, :] = weighted.astype(jnp.bfloat16)
            high = total.astype(jnp.bfloat16).astype(jnp.float32)
            sums = jnp.where(lane == 2 * r, high, sums)
            sums = jnp.where(lane == 2 * r + 1, total - high, sums)
        outs[n][capacity * QROWS :, :] = sums.astype(jnp.bfloat16)


def partial_terms(order, old_pages, lengths, queries, pages, capacity, keys):
    rows = (capacity + 1) * QROWS
    count = len(keys) * capacity
    return pl.pallas_call(
        functools.partial(partial_kernel, capacity, keys),
        out_shape=tuple(jax.ShapeDtypeStruct((rows, HD), jnp.bfloat16) for _ in keys),
        in_specs=[smem_spec()] * 3 + [vmem_spec(), any_spec()],
        out_specs=tuple(vmem_spec() for _ in keys),
        scratch_shapes=[
            pltpu.VMEM((count,) + pages.shape[1:], pages.dtype),
            pltpu.SemaphoreType.DMA((count,)),
        ],
        compiler_params=pltpu.CompilerParams(vmem_limit_bytes=VMEM_LIMIT),
        name="partial_terms",
    )(order, old_pages, lengths, queries, pages)


ALIGN = 16


def place_kernel(entries, attends, started, *refs):
    refs = list(refs)
    table_ref, order_ref, length_ref, fresh_ref = refs[:4]
    refs = refs[4:]
    queries_ref = refs.pop(0) if attends else None
    if started and attends:
        weighted_in, total_in = refs.pop(0), refs.pop(0)
    sources = 1 + max(source for source, _, _ in entries)
    source_refs, refs = refs[:sources], refs[sources:]
    if started:
        refs.pop(0)
    out_ref = refs.pop(0)
    if attends:
        weighted_ref, total_ref = refs.pop(0), refs.pop(0)
    stage, load_sem, store_sem = refs
    if attends:
        if started:
            weighted_ref[...] = weighted_in[...]
            total_ref[...] = total_in[...]
        else:
            weighted_ref[...] = jnp.zeros_like(weighted_ref)
            total_ref[...] = jnp.zeros_like(total_ref)
    loads = []
    for n, (source, index, _) in enumerate(entries):
        index = order_ref[index[0]] if isinstance(index, tuple) else index
        copy = pltpu.make_async_copy(
            source_refs[source].at[index], stage.at[n], load_sem.at[n]
        )
        copy.start()
        loads.append(copy)
    row = lax.broadcasted_iota(jnp.int32, (ALIGN, 2 * HD), 0)
    stores = []
    for n, (_, _, key) in enumerate(entries):
        w = table_ref[key[0]] if isinstance(key, tuple) else key
        unit, part = w // PER_UNIT, w % PER_UNIT
        length = length_ref[unit]
        loads[n].wait()
        for j in range(2):
            position = length + j

            @pl.when(position // PAGE == part)
            def _():
                inside = position % PAGE
                rows = pl.ds(pl.multiple_of(inside // ALIGN * ALIGN, ALIGN), ALIGN)
                block = stage[n, rows, :].astype(jnp.float32)
                token = fresh_ref[unit, j : j + 1, :].astype(jnp.float32)
                block = jnp.where(row == inside % ALIGN, token, block)
                stage[n, rows, :] = block.astype(jnp.bfloat16)

        copy = pltpu.make_async_copy(stage.at[n], out_ref.at[w], store_sem.at[n])
        copy.start()
        stores.append(copy)
    if attends:
        group = 4
        for first in range(0, len(entries), group):
            found = []
            for n in range(first, min(first + group, len(entries))):
                key = entries[n][2]
                w = table_ref[key[0]] if isinstance(key, tuple) else key
                unit, part = w // PER_UNIT, w % PER_UNIT
                weighted, total = attend(
                    queries_ref[unit],
                    stage[n, :, :HD],
                    stage[n, :, HD:],
                    length_ref[unit] - part * PAGE,
                )
                found.append((unit, weighted, total))
            for unit, weighted, total in found:
                weighted_ref[unit] += weighted
                total_ref[unit] += jnp.broadcast_to(total, (QROWS, HD))
    for copy in stores:
        copy.wait()


def place_pages(table, order, lengths, fresh, queries, sums, sources, entries, cache):
    attends, started = queries is not None, cache is not None
    page_shape = sources[0].shape[1:]
    pages_dev = U_DEV * PER_UNIT
    args = [table, order, lengths, fresh]
    specs = [smem_spec()] * 3 + [vmem_spec()]
    if attends:
        args.append(queries)
        specs.append(vmem_spec())
        if started:
            args += list(sums)
            specs += [vmem_spec()] * 2
    args += list(sources)
    specs += [any_spec()] * len(sources)
    aliases = {}
    if started:
        aliases = {len(args): 0}
        args.append(cache)
        specs.append(any_spec())
    outs = [jax.ShapeDtypeStruct((pages_dev,) + page_shape, jnp.bfloat16)]
    out_specs = [any_spec()]
    if attends:
        outs += [jax.ShapeDtypeStruct((U_DEV, QROWS, HD), jnp.float32)] * 2
        out_specs += [vmem_spec()] * 2
    count = len(entries)
    result = pl.pallas_call(
        functools.partial(place_kernel, entries, attends, started),
        out_shape=tuple(outs),
        in_specs=specs,
        out_specs=tuple(out_specs),
        input_output_aliases=aliases,
        scratch_shapes=[
            pltpu.VMEM((count,) + page_shape, jnp.bfloat16),
            pltpu.SemaphoreType.DMA((count,)),
            pltpu.SemaphoreType.DMA((count,)),
        ],
        compiler_params=pltpu.CompilerParams(vmem_limit_bytes=VMEM_LIMIT),
        name="place_pages",
    )(*args)
    return result[0], result[1:]


def combine_kernel(capacity, late, table_ref, weighted_ref, total_ref, queries_ref, fresh_ref, *rest):
    parts, out_ref, weighted_sum, total_sum = rest[:-3], rest[-3], rest[-2], rest[-1]
    scale = 1.0 / math.sqrt(HD)
    lane = lax.broadcasted_iota(jnp.int32, (QROWS, HD), 1)
    row = lax.broadcasted_iota(jnp.int32, (QROWS, 1), 0)
    weighted_sum[...] = weighted_ref[...]
    total_sum[...] = total_ref[...]
    for part, key in zip(parts, late):
        sums = part[capacity * QROWS :, :].astype(jnp.float32)
        for r in range(capacity):
            unit = table_ref[key * capacity + r] // PER_UNIT
            mine = (lane == 2 * r) | (lane == 2 * r + 1)
            total = jnp.sum(jnp.where(mine, sums, 0.0), axis=1, keepdims=True)
            weighted_sum[unit] += part[r * QROWS : (r + 1) * QROWS, :].astype(jnp.float32)
            total_sum[unit] += jnp.broadcast_to(total, (QROWS, HD))
    for unit in range(U_DEV):
        query = queries_ref[unit].astype(jnp.float32)
        weighted = weighted_sum[unit]
        total = total_sum[unit]
        for j in range(2):
            key = fresh_ref[unit, j : j + 1, :HD].astype(jnp.float32)
            value = fresh_ref[unit, j : j + 1, HD:].astype(jnp.float32)
            score = jnp.sum(query * key, axis=1, keepdims=True) * scale
            weight = jnp.where(row >= j * GROUP, jnp.exp(score), 0.0)
            total = total + weight
            weighted = weighted + weight.astype(jnp.bfloat16).astype(jnp.float32) * value
        out_ref[unit] = (weighted / total).astype(jnp.bfloat16)


def combine(table, sums, queries, fresh, parts, late, capacity):
    return pl.pallas_call(
        functools.partial(combine_kernel, capacity, late),
        out_shape=jax.ShapeDtypeStruct((U_DEV, QROWS, HD), jnp.bfloat16),
        in_specs=[smem_spec()] + [vmem_spec()] * (4 + len(parts)),
        out_specs=vmem_spec(),
        scratch_shapes=[pltpu.VMEM((U_DEV, QROWS, HD), jnp.float32)] * 2,
        name="combine",
    )(table, *sums, queries, fresh, *parts)


def swap(values, key, devices):
    return lax.ppermute(values, "tp", [(i, i ^ key) for i in range(devices)])


def gather_swaps(values, devices):
    values = values[None]
    step = devices // 2
    span = [0]
    while step:
        values = jnp.concatenate([values, swap(values, step, devices)], axis=0)
        span = span + [s ^ step for s in span]
        step //= 2
    return values, span


def exchange_plan(devices):
    half = devices // 2
    far = sorted(range(half, devices), key=lambda k: (k & 1, k & 2, k))
    near = sorted(range(1, half), key=lambda k: (-(k & (half // 2)), k & 1, k))
    plan = far[:3]
    far = far[3:]
    while far:
        take = -(-len(near) // len(far))
        plan += near[:take] + far[:1]
        near, far = near[take:], far[1:]
    return plan + near


def body(hidden_states, qkv_weight, out_weight, cache_pages, context_lengths, new_units, old_pages):
    devices = lax.axis_size("tp")
    device = lax.axis_index("tp")
    requests = hidden_states.shape[0]
    pages_dev, page_rows, page_width = cache_pages.shape
    capacity = max(1, pages_dev // devices)
    total_units = new_units.shape[0]
    total_pages = old_pages.shape[0]
    pairwise = devices <= 16 and devices & (devices - 1) == 0

    if pairwise:
        plan = exchange_plan(devices)
        first, order = first_pack(
            new_units, old_pages, cache_pages, devices, capacity, plan[:FIRST], True
        )
        second = next_pack(order, cache_pages, capacity, plan[FIRST:])
        moved = [swap(c, k, devices) for c, k in zip(tuple(first) + tuple(second), plan)]
    else:
        keys = list(range(devices))
        (packed,), order = first_pack(
            new_units, old_pages, cache_pages, devices, capacity, keys, False
        )
        arrived = lax.all_to_all(
            packed.reshape(devices, capacity, page_rows, page_width),
            "tp",
            split_axis=0,
            concat_axis=0,
            tiled=True,
        ).reshape(devices * capacity, page_rows, page_width)

    own_units = lax.dynamic_slice_in_dim(new_units, device * U_DEV, U_DEV)
    own_lengths = context_lengths[own_units // KVH]
    wanted = (
        own_units[:, None] * PER_UNIT + jnp.arange(PER_UNIT, dtype=jnp.int32)[None, :]
    ).reshape(pages_dev)
    source_pos = jnp.sum(
        jnp.where(
            wanted[:, None] == old_pages[None, :],
            jnp.arange(total_pages, dtype=jnp.int32)[None, :],
            0,
        ),
        axis=1,
    )
    source_dev = source_pos // pages_dev
    rank = jnp.sum(
        (
            (source_dev[:, None] == source_dev[None, :])
            & (source_pos[None, :] < source_pos[:, None])
        ).astype(jnp.int32),
        axis=1,
    )
    if pairwise:
        where = (source_dev ^ device) * capacity + rank
        spots = jnp.arange(devices * capacity, dtype=jnp.int32)
        slots = jnp.arange(pages_dev, dtype=jnp.int32)
        table = jnp.sum(jnp.where(where[None, :] == spots[:, None], slots[None, :], 0), axis=1)
    else:
        table = source_dev * capacity + rank

    flat_rows = hidden_states.reshape(requests * 2, D)
    own_part = lax.dot_general(
        flat_rows, qkv_weight, (((1,), (1,)), ((), ())), preferred_element_type=jnp.float32
    ).astype(jnp.bfloat16)
    if pairwise:
        rows, span = gather_swaps(own_part, devices)
        turn = jnp.array([span.index(i) for i in range(devices)], jnp.int32)
        rows = rows[turn[jnp.arange(devices, dtype=jnp.int32) ^ device]]
        rows = rows.transpose(1, 0, 2)
    else:
        rows = lax.all_gather(own_part, "tp", axis=1, tiled=True)
    rows = rows.reshape(requests, 2, KVH, GROUP + 2, HD)

    positions = context_lengths[:, None] + jnp.arange(2, dtype=jnp.int32)[None, :]
    cosine, sine = rope_tables(positions)
    turned = rotate(
        rows[..., : GROUP + 1, :].astype(jnp.float32),
        cosine[:, :, None, None, :],
        sine[:, :, None, None, :],
    ).astype(jnp.bfloat16)
    by_unit = turned.transpose(0, 2, 1, 3, 4).reshape(total_units, 2, GROUP + 1, HD)
    queries = by_unit[:, :, :GROUP].reshape(total_units, QROWS, HD)
    new_keys = by_unit[:, :, GROUP]
    new_values = rows[..., GROUP + 1, :].transpose(0, 2, 1, 3).reshape(total_units, 2, HD)
    own_queries = queries[own_units]
    fresh = jnp.concatenate([new_keys[own_units], new_values[own_units]], axis=-1)

    late, parts, sums, new_cache = [], [], None, None
    if pairwise:
        late = plan[len(plan) - LATE :]
        if late:
            sent = partial_terms(
                order, old_pages, context_lengths, queries, cache_pages, capacity, late
            )
            parts = [swap(p, k, devices) for p, k in zip(sent, late)]
        at = 0
        for size in GROUPS:
            keys, at = plan[at : at + size], at + size
            entries, sources = [], []
            for key, array in zip(keys, moved[at - size : at]):
                entries += [(len(sources), r, (key * capacity + r,)) for r in range(capacity)]
                sources.append(array)
            if at == size:
                entries = [(len(sources), (r,), (r,)) for r in range(capacity)] + entries
                sources.append(cache_pages)
            attending = at <= len(plan) - len(late)
            new_cache, found = place_pages(
                table,
                order,
                own_lengths,
                fresh,
                own_queries if attending else None,
                sums,
                sources,
                entries,
                new_cache,
            )
            sums = found if attending else sums
    else:
        entries = [(0, (w,), w) for w in range(pages_dev)]
        new_cache, sums = place_pages(
            table, table, own_lengths, fresh, own_queries, None, [arrived], entries, None
        )
    attended = combine(table, sums, own_queries, fresh, parts, late, capacity)

    slot_index = jnp.sum(
        jnp.where(
            new_units[None, :] == jnp.arange(total_units, dtype=jnp.int32)[:, None],
            jnp.arange(total_units, dtype=jnp.int32)[None, :],
            0,
        ),
        axis=1,
    )
    attended = attended.reshape(U_DEV, 2, GROUP * HD)
    if pairwise:
        heads, span = gather_swaps(attended, devices)
        holder = turn[(slot_index // U_DEV) ^ device]
        heads = heads.reshape(total_units, 2, GROUP * HD)[holder * U_DEV + slot_index % U_DEV]
    else:
        heads = lax.all_gather(attended, "tp", axis=0, tiled=True)[slot_index]
    logical = (
        heads.reshape(requests, KVH, 2, GROUP * HD)
        .transpose(0, 2, 1, 3)
        .reshape(requests * 2, HEADS * HD)
    )
    mixed_rows = lax.dot_general(
        logical, out_weight, (((1,), (1,)), ((), ())), preferred_element_type=jnp.float32
    )
    mixed_rows = mixed_rows.astype(jnp.bfloat16).reshape(requests, 2, out_weight.shape[0])
    return (mixed_rows, new_cache)


def solution(mesh):
    in_specs = (
        P("group", None, None),
        P("tp", None),
        P("tp", None),
        P(("group", "tp"), None, None),
        P("group"),
        P("group"),
        P("group"),
    )
    out_specs = (P("group", None, "tp"), P(("group", "tp"), None, None))
    return jax.shard_map(body, mesh=mesh, in_specs=in_specs, out_specs=out_specs, check_vma=False)
```

```python
import functools
import math

import jax
import jax.numpy as jnp
from jax import lax
from jax.experimental import pallas as pl
from jax.experimental.pallas import tpu as pltpu
from jax.sharding import PartitionSpec as P

D = 8192
HEADS = 64
KVH = 8
HD = 128
U_DEV = 4
MAXCTX = 2048
PAGE = 128
GROUP = HEADS // KVH
QROWS = 2 * GROUP
PER_UNIT = MAXCTX // PAGE
VMEM_LIMIT = 32 * 1024 * 1024

rope_base = 10000.0


def rope_tables(positions):
    half_dim = HD // 2
    frequency = rope_base ** (-(jnp.arange(half_dim, dtype=jnp.float32) * 2.0 / HD))
    angles = positions.astype(jnp.float32)[..., None] * frequency
    cosine = jnp.concatenate([jnp.cos(angles), jnp.cos(angles)], axis=-1)
    sine = jnp.concatenate([-jnp.sin(angles), jnp.sin(angles)], axis=-1)
    return cosine, sine


def rotate(values, cosine, sine):
    half_dim = HD // 2
    turned = jnp.concatenate([values[..., half_dim:], values[..., :half_dim]], axis=-1)
    return values * cosine + turned * sine


def any_spec():
    return pl.BlockSpec(memory_space=pl.ANY)


def smem_spec():
    return pl.BlockSpec(memory_space=pltpu.SMEM)


def vmem_spec():
    return pl.BlockSpec(memory_space=pltpu.VMEM)


def load_order(devices, capacity, relative, units_ref, old_ref, order_ref, slots, count):
    device = lax.axis_index("tp")
    total_units = units_ref.shape[0]
    pages_dev = old_ref.shape[0] // devices

    def clear(t, carry):
        count[t] = 0
        return carry

    def empty(t, carry):
        order_ref[t] = 0
        return carry

    def invert(q, carry):
        slots[units_ref[q]] = q
        return carry

    def assign(i, carry):
        unit = old_ref[device * pages_dev + i] // PER_UNIT
        target = slots[unit] // U_DEV
        if relative:
            target = target ^ device
        rank = count[target]
        count[target] = rank + 1
        order_ref[target * capacity + rank] = i
        return carry

    lax.fori_loop(0, devices, clear, 0, unroll=8)
    if devices * capacity > pages_dev:
        lax.fori_loop(0, devices * capacity, empty, 0, unroll=8)
    lax.fori_loop(0, total_units, invert, 0, unroll=8)
    lax.fori_loop(0, pages_dev, assign, 0, unroll=8)


def move_pages(capacity, keys, order_ref, pages_ref, outs, stage, load_sem, store_sem):
    loads, stores = [], []
    for n, key in enumerate(keys):
        for r in range(capacity):
            copy = pltpu.make_async_copy(
                pages_ref.at[order_ref[key * capacity + r]],
                stage.at[n * capacity + r],
                load_sem.at[n * capacity + r],
            )
            copy.start()
            loads.append(copy)
    for n, key in enumerate(keys):
        for r in range(capacity):
            loads[n * capacity + r].wait()
        target = outs[n] if len(outs) > 1 else outs[0].at[pl.ds(n * capacity, capacity)]
        copy = pltpu.make_async_copy(
            stage.at[pl.ds(n * capacity, capacity)], target, store_sem.at[n]
        )
        copy.start()
        stores.append(copy)
    for copy in stores:
        copy.wait()


def first_pack_kernel(devices, capacity, keys, relative, units_ref, old_ref, pages_ref, *rest):
    outs = rest[:-6]
    order_ref, slots, count, stage, load_sem, store_sem = rest[-6:]
    load_order(devices, capacity, relative, units_ref, old_ref, order_ref, slots, count)
    move_pages(capacity, keys, order_ref, pages_ref, outs, stage, load_sem, store_sem)


def next_pack_kernel(capacity, keys, order_ref, pages_ref, after_ref, *rest):
    outs = rest[:-3]
    stage, load_sem, store_sem = rest[-3:]
    move_pages(capacity, keys, order_ref, pages_ref, outs, stage, load_sem, store_sem)


def pack_scratch(count, pages):
    return [
        pltpu.VMEM((count,) + pages.shape[1:], pages.dtype),
        pltpu.SemaphoreType.DMA((count,)),
        pltpu.SemaphoreType.DMA((count,)),
    ]


def first_pack(new_units, old_pages, pages, devices, capacity, keys, relative):
    chunk = (capacity,) + pages.shape[1:]
    if relative:
        outs = [jax.ShapeDtypeStruct(chunk, pages.dtype) for _ in keys]
    else:
        outs = [jax.ShapeDtypeStruct((len(keys) * capacity,) + chunk[1:], pages.dtype)]
    result = pl.pallas_call(
        functools.partial(first_pack_kernel, devices, capacity, keys, relative),
        out_shape=tuple(outs) + (jax.ShapeDtypeStruct((devices * capacity,), jnp.int32),),
        in_specs=[smem_spec(), smem_spec(), any_spec()],
        out_specs=tuple(any_spec() for _ in outs) + (smem_spec(),),
        scratch_shapes=[
            pltpu.SMEM(new_units.shape, jnp.int32),
            pltpu.SMEM((devices,), jnp.int32),
        ]
        + pack_scratch(len(keys) * capacity, pages),
        compiler_params=pltpu.CompilerParams(vmem_limit_bytes=VMEM_LIMIT),
        name="first_pack",
    )(new_units, old_pages, pages)
    return result[:-1], result[-1]


def next_pack(order, pages, after, capacity, keys):
    chunk = (capacity,) + pages.shape[1:]
    return pl.pallas_call(
        functools.partial(next_pack_kernel, capacity, keys),
        out_shape=tuple(jax.ShapeDtypeStruct(chunk, pages.dtype) for _ in keys),
        in_specs=[smem_spec(), any_spec(), any_spec()],
        out_specs=tuple(any_spec() for _ in keys),
        scratch_shapes=pack_scratch(len(keys) * capacity, pages),
        compiler_params=pltpu.CompilerParams(vmem_limit_bytes=VMEM_LIMIT),
        name="next_pack",
    )(order, pages, after)


def attend(query, keys, values, limit):
    scale = 1.0 / math.sqrt(HD)
    scores = (
        lax.dot_general(query, keys, (((1,), (1,)), ((), ())), preferred_element_type=jnp.float32)
        * scale
    )
    lane = lax.broadcasted_iota(jnp.int32, scores.shape, 1)
    weights = jnp.where(lane < limit, jnp.exp(scores), 0.0)
    total = jnp.sum(weights, axis=1, keepdims=True)
    weighted = jnp.dot(weights.astype(jnp.bfloat16), values, preferred_element_type=jnp.float32)
    return weighted, total


ALIGN = 16


def place_kernel(entries, started, finish, *refs):
    refs = list(refs)
    table_ref, order_ref, length_ref, fresh_ref = refs[:4]
    refs = refs[4:]
    queries_ref = refs.pop(0)
    if started:
        weighted_in, total_in = refs.pop(0), refs.pop(0)
    sources = 1 + max(source for source, _, _ in entries)
    source_refs, refs = refs[:sources], refs[sources:]
    if started:
        refs.pop(0)
    out_ref, weighted_ref, total_ref = refs[:3]
    refs = refs[3:]
    attended_ref = refs.pop(0) if finish else None
    stage, load_sem, store_sem = refs
    if started:
        weighted_ref[...] = weighted_in[...]
        total_ref[...] = total_in[...]
    else:
        own_terms(queries_ref, fresh_ref, weighted_ref, total_ref)
    loads = []
    for n, (source, index, _) in enumerate(entries):
        index = order_ref[index[0]] if isinstance(index, tuple) else index
        copy = pltpu.make_async_copy(
            source_refs[source].at[index], stage.at[n], load_sem.at[n]
        )
        copy.start()
        loads.append(copy)
    row = lax.broadcasted_iota(jnp.int32, (ALIGN, 2 * HD), 0)
    stores = []
    for n, (_, _, key) in enumerate(entries):
        w = table_ref[key[0]] if isinstance(key, tuple) else key
        unit, part = w // PER_UNIT, w % PER_UNIT
        length = length_ref[unit]
        loads[n].wait()
        for j in range(2):
            position = length + j

            @pl.when(position // PAGE == part)
            def _():
                inside = position % PAGE
                rows = pl.ds(pl.multiple_of(inside // ALIGN * ALIGN, ALIGN), ALIGN)
                block = stage[n, rows, :].astype(jnp.float32)
                token = fresh_ref[pl.ds(2 * unit + j, 1), :]
                block = jnp.where(row == inside % ALIGN, token, block)
                stage[n, rows, :] = block.astype(jnp.bfloat16)

        copy = pltpu.make_async_copy(stage.at[n], out_ref.at[w], store_sem.at[n])
        copy.start()
        stores.append(copy)
    group = 4
    for first in range(0, len(entries), group):
        found = []
        for n in range(first, min(first + group, len(entries))):
            key = entries[n][2]
            w = table_ref[key[0]] if isinstance(key, tuple) else key
            unit, part = w // PER_UNIT, w % PER_UNIT
            weighted, total = attend(
                queries_ref[unit].astype(jnp.bfloat16),
                stage[n, :, :HD],
                stage[n, :, HD:],
                length_ref[unit] - part * PAGE,
            )
            found.append((unit, weighted, total))
        for unit, weighted, total in found:
            weighted_ref[unit] += weighted
            total_ref[unit] += jnp.broadcast_to(total, (QROWS, HD))
    if finish:
        attended_ref[...] = (weighted_ref[...] / total_ref[...]).astype(jnp.bfloat16)
    for copy in stores:
        copy.wait()


def own_terms(queries_ref, fresh_ref, weighted_ref, total_ref):
    scale = 1.0 / math.sqrt(HD)
    row = lax.broadcasted_iota(jnp.int32, (QROWS, 1), 0)
    for unit in range(U_DEV):
        query = queries_ref[unit]
        weighted = jnp.zeros((QROWS, HD), jnp.float32)
        total = jnp.zeros((QROWS, 1), jnp.float32)
        for j in range(2):
            at = 2 * unit + j
            key = fresh_ref[at : at + 1, :HD]
            value = fresh_ref[at : at + 1, HD:]
            score = jnp.sum(query * key, axis=1, keepdims=True) * scale
            weight = jnp.where(row >= j * GROUP, jnp.exp(score), 0.0)
            total = total + weight
            weighted = weighted + weight.astype(jnp.bfloat16).astype(jnp.float32) * value
        weighted_ref[unit] = weighted
        total_ref[unit] = jnp.broadcast_to(total, (QROWS, HD))


def place_pages(table, order, lengths, fresh, queries, sums, sources, entries, cache, finish):
    started = cache is not None
    page_shape = sources[0].shape[1:]
    pages_dev = U_DEV * PER_UNIT
    args = [table, order, lengths, fresh, queries]
    specs = [smem_spec()] * 3 + [vmem_spec()] * 2
    if started:
        args += list(sums)
        specs += [vmem_spec()] * 2
    args += list(sources)
    specs += [any_spec()] * len(sources)
    aliases = {}
    if started:
        aliases = {len(args): 0}
        args.append(cache)
        specs.append(any_spec())
    outs = [jax.ShapeDtypeStruct((pages_dev,) + page_shape, jnp.bfloat16)]
    outs += [jax.ShapeDtypeStruct((U_DEV, QROWS, HD), jnp.float32)] * 2
    out_specs = [any_spec()] + [vmem_spec()] * 2
    if finish:
        outs.append(jax.ShapeDtypeStruct((U_DEV, QROWS, HD), jnp.bfloat16))
        out_specs.append(vmem_spec())
    count = len(entries)
    result = pl.pallas_call(
        functools.partial(place_kernel, entries, started, finish),
        out_shape=tuple(outs),
        in_specs=specs,
        out_specs=tuple(out_specs),
        input_output_aliases=aliases,
        scratch_shapes=[
            pltpu.VMEM((count,) + page_shape, jnp.bfloat16),
            pltpu.SemaphoreType.DMA((count,)),
            pltpu.SemaphoreType.DMA((count,)),
        ],
        compiler_params=pltpu.CompilerParams(vmem_limit_bytes=VMEM_LIMIT),
        name="place_pages",
    )(*args)
    return result[0], result[1:3], result[3] if finish else None


def own_rows_kernel(rows_ref, place_ref, request_ref, cosine_ref, sine_ref, queries_ref, fresh_ref):
    width = rows_ref.shape[2]
    pieces = place_ref.shape[0] // U_DEV
    row = lax.broadcasted_iota(jnp.int32, rows_ref.shape[1:], 0)
    half_dim = HD // 2
    for unit in range(U_DEV):
        found = []
        for piece in range(pieces):
            block = rows_ref[place_ref[unit * pieces + piece]].astype(jnp.float32)
            picked = [
                jnp.sum(
                    jnp.where(row == 2 * request_ref[unit] + j, block, 0.0), axis=0, keepdims=True
                )
                for j in range(2)
            ]
            for at in range(0, width, HD):
                found.append([line[:, at : at + HD] for line in picked])
        for j in range(2):
            heads = jnp.concatenate([head[j] for head in found[: GROUP + 1]], axis=0)
            turned = jnp.concatenate([heads[:, half_dim:], heads[:, :half_dim]], axis=1)
            cosine = cosine_ref[2 * unit + j : 2 * unit + j + 1, :]
            sine = sine_ref[2 * unit + j : 2 * unit + j + 1, :]
            heads = (heads * cosine + turned * sine).astype(jnp.bfloat16).astype(jnp.float32)
            queries_ref[unit, j * GROUP : (j + 1) * GROUP, :] = heads[:GROUP]
            fresh_ref[2 * unit + j : 2 * unit + j + 1, :HD] = heads[GROUP:]
            fresh_ref[2 * unit + j : 2 * unit + j + 1, HD:] = found[GROUP + 1][j]


def own_rows(rows, places, requests, cosine, sine):
    queries, fresh = pl.pallas_call(
        own_rows_kernel,
        out_shape=(
            jax.ShapeDtypeStruct((U_DEV, QROWS, HD), jnp.float32),
            jax.ShapeDtypeStruct((2 * U_DEV, 2 * HD), jnp.float32),
        ),
        in_specs=[vmem_spec(), smem_spec(), smem_spec(), vmem_spec(), vmem_spec()],
        out_specs=(vmem_spec(), vmem_spec()),
        name="own_rows",
    )(rows, places, requests, cosine, sine)
    return queries, fresh


def swap(values, key, devices):
    return lax.ppermute(values, "tp", [(i, i ^ key) for i in range(devices)])


def gather_swaps(values, devices, direct):
    values = values[None]
    step = devices // 2
    span = [0]
    if direct and devices >= 4:
        keys = [step, step // 2, step + step // 2]
        values = jnp.concatenate([values] + [swap(values, k, devices) for k in keys], axis=0)
        span = [0] + keys
        step //= 4
    while step:
        values = jnp.concatenate([values, swap(values, step, devices)], axis=0)
        span = span + [s ^ step for s in span]
        step //= 2
    return values, span


def exchange_plan(devices):
    half = devices // 2
    far = sorted(range(half, devices), key=lambda k: (k & 1, k & 2, k))
    across = [k for k in range(1, half) if k >= half // 2]
    beside = [k for k in range(1, half) if k < half // 2]
    if devices < 16:
        return [far + across + beside]
    return [
        far[:2] + beside[:1],
        far[2:4] + across[:2],
        far[4:6] + across[2:] + beside[1:2],
        far[6:] + beside[2:],
    ]


def body(hidden_states, qkv_weight, out_weight, cache_pages, context_lengths, new_units, old_pages):
    devices = lax.axis_size("tp")
    device = lax.axis_index("tp")
    requests = hidden_states.shape[0]
    pages_dev, page_rows, page_width = cache_pages.shape
    capacity = max(1, pages_dev // devices)
    total_units = new_units.shape[0]
    total_pages = old_pages.shape[0]
    pairwise = devices <= 16 and devices & (devices - 1) == 0

    if pairwise:
        plan = exchange_plan(devices)
        chunks, order = first_pack(
            new_units, old_pages, cache_pages, devices, capacity, plan[0], True
        )
        moved = [swap(c, k, devices) for c, k in zip(chunks, plan[0])]
    else:
        keys = list(range(devices))
        (packed,), order = first_pack(
            new_units, old_pages, cache_pages, devices, capacity, keys, False
        )
        arrived = lax.all_to_all(
            packed.reshape(devices, capacity, page_rows, page_width),
            "tp",
            split_axis=0,
            concat_axis=0,
            tiled=True,
        ).reshape(devices * capacity, page_rows, page_width)

    own_units = lax.dynamic_slice_in_dim(new_units, device * U_DEV, U_DEV)
    own_lengths = context_lengths[own_units // KVH]
    wanted = (
        own_units[:, None] * PER_UNIT + jnp.arange(PER_UNIT, dtype=jnp.int32)[None, :]
    ).reshape(pages_dev)
    source_pos = jnp.sum(
        jnp.where(
            wanted[:, None] == old_pages[None, :],
            jnp.arange(total_pages, dtype=jnp.int32)[None, :],
            0,
        ),
        axis=1,
    )
    source_dev = source_pos // pages_dev
    rank = jnp.sum(
        (
            (source_dev[:, None] == source_dev[None, :])
            & (source_pos[None, :] < source_pos[:, None])
        ).astype(jnp.int32),
        axis=1,
    )
    if pairwise:
        where = (source_dev ^ device) * capacity + rank
        spots = jnp.arange(devices * capacity, dtype=jnp.int32)
        slots = jnp.arange(pages_dev, dtype=jnp.int32)
        table = jnp.sum(jnp.where(where[None, :] == spots[:, None], slots[None, :], 0), axis=1)
    else:
        table = source_dev * capacity + rank

    flat_rows = hidden_states.reshape(requests * 2, D)
    flat_rows = flat_rows + jnp.minimum(order[0], 0).astype(jnp.bfloat16)
    own_part = lax.dot_general(
        flat_rows, qkv_weight, (((1,), (1,)), ((), ())), preferred_element_type=jnp.float32
    ).astype(jnp.bfloat16)
    own_requests, own_heads = own_units // KVH, own_units % KVH
    positions = own_lengths[:, None] + jnp.arange(2, dtype=jnp.int32)[None, :]
    cosine, sine = rope_tables(positions.reshape(2 * U_DEV))
    if pairwise:
        rows, span = gather_swaps(own_part, devices, True)
        turn = jnp.array([span.index(i) for i in range(devices)], jnp.int32)
        pieces = devices // KVH
        holders = own_heads[:, None] * pieces + jnp.arange(pieces, dtype=jnp.int32)[None, :]
        places = turn[(holders ^ device).reshape(U_DEV * pieces)]
        queries, fresh = own_rows(rows, places, own_requests, cosine, sine)
        new_cache, sums = None, None
        if len(plan) > 1:
            chunks = next_pack(order, cache_pages, own_part, capacity, plan[1])
            moved += [swap(c, k, devices) for c, k in zip(chunks, plan[1])]
            chunks = next_pack(order, cache_pages, queries, capacity, plan[2])
            moved += [swap(c, k, devices) for c, k in zip(chunks, plan[2])]
        at = 0
        keys = sum(plan, [])
        groups = [len(p) for p in plan[:-1]] + [len(plan[-1]) - 1, 1]
        for step, size in enumerate(groups):
            entries, sources = [], []
            for key, array in zip(keys[at : at + size], moved[at : at + size]):
                entries += [(len(sources), r, (key * capacity + r,)) for r in range(capacity)]
                sources.append(array)
            at += size
            if step == 0:
                entries = [(len(sources), (r,), (r,)) for r in range(capacity)] + entries
                sources.append(cache_pages)
            new_cache, sums, attended = place_pages(
                table,
                order,
                own_lengths,
                fresh,
                queries,
                sums,
                sources,
                entries,
                new_cache,
                step == len(groups) - 1,
            )
            if step == 0 and len(plan) > 1:
                chunks = next_pack(order, cache_pages, sums[0], capacity, plan[3])
                moved += [swap(c, k, devices) for c, k in zip(chunks, plan[3])]
    else:
        rows = lax.all_gather(own_part, "tp", axis=1, tiled=True)
        rows = rows.reshape(requests, 2, KVH, GROUP + 2, HD)
        rows = rows[own_requests, :, own_heads].astype(jnp.float32)
        turned = rotate(
            rows[:, :, : GROUP + 1],
            cosine.reshape(U_DEV, 2, 1, HD),
            sine.reshape(U_DEV, 2, 1, HD),
        )
        queries = turned[:, :, :GROUP].reshape(U_DEV, QROWS, HD)
        fresh = jnp.concatenate([turned[:, :, GROUP], rows[:, :, GROUP + 1]], axis=-1)
        fresh = fresh.reshape(2 * U_DEV, 2 * HD).astype(jnp.bfloat16).astype(jnp.float32)
        queries = queries.astype(jnp.bfloat16).astype(jnp.float32)
        entries = [(0, (w,), w) for w in range(pages_dev)]
        new_cache, sums, attended = place_pages(
            table, table, own_lengths, fresh, queries, None, [arrived], entries, None, True
        )

    slot_index = jnp.sum(
        jnp.where(
            new_units[None, :] == jnp.arange(total_units, dtype=jnp.int32)[:, None],
            jnp.arange(total_units, dtype=jnp.int32)[None, :],
            0,
        ),
        axis=1,
    )
    attended = attended.reshape(U_DEV, 2, GROUP * HD)
    if pairwise:
        heads, span = gather_swaps(attended, devices, False)
        turn = jnp.array([span.index(i) for i in range(devices)], jnp.int32)
        holder = turn[(slot_index // U_DEV) ^ device]
        heads = heads.reshape(total_units, 2, GROUP * HD)[holder * U_DEV + slot_index % U_DEV]
    else:
        heads = lax.all_gather(attended, "tp", axis=0, tiled=True)[slot_index]
    logical = (
        heads.reshape(requests, KVH, 2, GROUP * HD)
        .transpose(0, 2, 1, 3)
        .reshape(requests * 2, HEADS * HD)
    )
    mixed_rows = lax.dot_general(
        logical, out_weight, (((1,), (1,)), ((), ())), preferred_element_type=jnp.float32
    )
    mixed_rows = mixed_rows.astype(jnp.bfloat16).reshape(requests, 2, out_weight.shape[0])
    return (mixed_rows, new_cache)


def solution(mesh):
    in_specs = (
        P("group", None, None),
        P("tp", None),
        P("tp", None),
        P(("group", "tp"), None, None),
        P("group"),
        P("group"),
        P("group"),
    )
    out_specs = (P("group", None, "tp"), P(("group", "tp"), None, None))
    return jax.shard_map(body, mesh=mesh, in_specs=in_specs, out_specs=out_specs, check_vma=False)
```

```python
import functools
import math

import jax
import jax.numpy as jnp
from jax import lax
from jax.experimental import pallas as pl
from jax.experimental.pallas import tpu as pltpu
from jax.sharding import PartitionSpec as P

D = 8192
HEADS = 64
KVH = 8
HD = 128
U_DEV = 4
MAXCTX = 2048
PAGE = 128
GROUP = HEADS // KVH
QROWS = 2 * GROUP
PER_UNIT = MAXCTX // PAGE
VMEM_LIMIT = 56 * 1024 * 1024

rope_base = 10000.0


def rope_tables(positions):
    half_dim = HD // 2
    frequency = rope_base ** (-(jnp.arange(half_dim, dtype=jnp.float32) * 2.0 / HD))
    angles = positions.astype(jnp.float32)[..., None] * frequency
    cosine = jnp.concatenate([jnp.cos(angles), jnp.cos(angles)], axis=-1)
    sine = jnp.concatenate([-jnp.sin(angles), jnp.sin(angles)], axis=-1)
    return cosine, sine


def rotate(values, cosine, sine):
    half_dim = HD // 2
    turned = jnp.concatenate([values[..., half_dim:], values[..., :half_dim]], axis=-1)
    return values * cosine + turned * sine


def any_spec():
    return pl.BlockSpec(memory_space=pl.ANY)


def smem_spec():
    return pl.BlockSpec(memory_space=pltpu.SMEM)


def vmem_spec():
    return pl.BlockSpec(memory_space=pltpu.VMEM)


def load_order(devices, capacity, relative, units_ref, old_ref, order_ref, slots, count):
    device = lax.axis_index("tp")
    total_units = units_ref.shape[0]
    pages_dev = old_ref.shape[0] // devices

    def clear(t, carry):
        count[t] = 0
        return carry

    def empty(t, carry):
        order_ref[t] = 0
        return carry

    def invert(q, carry):
        slots[units_ref[q]] = q
        return carry

    def assign(i, carry):
        unit = old_ref[device * pages_dev + i] // PER_UNIT
        target = slots[unit] // U_DEV
        if relative:
            target = target ^ device
        rank = count[target]
        count[target] = rank + 1
        order_ref[target * capacity + rank] = i
        return carry

    lax.fori_loop(0, devices, clear, 0, unroll=8)
    if devices * capacity > pages_dev:
        lax.fori_loop(0, devices * capacity, empty, 0, unroll=8)
    lax.fori_loop(0, total_units, invert, 0, unroll=8)
    lax.fori_loop(0, pages_dev, assign, 0, unroll=8)


def move_pages(capacity, items, order_ref, pages_ref, outs, stage, load_sem, store_sem):
    loads, stores, slot = [], [], 0
    for key, first, count in items:
        for r in range(first, first + count):
            copy = pltpu.make_async_copy(
                pages_ref.at[order_ref[key * capacity + r]], stage.at[slot], load_sem.at[slot]
            )
            copy.start()
            loads.append(copy)
            slot += 1
    slot = 0
    for n, (key, first, count) in enumerate(items):
        for copy in loads[slot : slot + count]:
            copy.wait()
        target = outs[n] if len(outs) > 1 else outs[0].at[pl.ds(slot, count)]
        copy = pltpu.make_async_copy(stage.at[pl.ds(slot, count)], target, store_sem.at[n])
        copy.start()
        stores.append(copy)
        slot += count
    for copy in stores:
        copy.wait()


def first_pack_kernel(devices, capacity, keys, relative, units_ref, old_ref, pages_ref, *rest):
    outs = rest[:-6]
    order_ref, slots, count, stage, load_sem, store_sem = rest[-6:]
    load_order(devices, capacity, relative, units_ref, old_ref, order_ref, slots, count)
    move_pages(capacity, keys, order_ref, pages_ref, outs, stage, load_sem, store_sem)


def next_pack_kernel(capacity, keys, order_ref, pages_ref, after_ref, *rest):
    outs = rest[:-3]
    stage, load_sem, store_sem = rest[-3:]
    move_pages(capacity, keys, order_ref, pages_ref, outs, stage, load_sem, store_sem)


def pack_scratch(count, pages):
    return [
        pltpu.VMEM((count,) + pages.shape[1:], pages.dtype),
        pltpu.SemaphoreType.DMA((count,)),
        pltpu.SemaphoreType.DMA((count,)),
    ]


def first_pack(new_units, old_pages, pages, devices, capacity, keys, relative):
    shape = pages.shape[1:]
    total = sum(count for _, _, count in keys)
    if relative:
        outs = [jax.ShapeDtypeStruct((count,) + shape, pages.dtype) for _, _, count in keys]
    else:
        outs = [jax.ShapeDtypeStruct((total,) + shape, pages.dtype)]
    result = pl.pallas_call(
        functools.partial(first_pack_kernel, devices, capacity, keys, relative),
        out_shape=tuple(outs) + (jax.ShapeDtypeStruct((devices * capacity,), jnp.int32),),
        in_specs=[smem_spec(), smem_spec(), any_spec()],
        out_specs=tuple(any_spec() for _ in outs) + (smem_spec(),),
        scratch_shapes=[
            pltpu.SMEM(new_units.shape, jnp.int32),
            pltpu.SMEM((devices,), jnp.int32),
        ]
        + pack_scratch(total, pages),
        compiler_params=pltpu.CompilerParams(vmem_limit_bytes=VMEM_LIMIT),
        name="first_pack",
    )(new_units, old_pages, pages)
    return result[:-1], result[-1]


def next_pack(order, pages, after, capacity, keys):
    shape = pages.shape[1:]
    total = sum(count for _, _, count in keys)
    return pl.pallas_call(
        functools.partial(next_pack_kernel, capacity, keys),
        out_shape=tuple(
            jax.ShapeDtypeStruct((count,) + shape, pages.dtype) for _, _, count in keys
        ),
        in_specs=[smem_spec(), any_spec(), any_spec()],
        out_specs=tuple(any_spec() for _ in keys),
        scratch_shapes=pack_scratch(total, pages),
        compiler_params=pltpu.CompilerParams(vmem_limit_bytes=VMEM_LIMIT),
        name="next_pack",
    )(order, pages, after)


def attend(query, keys, values, limit):
    scale = 1.0 / math.sqrt(HD)
    scores = (
        lax.dot_general(query, keys, (((1,), (1,)), ((), ())), preferred_element_type=jnp.float32)
        * scale
    )
    lane = lax.broadcasted_iota(jnp.int32, scores.shape, 1)
    weights = jnp.where(lane < limit, jnp.exp(scores), 0.0)
    total = jnp.sum(weights, axis=1, keepdims=True)
    weighted = jnp.dot(weights.astype(jnp.bfloat16), values, preferred_element_type=jnp.float32)
    return weighted, total


ALIGN = 16


def place_kernel(entries, started, finish, *refs):
    refs = list(refs)
    table_ref, order_ref, length_ref, fresh_ref = refs[:4]
    refs = refs[4:]
    queries_ref = refs.pop(0)
    if started:
        weighted_in, total_in = refs.pop(0), refs.pop(0)
    sources = 1 + max(source for source, _, _ in entries)
    source_refs, refs = refs[:sources], refs[sources:]
    if started:
        refs.pop(0)
    out_ref, weighted_ref, total_ref = refs[:3]
    refs = refs[3:]
    attended_ref = refs.pop(0) if finish else None
    stage, load_sem, store_sem = refs
    if started:
        weighted_ref[...] = weighted_in[...]
        total_ref[...] = total_in[...]
    else:
        own_terms(queries_ref, fresh_ref, weighted_ref, total_ref)
    loads = []
    for n, (source, index, _) in enumerate(entries):
        index = order_ref[index[0]] if isinstance(index, tuple) else index
        copy = pltpu.make_async_copy(
            source_refs[source].at[index], stage.at[n], load_sem.at[n]
        )
        copy.start()
        loads.append(copy)
    row = lax.broadcasted_iota(jnp.int32, (ALIGN, 2 * HD), 0)
    stores = []
    for n, (_, _, key) in enumerate(entries):
        w = table_ref[key[0]] if isinstance(key, tuple) else key
        unit, part = w // PER_UNIT, w % PER_UNIT
        length = length_ref[unit]
        loads[n].wait()
        for j in range(2):
            position = length + j

            @pl.when(position // PAGE == part)
            def _():
                inside = position % PAGE
                rows = pl.ds(pl.multiple_of(inside // ALIGN * ALIGN, ALIGN), ALIGN)
                block = stage[n, rows, :].astype(jnp.float32)
                token = fresh_ref[pl.ds(2 * unit + j, 1), :]
                block = jnp.where(row == inside % ALIGN, token, block)
                stage[n, rows, :] = block.astype(jnp.bfloat16)

        copy = pltpu.make_async_copy(stage.at[n], out_ref.at[w], store_sem.at[n])
        copy.start()
        stores.append(copy)
    group = 4
    for first in range(0, len(entries), group):
        found = []
        for n in range(first, min(first + group, len(entries))):
            key = entries[n][2]
            w = table_ref[key[0]] if isinstance(key, tuple) else key
            unit, part = w // PER_UNIT, w % PER_UNIT
            weighted, total = attend(
                queries_ref[unit].astype(jnp.bfloat16),
                stage[n, :, :HD],
                stage[n, :, HD:],
                length_ref[unit] - part * PAGE,
            )
            found.append((unit, weighted, total))
        for unit, weighted, total in found:
            weighted_ref[unit] += weighted
            total_ref[unit] += jnp.broadcast_to(total, (QROWS, HD))
    if finish:
        attended_ref[...] = (weighted_ref[...] / total_ref[...]).astype(jnp.bfloat16)
    for copy in stores:
        copy.wait()


def own_terms(queries_ref, fresh_ref, weighted_ref, total_ref):
    scale = 1.0 / math.sqrt(HD)
    row = lax.broadcasted_iota(jnp.int32, (QROWS, 1), 0)
    for unit in range(U_DEV):
        query = queries_ref[unit]
        weighted = jnp.zeros((QROWS, HD), jnp.float32)
        total = jnp.zeros((QROWS, 1), jnp.float32)
        for j in range(2):
            at = 2 * unit + j
            key = fresh_ref[at : at + 1, :HD]
            value = fresh_ref[at : at + 1, HD:]
            score = jnp.sum(query * key, axis=1, keepdims=True) * scale
            weight = jnp.where(row >= j * GROUP, jnp.exp(score), 0.0)
            total = total + weight
            weighted = weighted + weight.astype(jnp.bfloat16).astype(jnp.float32) * value
        weighted_ref[unit] = weighted
        total_ref[unit] = jnp.broadcast_to(total, (QROWS, HD))


def place_pages(table, order, lengths, fresh, queries, sums, sources, entries, cache, finish):
    started = cache is not None
    page_shape = sources[0].shape[1:]
    pages_dev = U_DEV * PER_UNIT
    args = [table, order, lengths, fresh, queries]
    specs = [smem_spec()] * 3 + [vmem_spec()] * 2
    if started:
        args += list(sums)
        specs += [vmem_spec()] * 2
    args += list(sources)
    specs += [any_spec()] * len(sources)
    aliases = {}
    if started:
        aliases = {len(args): 0}
        args.append(cache)
        specs.append(any_spec())
    outs = [jax.ShapeDtypeStruct((pages_dev,) + page_shape, jnp.bfloat16)]
    outs += [jax.ShapeDtypeStruct((U_DEV, QROWS, HD), jnp.float32)] * 2
    out_specs = [any_spec()] + [vmem_spec()] * 2
    if finish:
        outs.append(jax.ShapeDtypeStruct((U_DEV, QROWS, HD), jnp.bfloat16))
        out_specs.append(vmem_spec())
    count = len(entries)
    result = pl.pallas_call(
        functools.partial(place_kernel, entries, started, finish),
        out_shape=tuple(outs),
        in_specs=specs,
        out_specs=tuple(out_specs),
        input_output_aliases=aliases,
        scratch_shapes=[
            pltpu.VMEM((count,) + page_shape, jnp.bfloat16),
            pltpu.SemaphoreType.DMA((count,)),
            pltpu.SemaphoreType.DMA((count,)),
        ],
        compiler_params=pltpu.CompilerParams(vmem_limit_bytes=VMEM_LIMIT),
        name="place_pages",
    )(*args)
    return result[0], result[1:3], result[3] if finish else None


def own_rows_kernel(rows_ref, place_ref, request_ref, cosine_ref, sine_ref, queries_ref, fresh_ref):
    width = rows_ref.shape[2]
    pieces = place_ref.shape[0] // U_DEV
    row = lax.broadcasted_iota(jnp.int32, rows_ref.shape[1:], 0)
    half_dim = HD // 2
    for unit in range(U_DEV):
        found = []
        for piece in range(pieces):
            block = rows_ref[place_ref[unit * pieces + piece]].astype(jnp.float32)
            picked = [
                jnp.sum(
                    jnp.where(row == 2 * request_ref[unit] + j, block, 0.0), axis=0, keepdims=True
                )
                for j in range(2)
            ]
            for at in range(0, width, HD):
                found.append([line[:, at : at + HD] for line in picked])
        for j in range(2):
            heads = jnp.concatenate([head[j] for head in found[: GROUP + 1]], axis=0)
            turned = jnp.concatenate([heads[:, half_dim:], heads[:, :half_dim]], axis=1)
            cosine = cosine_ref[2 * unit + j : 2 * unit + j + 1, :]
            sine = sine_ref[2 * unit + j : 2 * unit + j + 1, :]
            heads = (heads * cosine + turned * sine).astype(jnp.bfloat16).astype(jnp.float32)
            queries_ref[unit, j * GROUP : (j + 1) * GROUP, :] = heads[:GROUP]
            fresh_ref[2 * unit + j : 2 * unit + j + 1, :HD] = heads[GROUP:]
            fresh_ref[2 * unit + j : 2 * unit + j + 1, HD:] = found[GROUP + 1][j]


def own_rows(rows, places, requests, cosine, sine):
    queries, fresh = pl.pallas_call(
        own_rows_kernel,
        out_shape=(
            jax.ShapeDtypeStruct((U_DEV, QROWS, HD), jnp.float32),
            jax.ShapeDtypeStruct((2 * U_DEV, 2 * HD), jnp.float32),
        ),
        in_specs=[vmem_spec(), smem_spec(), smem_spec(), vmem_spec(), vmem_spec()],
        out_specs=(vmem_spec(), vmem_spec()),
        name="own_rows",
    )(rows, places, requests, cosine, sine)
    return queries, fresh


def swap(values, key, devices):
    return lax.ppermute(values, "tp", [(i, i ^ key) for i in range(devices)])


def gather_swaps(values, devices, direct):
    values = values[None]
    step = devices // 2
    span = [0]
    if direct and devices >= 4:
        keys = [step, step // 2, step + step // 2]
        values = jnp.concatenate([values] + [swap(values, k, devices) for k in keys], axis=0)
        span = [0] + keys
        step //= 4
    while step:
        values = jnp.concatenate([values, swap(values, step, devices)], axis=0)
        span = span + [s ^ step for s in span]
        step //= 2
    return values, span


def exchange_plan(devices, capacity):
    half = devices // 2
    far = sorted(range(half, devices), key=lambda k: (k & 1, k & 2, k))
    across = [k for k in range(1, half) if k >= half // 2]
    beside = [k for k in range(1, half) if k < half // 2]
    whole = lambda keys: [(k, 0, capacity) for k in keys]
    if devices < 16:
        return [whole(far + across + beside)]
    cut = max(1, capacity // 2)
    head = [(far[0], 0, cut)] + [(far[0], cut, capacity - cut)] * (capacity > cut)
    return [
        head + whole(far[1:2] + beside[:1]),
        whole(far[2:4] + across[:2]),
        whole(far[4:6] + across[2:] + beside[1:2]),
        whole(beside[2:] + far[6:]),
    ]


def body(hidden_states, qkv_weight, out_weight, cache_pages, context_lengths, new_units, old_pages):
    devices = lax.axis_size("tp")
    device = lax.axis_index("tp")
    requests = hidden_states.shape[0]
    pages_dev, page_rows, page_width = cache_pages.shape
    capacity = max(1, pages_dev // devices)
    total_units = new_units.shape[0]
    total_pages = old_pages.shape[0]
    pairwise = devices <= 16 and devices & (devices - 1) == 0

    if pairwise:
        plan = exchange_plan(devices, capacity)
        chunks, order = first_pack(
            new_units, old_pages, cache_pages, devices, capacity, plan[0], True
        )
        moved = [swap(c, k[0], devices) for c, k in zip(chunks, plan[0])]
    else:
        keys = [(k, 0, capacity) for k in range(devices)]
        (packed,), order = first_pack(
            new_units, old_pages, cache_pages, devices, capacity, keys, False
        )
        arrived = lax.all_to_all(
            packed.reshape(devices, capacity, page_rows, page_width),
            "tp",
            split_axis=0,
            concat_axis=0,
            tiled=True,
        ).reshape(devices * capacity, page_rows, page_width)

    own_units = lax.dynamic_slice_in_dim(new_units, device * U_DEV, U_DEV)
    own_lengths = context_lengths[own_units // KVH]
    wanted = (
        own_units[:, None] * PER_UNIT + jnp.arange(PER_UNIT, dtype=jnp.int32)[None, :]
    ).reshape(pages_dev)
    source_pos = jnp.sum(
        jnp.where(
            wanted[:, None] == old_pages[None, :],
            jnp.arange(total_pages, dtype=jnp.int32)[None, :],
            0,
        ),
        axis=1,
    )
    source_dev = source_pos // pages_dev
    rank = jnp.sum(
        (
            (source_dev[:, None] == source_dev[None, :])
            & (source_pos[None, :] < source_pos[:, None])
        ).astype(jnp.int32),
        axis=1,
    )
    if pairwise:
        where = (source_dev ^ device) * capacity + rank
        spots = jnp.arange(devices * capacity, dtype=jnp.int32)
        slots = jnp.arange(pages_dev, dtype=jnp.int32)
        table = jnp.sum(jnp.where(where[None, :] == spots[:, None], slots[None, :], 0), axis=1)
    else:
        table = source_dev * capacity + rank

    flat_rows = hidden_states.reshape(requests * 2, D)
    if pairwise:
        flat_rows, _ = lax.optimization_barrier((flat_rows, moved[0]))
    own_part = lax.dot_general(
        flat_rows, qkv_weight, (((1,), (1,)), ((), ())), preferred_element_type=jnp.float32
    ).astype(jnp.bfloat16)
    own_requests, own_heads = own_units // KVH, own_units % KVH
    positions = own_lengths[:, None] + jnp.arange(2, dtype=jnp.int32)[None, :]
    cosine, sine = rope_tables(positions.reshape(2 * U_DEV))
    if pairwise:
        rows, span = gather_swaps(own_part, devices, True)
        turn = jnp.array([span.index(i) for i in range(devices)], jnp.int32)
        pieces = devices // KVH
        holders = own_heads[:, None] * pieces + jnp.arange(pieces, dtype=jnp.int32)[None, :]
        places = turn[(holders ^ device).reshape(U_DEV * pieces)]
        queries, fresh = own_rows(rows, places, own_requests, cosine, sine)
        new_cache, sums = None, None
        if len(plan) > 1:
            chunks = next_pack(order, cache_pages, own_part, capacity, plan[1])
            moved += [swap(c, k[0], devices) for c, k in zip(chunks, plan[1])]
            chunks = next_pack(order, cache_pages, moved[2], capacity, plan[2])
            moved += [swap(c, k[0], devices) for c, k in zip(chunks, plan[2])]
        at = 0
        keys = sum(plan, [])
        groups = [len(p) for p in plan[:-1]] + [len(plan[-1]) - 1, 1]
        for step, size in enumerate(groups):
            entries, sources = [], []
            for (key, low, count), array in zip(keys[at : at + size], moved[at : at + size]):
                entries += [
                    (len(sources), r, (key * capacity + low + r,)) for r in range(count)
                ]
                sources.append(array)
            at += size
            if step == 0:
                entries = [(len(sources), (r,), (r,)) for r in range(capacity)] + entries
                sources.append(cache_pages)
            new_cache, sums, attended = place_pages(
                table,
                order,
                own_lengths,
                fresh,
                queries,
                sums,
                sources,
                entries,
                new_cache,
                step == len(groups) - 1,
            )
            if step == 0 and len(plan) > 1:
                chunks = next_pack(order, cache_pages, sums[0], capacity, plan[3])
                moved += [swap(c, k[0], devices) for c, k in zip(chunks, plan[3])]
    else:
        rows = lax.all_gather(own_part, "tp", axis=1, tiled=True)
        rows = rows.reshape(requests, 2, KVH, GROUP + 2, HD)
        rows = rows[own_requests, :, own_heads].astype(jnp.float32)
        turned = rotate(
            rows[:, :, : GROUP + 1],
            cosine.reshape(U_DEV, 2, 1, HD),
            sine.reshape(U_DEV, 2, 1, HD),
        )
        queries = turned[:, :, :GROUP].reshape(U_DEV, QROWS, HD)
        fresh = jnp.concatenate([turned[:, :, GROUP], rows[:, :, GROUP + 1]], axis=-1)
        fresh = fresh.reshape(2 * U_DEV, 2 * HD).astype(jnp.bfloat16).astype(jnp.float32)
        queries = queries.astype(jnp.bfloat16).astype(jnp.float32)
        entries = [(0, (w,), w) for w in range(pages_dev)]
        new_cache, sums, attended = place_pages(
            table, table, own_lengths, fresh, queries, None, [arrived], entries, None, True
        )

    slot_index = jnp.sum(
        jnp.where(
            new_units[None, :] == jnp.arange(total_units, dtype=jnp.int32)[:, None],
            jnp.arange(total_units, dtype=jnp.int32)[None, :],
            0,
        ),
        axis=1,
    )
    attended = attended.reshape(U_DEV, 2, GROUP * HD)
    if pairwise:
        heads, span = gather_swaps(attended, devices, False)
        turn = jnp.array([span.index(i) for i in range(devices)], jnp.int32)
        holder = turn[(slot_index // U_DEV) ^ device]
        heads = heads.reshape(total_units, 2, GROUP * HD)[holder * U_DEV + slot_index % U_DEV]
    else:
        heads = lax.all_gather(attended, "tp", axis=0, tiled=True)[slot_index]
    logical = (
        heads.reshape(requests, KVH, 2, GROUP * HD)
        .transpose(0, 2, 1, 3)
        .reshape(requests * 2, HEADS * HD)
    )
    mixed_rows = lax.dot_general(
        logical, out_weight, (((1,), (1,)), ((), ())), preferred_element_type=jnp.float32
    )
    mixed_rows = mixed_rows.astype(jnp.bfloat16).reshape(requests, 2, out_weight.shape[0])
    return (mixed_rows, new_cache)


def solution(mesh):
    in_specs = (
        P("group", None, None),
        P("tp", None),
        P("tp", None),
        P(("group", "tp"), None, None),
        P("group"),
        P("group"),
        P("group"),
    )
    out_specs = (P("group", None, "tp"), P(("group", "tp"), None, None))
    return jax.shard_map(body, mesh=mesh, in_specs=in_specs, out_specs=out_specs, check_vma=False)
```

```python
import functools
import math

import jax
import jax.numpy as jnp
from jax import lax
from jax.experimental import pallas as pl
from jax.experimental.pallas import tpu as pltpu
from jax.sharding import PartitionSpec as P

D = 8192
HEADS = 64
KVH = 8
HD = 128
U_DEV = 4
MAXCTX = 2048
PAGE = 128
GROUP = HEADS // KVH
QROWS = 2 * GROUP
PER_UNIT = MAXCTX // PAGE
VMEM_LIMIT = 56 * 1024 * 1024

rope_base = 10000.0


def rope_tables(positions):
    half_dim = HD // 2
    frequency = rope_base ** (-(jnp.arange(half_dim, dtype=jnp.float32) * 2.0 / HD))
    angles = positions.astype(jnp.float32)[..., None] * frequency
    cosine = jnp.concatenate([jnp.cos(angles), jnp.cos(angles)], axis=-1)
    sine = jnp.concatenate([-jnp.sin(angles), jnp.sin(angles)], axis=-1)
    return cosine, sine


def rotate(values, cosine, sine):
    half_dim = HD // 2
    turned = jnp.concatenate([values[..., half_dim:], values[..., :half_dim]], axis=-1)
    return values * cosine + turned * sine


def any_spec():
    return pl.BlockSpec(memory_space=pl.ANY)


def smem_spec():
    return pl.BlockSpec(memory_space=pltpu.SMEM)


def vmem_spec():
    return pl.BlockSpec(memory_space=pltpu.VMEM)


def load_order(devices, capacity, relative, units_ref, old_ref, order_ref, slots, count):
    device = lax.axis_index("tp")
    total_units = units_ref.shape[0]
    pages_dev = old_ref.shape[0] // devices

    def clear(t, carry):
        count[t] = 0
        return carry

    def empty(t, carry):
        order_ref[t] = 0
        return carry

    def invert(q, carry):
        slots[units_ref[q]] = q
        return carry

    def assign(i, carry):
        unit = old_ref[device * pages_dev + i] // PER_UNIT
        target = slots[unit] // U_DEV
        if relative:
            target = target ^ device
        rank = count[target]
        count[target] = rank + 1
        order_ref[target * capacity + rank] = i
        return carry

    lax.fori_loop(0, devices, clear, 0, unroll=8)
    if devices * capacity > pages_dev:
        lax.fori_loop(0, devices * capacity, empty, 0, unroll=8)
    lax.fori_loop(0, total_units, invert, 0, unroll=8)
    lax.fori_loop(0, pages_dev, assign, 0, unroll=8)


def move_pages(outs_pages, capacity, order_ref, sources, outs, stage, load_sem, store_sem):
    loads, stores = [], []
    for source, key, r in sum(outs_pages, []):
        slot = len(loads)
        index = order_ref[key * capacity + r] if source == 0 else r
        copy = pltpu.make_async_copy(
            sources[source].at[index], stage.at[slot], load_sem.at[slot]
        )
        copy.start()
        loads.append(copy)
    slot = 0
    for n, pages in enumerate(outs_pages):
        count = len(pages)
        for copy in loads[slot : slot + count]:
            copy.wait()
        copy = pltpu.make_async_copy(stage.at[pl.ds(slot, count)], outs[n], store_sem.at[n])
        copy.start()
        stores.append(copy)
        slot += count
    for copy in stores:
        copy.wait()


def first_pack_kernel(
    devices, capacity, outs_pages, relative, units_ref, old_ref, pages_ref, *rest
):
    outs = rest[:-6]
    order_ref, slots, count, stage, load_sem, store_sem = rest[-6:]
    load_order(devices, capacity, relative, units_ref, old_ref, order_ref, slots, count)
    move_pages(
        outs_pages, capacity, order_ref, [pages_ref], outs, stage, load_sem, store_sem
    )


def next_pack_kernel(capacity, outs_pages, sources, order_ref, *rest):
    source_refs, outs = rest[:sources], rest[sources:-3]
    stage, load_sem, store_sem = rest[-3:]
    move_pages(
        outs_pages, capacity, order_ref, source_refs, outs, stage, load_sem, store_sem
    )


def pack_shapes(outs_pages, pages):
    total = sum(len(p) for p in outs_pages)
    shapes = [jax.ShapeDtypeStruct((len(p),) + pages.shape[1:], pages.dtype) for p in outs_pages]
    scratch = [
        pltpu.VMEM((total,) + pages.shape[1:], pages.dtype),
        pltpu.SemaphoreType.DMA((total,)),
        pltpu.SemaphoreType.DMA((len(outs_pages),)),
    ]
    return shapes, scratch


def first_pack(new_units, old_pages, pages, devices, capacity, outs_pages, relative):
    outs, scratch = pack_shapes(outs_pages, pages)
    result = pl.pallas_call(
        functools.partial(first_pack_kernel, devices, capacity, outs_pages, relative),
        out_shape=tuple(outs) + (jax.ShapeDtypeStruct((devices * capacity,), jnp.int32),),
        in_specs=[smem_spec(), smem_spec(), any_spec()],
        out_specs=tuple(any_spec() for _ in outs) + (smem_spec(),),
        scratch_shapes=[
            pltpu.SMEM(new_units.shape, jnp.int32),
            pltpu.SMEM((devices,), jnp.int32),
        ]
        + scratch,
        compiler_params=pltpu.CompilerParams(vmem_limit_bytes=VMEM_LIMIT),
        name="first_pack",
    )(new_units, old_pages, pages)
    return result[:-1], result[-1]


def next_pack(order, sources, capacity, outs_pages):
    outs, scratch = pack_shapes(outs_pages, sources[0])
    return pl.pallas_call(
        functools.partial(next_pack_kernel, capacity, outs_pages, len(sources)),
        out_shape=tuple(outs),
        in_specs=[smem_spec()] + [any_spec()] * len(sources),
        out_specs=tuple(any_spec() for _ in outs),
        scratch_shapes=scratch,
        compiler_params=pltpu.CompilerParams(vmem_limit_bytes=VMEM_LIMIT),
        name="next_pack",
    )(order, *sources)


def attend(query, keys, values, limit):
    scale = 1.0 / math.sqrt(HD)
    scores = (
        lax.dot_general(query, keys, (((1,), (1,)), ((), ())), preferred_element_type=jnp.float32)
        * scale
    )
    lane = lax.broadcasted_iota(jnp.int32, scores.shape, 1)
    weights = jnp.where(lane < limit, jnp.exp(scores), 0.0)
    total = jnp.sum(weights, axis=1, keepdims=True)
    weighted = jnp.dot(weights.astype(jnp.bfloat16), values, preferred_element_type=jnp.float32)
    return weighted, total


ALIGN = 16


def place_kernel(entries, started, finish, *refs):
    refs = list(refs)
    table_ref, order_ref, length_ref, fresh_ref = refs[:4]
    refs = refs[4:]
    queries_ref = refs.pop(0)
    if started:
        weighted_in, total_in = refs.pop(0), refs.pop(0)
    sources = 1 + max(source for source, _, _ in entries)
    source_refs, refs = refs[:sources], refs[sources:]
    if started:
        refs.pop(0)
    out_ref, weighted_ref, total_ref = refs[:3]
    refs = refs[3:]
    attended_ref = refs.pop(0) if finish else None
    stage, load_sem, store_sem = refs
    if started:
        weighted_ref[...] = weighted_in[...]
        total_ref[...] = total_in[...]
    else:
        own_terms(queries_ref, fresh_ref, weighted_ref, total_ref)
    loads = []
    for n, (source, index, _) in enumerate(entries):
        index = order_ref[index[0]] if isinstance(index, tuple) else index
        copy = pltpu.make_async_copy(
            source_refs[source].at[index], stage.at[n], load_sem.at[n]
        )
        copy.start()
        loads.append(copy)
    row = lax.broadcasted_iota(jnp.int32, (ALIGN, 2 * HD), 0)
    stores = []
    for n, (_, _, key) in enumerate(entries):
        w = table_ref[key[0]] if isinstance(key, tuple) else key
        unit, part = w // PER_UNIT, w % PER_UNIT
        length = length_ref[unit]
        loads[n].wait()
        for j in range(2):
            position = length + j

            @pl.when(position // PAGE == part)
            def _():
                inside = position % PAGE
                rows = pl.ds(pl.multiple_of(inside // ALIGN * ALIGN, ALIGN), ALIGN)
                block = stage[n, rows, :].astype(jnp.float32)
                token = fresh_ref[pl.ds(2 * unit + j, 1), :]
                block = jnp.where(row == inside % ALIGN, token, block)
                stage[n, rows, :] = block.astype(jnp.bfloat16)

        copy = pltpu.make_async_copy(stage.at[n], out_ref.at[w], store_sem.at[n])
        copy.start()
        stores.append(copy)
    group = 4
    for first in range(0, len(entries), group):
        found = []
        for n in range(first, min(first + group, len(entries))):
            key = entries[n][2]
            w = table_ref[key[0]] if isinstance(key, tuple) else key
            unit, part = w // PER_UNIT, w % PER_UNIT
            weighted, total = attend(
                queries_ref[unit].astype(jnp.bfloat16),
                stage[n, :, :HD],
                stage[n, :, HD:],
                length_ref[unit] - part * PAGE,
            )
            found.append((unit, weighted, total))
        for unit, weighted, total in found:
            weighted_ref[unit] += weighted
            total_ref[unit] += jnp.broadcast_to(total, (QROWS, HD))
    if finish:
        attended_ref[...] = (weighted_ref[...] / total_ref[...]).astype(jnp.bfloat16)
    for copy in stores:
        copy.wait()


def own_terms(queries_ref, fresh_ref, weighted_ref, total_ref):
    scale = 1.0 / math.sqrt(HD)
    row = lax.broadcasted_iota(jnp.int32, (QROWS, 1), 0)
    for unit in range(U_DEV):
        query = queries_ref[unit]
        weighted = jnp.zeros((QROWS, HD), jnp.float32)
        total = jnp.zeros((QROWS, 1), jnp.float32)
        for j in range(2):
            at = 2 * unit + j
            key = fresh_ref[at : at + 1, :HD]
            value = fresh_ref[at : at + 1, HD:]
            score = jnp.sum(query * key, axis=1, keepdims=True) * scale
            weight = jnp.where(row >= j * GROUP, jnp.exp(score), 0.0)
            total = total + weight
            weighted = weighted + weight.astype(jnp.bfloat16).astype(jnp.float32) * value
        weighted_ref[unit] = weighted
        total_ref[unit] = jnp.broadcast_to(total, (QROWS, HD))


def place_pages(table, order, lengths, fresh, queries, sums, sources, entries, cache, finish):
    started = cache is not None
    page_shape = sources[0].shape[1:]
    pages_dev = U_DEV * PER_UNIT
    args = [table, order, lengths, fresh, queries]
    specs = [smem_spec()] * 3 + [vmem_spec()] * 2
    if started:
        args += list(sums)
        specs += [vmem_spec()] * 2
    args += list(sources)
    specs += [any_spec()] * len(sources)
    aliases = {}
    if started:
        aliases = {len(args): 0}
        args.append(cache)
        specs.append(any_spec())
    outs = [jax.ShapeDtypeStruct((pages_dev,) + page_shape, jnp.bfloat16)]
    outs += [jax.ShapeDtypeStruct((U_DEV, QROWS, HD), jnp.float32)] * 2
    out_specs = [any_spec()] + [vmem_spec()] * 2
    if finish:
        outs.append(jax.ShapeDtypeStruct((U_DEV, QROWS, HD), jnp.bfloat16))
        out_specs.append(vmem_spec())
    count = len(entries)
    result = pl.pallas_call(
        functools.partial(place_kernel, entries, started, finish),
        out_shape=tuple(outs),
        in_specs=specs,
        out_specs=tuple(out_specs),
        input_output_aliases=aliases,
        scratch_shapes=[
            pltpu.VMEM((count,) + page_shape, jnp.bfloat16),
            pltpu.SemaphoreType.DMA((count,)),
            pltpu.SemaphoreType.DMA((count,)),
        ],
        compiler_params=pltpu.CompilerParams(vmem_limit_bytes=VMEM_LIMIT),
        name="place_pages",
    )(*args)
    return result[0], result[1:3], result[3] if finish else None


def own_rows_kernel(rows_ref, place_ref, request_ref, cosine_ref, sine_ref, queries_ref, fresh_ref):
    width = rows_ref.shape[2]
    pieces = place_ref.shape[0] // U_DEV
    row = lax.broadcasted_iota(jnp.int32, rows_ref.shape[1:], 0)
    half_dim = HD // 2
    for unit in range(U_DEV):
        found = []
        for piece in range(pieces):
            block = rows_ref[place_ref[unit * pieces + piece]].astype(jnp.float32)
            picked = [
                jnp.sum(
                    jnp.where(row == 2 * request_ref[unit] + j, block, 0.0), axis=0, keepdims=True
                )
                for j in range(2)
            ]
            for at in range(0, width, HD):
                found.append([line[:, at : at + HD] for line in picked])
        for j in range(2):
            heads = jnp.concatenate([head[j] for head in found[: GROUP + 1]], axis=0)
            turned = jnp.concatenate([heads[:, half_dim:], heads[:, :half_dim]], axis=1)
            cosine = cosine_ref[2 * unit + j : 2 * unit + j + 1, :]
            sine = sine_ref[2 * unit + j : 2 * unit + j + 1, :]
            heads = (heads * cosine + turned * sine).astype(jnp.bfloat16).astype(jnp.float32)
            queries_ref[unit, j * GROUP : (j + 1) * GROUP, :] = heads[:GROUP]
            fresh_ref[2 * unit + j : 2 * unit + j + 1, :HD] = heads[GROUP:]
            fresh_ref[2 * unit + j : 2 * unit + j + 1, HD:] = found[GROUP + 1][j]


def own_rows(rows, places, requests, cosine, sine):
    queries, fresh = pl.pallas_call(
        own_rows_kernel,
        out_shape=(
            jax.ShapeDtypeStruct((U_DEV, QROWS, HD), jnp.float32),
            jax.ShapeDtypeStruct((2 * U_DEV, 2 * HD), jnp.float32),
        ),
        in_specs=[vmem_spec(), smem_spec(), smem_spec(), vmem_spec(), vmem_spec()],
        out_specs=(vmem_spec(), vmem_spec()),
        name="own_rows",
    )(rows, places, requests, cosine, sine)
    return queries, fresh


def swap(values, key, devices):
    return lax.ppermute(values, "tp", [(i, i ^ key) for i in range(devices)])


def gather_swaps(values, devices, direct):
    values = values[None]
    step = devices // 2
    span = [0]
    if direct and devices >= 4:
        keys = [step, step // 2, step + step // 2]
        values = jnp.concatenate([values] + [swap(values, k, devices) for k in keys], axis=0)
        span = [0] + keys
        step //= 4
    while step:
        values = jnp.concatenate([values, swap(values, step, devices)], axis=0)
        span = span + [s ^ step for s in span]
        step //= 2
    return values, span


def after(value, *others):
    return lax.optimization_barrier((value,) + others)[0]


def body(hidden_states, qkv_weight, out_weight, cache_pages, context_lengths, new_units, old_pages):
    devices = lax.axis_size("tp")
    device = lax.axis_index("tp")
    requests = hidden_states.shape[0]
    pages_dev, page_rows, page_width = cache_pages.shape
    capacity = max(1, pages_dev // devices)
    total_units = new_units.shape[0]
    total_pages = old_pages.shape[0]
    pairwise = devices == 2 * KVH

    def own(*keys):
        return [(0, key, r) for key in keys for r in range(capacity)]

    def passed(source, piece):
        return [(source, 0, piece * capacity + r) for r in range(capacity)]

    def piece(chunk, n):
        return chunk[n * capacity : (n + 1) * capacity]

    def send(chunk, key):
        return swap(chunk, key, devices)

    if pairwise:
        half, quarter = devices // 2, devices // 4
        a, b = half, half + quarter
        c, d = a + 2, b + 2
        (chunk_a, cross_far), order = first_pack(
            new_units,
            old_pages,
            cache_pages,
            devices,
            capacity,
            [own(a), own(a + 1, b + 1, c + 1, d + 1)],
            True,
        )
        moved_a, cross_far = send(chunk_a, a), send(cross_far, 1)
        near = list(range(2, half, 2))
        chunk_b, cross_near = next_pack(
            order, [cache_pages], capacity, [own(b), own(1, *[k + 1 for k in near])]
        )
        moved_b, cross_near = send(chunk_b, b), send(cross_near, 1)
    else:
        (packed,), order = first_pack(
            new_units, old_pages, cache_pages, devices, capacity, [own(*range(devices))], False
        )
        arrived = lax.all_to_all(
            packed.reshape(devices, capacity, page_rows, page_width),
            "tp",
            split_axis=0,
            concat_axis=0,
            tiled=True,
        ).reshape(devices * capacity, page_rows, page_width)

    own_units = lax.dynamic_slice_in_dim(new_units, device * U_DEV, U_DEV)
    own_lengths = context_lengths[own_units // KVH]
    wanted = (
        own_units[:, None] * PER_UNIT + jnp.arange(PER_UNIT, dtype=jnp.int32)[None, :]
    ).reshape(pages_dev)
    source_pos = jnp.sum(
        jnp.where(
            wanted[:, None] == old_pages[None, :],
            jnp.arange(total_pages, dtype=jnp.int32)[None, :],
            0,
        ),
        axis=1,
    )
    source_dev = source_pos // pages_dev
    rank = jnp.sum(
        (
            (source_dev[:, None] == source_dev[None, :])
            & (source_pos[None, :] < source_pos[:, None])
        ).astype(jnp.int32),
        axis=1,
    )
    if pairwise:
        where = (source_dev ^ device) * capacity + rank
        spots = jnp.arange(devices * capacity, dtype=jnp.int32)
        slots = jnp.arange(pages_dev, dtype=jnp.int32)
        table = jnp.sum(jnp.where(where[None, :] == spots[:, None], slots[None, :], 0), axis=1)
    else:
        table = source_dev * capacity + rank

    flat_rows = hidden_states.reshape(requests * 2, D)
    if pairwise:
        flat_rows = after(flat_rows, cross_near)
    own_part = lax.dot_general(
        flat_rows, qkv_weight, (((1,), (1,)), ((), ())), preferred_element_type=jnp.float32
    ).astype(jnp.bfloat16)
    own_requests, own_heads = own_units // KVH, own_units % KVH
    positions = own_lengths[:, None] + jnp.arange(2, dtype=jnp.int32)[None, :]
    cosine, sine = rope_tables(positions.reshape(2 * U_DEV))
    if pairwise:
        rows, span = gather_swaps(own_part, devices, True)
        turn = jnp.array([span.index(i) for i in range(devices)], jnp.int32)
        pieces = devices // KVH
        holders = own_heads[:, None] * pieces + jnp.arange(pieces, dtype=jnp.int32)[None, :]
        places = turn[(holders ^ device).reshape(U_DEV * pieces)]
        queries, fresh = own_rows(rows, places, own_requests, cosine, sine)
        moved_a2 = send(after(piece(cross_far, 0), own_part), a + 0)
        moved_b2 = send(after(piece(cross_far, 1), own_part), b + 0)
        near_chunks = next_pack(
            order,
            [cache_pages, after(cross_near, own_part)],
            capacity,
            [own(k) + passed(1, n + 1) for n, k in enumerate(near)],
        )
        moved_near = [send(chunk, k) for chunk, k in zip(near_chunks, near)]
        chunk_c, chunk_d = next_pack(
            order,
            [cache_pages, after(cross_far, moved_a)],
            capacity,
            [own(c) + passed(1, 2), own(d)],
        )
        moved_c = send(after(chunk_c, moved_b), c)

        def place(groups, sums, cache, finish):
            entries, sources = [], []
            for array, keys, first in groups:
                for n, key in enumerate(keys):
                    for r in range(capacity):
                        at = (r,) if array is cache_pages else first + n * capacity + r
                        entries.append((len(sources), at, (key * capacity + r,)))
                sources.append(array)
            return place_pages(
                table, order, own_lengths, fresh, queries, sums, sources, entries, cache, finish
            )

        new_cache, sums, _ = place(
            [(cache_pages, [0], 0), (cross_near, [1], 0), (moved_a, [a], 0), (moved_b, [b], 0)],
            None,
            None,
            False,
        )
        moved_d = send(after(chunk_d, moved_a2, sums[0]), d)
        new_cache, sums, _ = place(
            [(moved_a2, [a + 1], 0), (moved_b2, [b + 1], 0), (moved_near[0], [2, 3], 0)],
            sums,
            new_cache,
            False,
        )
        moved_d2 = send(after(piece(cross_far, 3), moved_b2, sums[0]), d)
        new_cache, sums, _ = place(
            [(m, [k, k + 1], 0) for m, k in zip(moved_near[1:], near[1:])], sums, new_cache, False
        )
        new_cache, sums, _ = place(
            [(moved_c, [c, c + 1], 0), (moved_d, [d], 0)], sums, new_cache, False
        )
        new_cache, sums, attended = place([(moved_d2, [d + 1], 0)], sums, new_cache, True)
    else:
        rows = lax.all_gather(own_part, "tp", axis=1, tiled=True)
        rows = rows.reshape(requests, 2, KVH, GROUP + 2, HD)
        rows = rows[own_requests, :, own_heads].astype(jnp.float32)
        turned = rotate(
            rows[:, :, : GROUP + 1],
            cosine.reshape(U_DEV, 2, 1, HD),
            sine.reshape(U_DEV, 2, 1, HD),
        )
        queries = turned[:, :, :GROUP].reshape(U_DEV, QROWS, HD)
        fresh = jnp.concatenate([turned[:, :, GROUP], rows[:, :, GROUP + 1]], axis=-1)
        fresh = fresh.reshape(2 * U_DEV, 2 * HD).astype(jnp.bfloat16).astype(jnp.float32)
        queries = queries.astype(jnp.bfloat16).astype(jnp.float32)
        entries = [(0, (w,), w) for w in range(pages_dev)]
        new_cache, sums, attended = place_pages(
            table, table, own_lengths, fresh, queries, None, [arrived], entries, None, True
        )

    slot_index = jnp.sum(
        jnp.where(
            new_units[None, :] == jnp.arange(total_units, dtype=jnp.int32)[:, None],
            jnp.arange(total_units, dtype=jnp.int32)[None, :],
            0,
        ),
        axis=1,
    )
    attended = attended.reshape(U_DEV, 2, GROUP * HD)
    if pairwise:
        heads, span = gather_swaps(attended, devices, False)
        turn = jnp.array([span.index(i) for i in range(devices)], jnp.int32)
        holder = turn[(slot_index // U_DEV) ^ device]
        heads = heads.reshape(total_units, 2, GROUP * HD)[holder * U_DEV + slot_index % U_DEV]
    else:
        heads = lax.all_gather(attended, "tp", axis=0, tiled=True)[slot_index]
    logical = (
        heads.reshape(requests, KVH, 2, GROUP * HD)
        .transpose(0, 2, 1, 3)
        .reshape(requests * 2, HEADS * HD)
    )
    mixed_rows = lax.dot_general(
        logical, out_weight, (((1,), (1,)), ((), ())), preferred_element_type=jnp.float32
    )
    mixed_rows = mixed_rows.astype(jnp.bfloat16).reshape(requests, 2, out_weight.shape[0])
    return (mixed_rows, new_cache)


def solution(mesh):
    in_specs = (
        P("group", None, None),
        P("tp", None),
        P("tp", None),
        P(("group", "tp"), None, None),
        P("group"),
        P("group"),
        P("group"),
    )
    out_specs = (P("group", None, "tp"), P(("group", "tp"), None, None))
    return jax.shard_map(body, mesh=mesh, in_specs=in_specs, out_specs=out_specs, check_vma=False)
```

```python
import functools
import math

import jax
import jax.numpy as jnp
from jax import lax
from jax.experimental import pallas as pl
from jax.experimental.pallas import tpu as pltpu
from jax.sharding import PartitionSpec as P

D = 8192
HEADS = 64
KVH = 8
HD = 128
U_DEV = 4
MAXCTX = 2048
PAGE = 128
GROUP = HEADS // KVH
QROWS = 2 * GROUP
PER_UNIT = MAXCTX // PAGE
VMEM_LIMIT = 56 * 1024 * 1024

rope_base = 10000.0


def rope_tables(positions):
    half_dim = HD // 2
    frequency = rope_base ** (-(jnp.arange(half_dim, dtype=jnp.float32) * 2.0 / HD))
    angles = positions.astype(jnp.float32)[..., None] * frequency
    cosine = jnp.concatenate([jnp.cos(angles), jnp.cos(angles)], axis=-1)
    sine = jnp.concatenate([-jnp.sin(angles), jnp.sin(angles)], axis=-1)
    return cosine, sine


def rotate(values, cosine, sine):
    half_dim = HD // 2
    turned = jnp.concatenate([values[..., half_dim:], values[..., :half_dim]], axis=-1)
    return values * cosine + turned * sine


def any_spec():
    return pl.BlockSpec(memory_space=pl.ANY)


def smem_spec():
    return pl.BlockSpec(memory_space=pltpu.SMEM)


def vmem_spec():
    return pl.BlockSpec(memory_space=pltpu.VMEM)


def load_order(devices, capacity, relative, units_ref, old_ref, order_ref, slots, count):
    device = lax.axis_index("tp")
    total_units = units_ref.shape[0]
    pages_dev = old_ref.shape[0] // devices

    def clear(t, carry):
        count[t] = 0
        return carry

    def empty(t, carry):
        order_ref[t] = 0
        return carry

    def invert(q, carry):
        slots[units_ref[q]] = q
        return carry

    def assign(i, carry):
        unit = old_ref[device * pages_dev + i] // PER_UNIT
        target = slots[unit] // U_DEV
        if relative:
            target = target ^ device
        rank = count[target]
        count[target] = rank + 1
        order_ref[target * capacity + rank] = i
        return carry

    lax.fori_loop(0, devices, clear, 0, unroll=8)
    if devices * capacity > pages_dev:
        lax.fori_loop(0, devices * capacity, empty, 0, unroll=8)
    lax.fori_loop(0, total_units, invert, 0, unroll=8)
    lax.fori_loop(0, pages_dev, assign, 0, unroll=8)


def move_pages(outs_pages, capacity, order_ref, sources, outs, stage, load_sem, store_sem):
    loads, stores = [], []
    for source, key, r in sum(outs_pages, []):
        slot = len(loads)
        index = order_ref[key * capacity + r] if source == 0 else r
        copy = pltpu.make_async_copy(
            sources[source].at[index], stage.at[slot], load_sem.at[slot]
        )
        copy.start()
        loads.append(copy)
    slot = 0
    for n, pages in enumerate(outs_pages):
        count = len(pages)
        for copy in loads[slot : slot + count]:
            copy.wait()
        copy = pltpu.make_async_copy(stage.at[pl.ds(slot, count)], outs[n], store_sem.at[n])
        copy.start()
        stores.append(copy)
        slot += count
    for copy in stores:
        copy.wait()


def first_pack_kernel(
    devices, capacity, outs_pages, relative, units_ref, old_ref, pages_ref, *rest
):
    outs = rest[:-6]
    order_ref, slots, count, stage, load_sem, store_sem = rest[-6:]
    load_order(devices, capacity, relative, units_ref, old_ref, order_ref, slots, count)
    move_pages(
        outs_pages, capacity, order_ref, [pages_ref], outs, stage, load_sem, store_sem
    )


def next_pack_kernel(capacity, outs_pages, sources, order_ref, *rest):
    source_refs, outs = rest[:sources], rest[sources:-3]
    stage, load_sem, store_sem = rest[-3:]
    move_pages(
        outs_pages, capacity, order_ref, source_refs, outs, stage, load_sem, store_sem
    )


def pack_shapes(outs_pages, pages):
    total = sum(len(p) for p in outs_pages)
    shapes = [jax.ShapeDtypeStruct((len(p),) + pages.shape[1:], pages.dtype) for p in outs_pages]
    scratch = [
        pltpu.VMEM((total,) + pages.shape[1:], pages.dtype),
        pltpu.SemaphoreType.DMA((total,)),
        pltpu.SemaphoreType.DMA((len(outs_pages),)),
    ]
    return shapes, scratch


def first_pack(new_units, old_pages, pages, devices, capacity, outs_pages, relative):
    outs, scratch = pack_shapes(outs_pages, pages)
    result = pl.pallas_call(
        functools.partial(first_pack_kernel, devices, capacity, outs_pages, relative),
        out_shape=tuple(outs) + (jax.ShapeDtypeStruct((devices * capacity,), jnp.int32),),
        in_specs=[smem_spec(), smem_spec(), any_spec()],
        out_specs=tuple(any_spec() for _ in outs) + (smem_spec(),),
        scratch_shapes=[
            pltpu.SMEM(new_units.shape, jnp.int32),
            pltpu.SMEM((devices,), jnp.int32),
        ]
        + scratch,
        compiler_params=pltpu.CompilerParams(vmem_limit_bytes=VMEM_LIMIT),
        name="first_pack",
    )(new_units, old_pages, pages)
    return result[:-1], result[-1]


def next_pack(order, sources, capacity, outs_pages):
    outs, scratch = pack_shapes(outs_pages, sources[0])
    return pl.pallas_call(
        functools.partial(next_pack_kernel, capacity, outs_pages, len(sources)),
        out_shape=tuple(outs),
        in_specs=[smem_spec()] + [any_spec()] * len(sources),
        out_specs=tuple(any_spec() for _ in outs),
        scratch_shapes=scratch,
        compiler_params=pltpu.CompilerParams(vmem_limit_bytes=VMEM_LIMIT),
        name="next_pack",
    )(order, *sources)


def attend(query, keys, values, limit):
    scale = 1.0 / math.sqrt(HD)
    scores = (
        lax.dot_general(query, keys, (((1,), (1,)), ((), ())), preferred_element_type=jnp.float32)
        * scale
    )
    lane = lax.broadcasted_iota(jnp.int32, scores.shape, 1)
    weights = jnp.where(lane < limit, jnp.exp(scores), 0.0)
    total = jnp.sum(weights, axis=1, keepdims=True)
    weighted = jnp.dot(weights.astype(jnp.bfloat16), values, preferred_element_type=jnp.float32)
    return weighted, total


ALIGN = 16


def place_kernel(entries, started, attends, finish, late, *refs):
    refs = list(refs)
    table_ref, order_ref, length_ref, fresh_ref = refs[:4]
    refs = refs[4:]
    if attends:
        queries_ref = refs.pop(0)
        if started:
            weighted_in, total_in = refs.pop(0), refs.pop(0)
        part_ref = refs.pop(0) if late else None
    sources = 1 + max(source for source, _, _ in entries)
    source_refs, refs = refs[:sources], refs[sources:]
    if started:
        refs.pop(0)
    out_ref = refs.pop(0)
    if attends:
        weighted_ref, total_ref = refs.pop(0), refs.pop(0)
    attended_ref = refs.pop(0) if finish else None
    stage, load_sem, store_sem = refs
    if attends and started:
        weighted_ref[...] = weighted_in[...]
        total_ref[...] = total_in[...]
    loads = []
    for n, (source, index, _) in enumerate(entries):
        index = order_ref[index[0]] if isinstance(index, tuple) else index
        copy = pltpu.make_async_copy(
            source_refs[source].at[index], stage.at[n], load_sem.at[n]
        )
        copy.start()
        loads.append(copy)
    row = lax.broadcasted_iota(jnp.int32, (ALIGN, 2 * HD), 0)
    stores = []
    for n, (_, _, key) in enumerate(entries):
        w = table_ref[key[0]] if isinstance(key, tuple) else key
        unit, part = w // PER_UNIT, w % PER_UNIT
        length = length_ref[unit]
        loads[n].wait()
        for j in range(2):
            position = length + j

            @pl.when(position // PAGE == part)
            def _():
                inside = position % PAGE
                rows = pl.ds(pl.multiple_of(inside // ALIGN * ALIGN, ALIGN), ALIGN)
                block = stage[n, rows, :].astype(jnp.float32)
                token = fresh_ref[pl.ds(2 * unit + j, 1), :]
                block = jnp.where(row == inside % ALIGN, token, block)
                stage[n, rows, :] = block.astype(jnp.bfloat16)

        copy = pltpu.make_async_copy(stage.at[n], out_ref.at[w], store_sem.at[n])
        copy.start()
        stores.append(copy)
    if attends and not started:
        own_terms(queries_ref, fresh_ref, weighted_ref, total_ref)
    lane = lax.broadcasted_iota(jnp.int32, (QROWS, HD), 1)
    if late:
        sums = part_ref[len(late) * QROWS :, :].astype(jnp.float32)
    for n, at in enumerate(late):
        unit = table_ref[at] // PER_UNIT
        mine = (lane == 2 * n) | (lane == 2 * n + 1)
        total = jnp.sum(jnp.where(mine, sums, 0.0), axis=1, keepdims=True)
        weighted_ref[unit] += part_ref[n * QROWS : (n + 1) * QROWS, :].astype(jnp.float32)
        total_ref[unit] += jnp.broadcast_to(total, (QROWS, HD))
    group = 4
    for first in range(0, len(entries) if attends else 0, group):
        found = []
        for n in range(first, min(first + group, len(entries))):
            key = entries[n][2]
            w = table_ref[key[0]] if isinstance(key, tuple) else key
            unit, part = w // PER_UNIT, w % PER_UNIT
            weighted, total = attend(
                queries_ref[unit].astype(jnp.bfloat16),
                stage[n, :, :HD],
                stage[n, :, HD:],
                length_ref[unit] - part * PAGE,
            )
            found.append((unit, weighted, total))
        for unit, weighted, total in found:
            weighted_ref[unit] += weighted
            total_ref[unit] += jnp.broadcast_to(total, (QROWS, HD))
    if finish:
        attended_ref[...] = (weighted_ref[...] / total_ref[...]).astype(jnp.bfloat16)
    for copy in stores:
        copy.wait()


def own_terms(queries_ref, fresh_ref, weighted_ref, total_ref):
    scale = 1.0 / math.sqrt(HD)
    row = lax.broadcasted_iota(jnp.int32, (QROWS, 1), 0)
    for unit in range(U_DEV):
        query = queries_ref[unit]
        weighted = jnp.zeros((QROWS, HD), jnp.float32)
        total = jnp.zeros((QROWS, 1), jnp.float32)
        for j in range(2):
            at = 2 * unit + j
            key = fresh_ref[at : at + 1, :HD]
            value = fresh_ref[at : at + 1, HD:]
            score = jnp.sum(query * key, axis=1, keepdims=True) * scale
            weight = jnp.where(row >= j * GROUP, jnp.exp(score), 0.0)
            total = total + weight
            weighted = weighted + weight.astype(jnp.bfloat16).astype(jnp.float32) * value
        weighted_ref[unit] = weighted
        total_ref[unit] = jnp.broadcast_to(total, (QROWS, HD))


def place_pages(
    table, order, lengths, fresh, queries, sums, parts, late, sources, entries, cache, finish
):
    started, attends = cache is not None, queries is not None
    page_shape = sources[0].shape[1:]
    pages_dev = U_DEV * PER_UNIT
    args = [table, order, lengths, fresh]
    specs = [smem_spec()] * 3 + [vmem_spec()]
    if attends:
        vmem_args = [queries] + (list(sums) if started else []) + list(parts)
        args += vmem_args
        specs += [vmem_spec()] * len(vmem_args)
    args += list(sources)
    specs += [any_spec()] * len(sources)
    aliases = {}
    if started:
        aliases = {len(args): 0}
        args.append(cache)
        specs.append(any_spec())
    outs = [jax.ShapeDtypeStruct((pages_dev,) + page_shape, jnp.bfloat16)]
    out_specs = [any_spec()]
    if attends:
        outs += [jax.ShapeDtypeStruct((U_DEV, QROWS, HD), jnp.float32)] * 2
        out_specs += [vmem_spec()] * 2
    if finish:
        outs.append(jax.ShapeDtypeStruct((U_DEV, QROWS, HD), jnp.bfloat16))
        out_specs.append(vmem_spec())
    count = len(entries)
    result = pl.pallas_call(
        functools.partial(place_kernel, entries, started, attends, finish, late),
        out_shape=tuple(outs),
        in_specs=specs,
        out_specs=tuple(out_specs),
        input_output_aliases=aliases,
        scratch_shapes=[
            pltpu.VMEM((count,) + page_shape, jnp.bfloat16),
            pltpu.SemaphoreType.DMA((count,)),
            pltpu.SemaphoreType.DMA((count,)),
        ],
        compiler_params=pltpu.CompilerParams(vmem_limit_bytes=VMEM_LIMIT),
        name="place_pages",
    )(*args)
    return result[0], result[1:3], result[3] if finish else None


def rows_kernel(
    late,
    units_ref,
    turn_ref,
    order_ref,
    ids_ref,
    lengths_ref,
    rows_ref,
    cosine_ref,
    sine_ref,
    pages_ref,
    passed_ref,
    queries_ref,
    fresh_ref,
    part_ref,
    stage,
    load_sem,
):
    device = lax.axis_index("tp")
    devices, _, width = rows_ref.shape
    pieces = (GROUP + 2) * HD // width
    half_dim = HD // 2
    row = lax.broadcasted_iota(jnp.int32, rows_ref.shape[1:], 0)
    lane = lax.broadcasted_iota(jnp.int32, (QROWS, HD), 1)

    def unit_rows(unit):
        request, head = unit // KVH, unit % KVH
        found = []
        for piece in range(pieces):
            place = turn_ref[(head * pieces + piece) ^ device]
            block = rows_ref[place].astype(jnp.float32)
            picked = [
                jnp.sum(jnp.where(row == 2 * request + j, block, 0.0), axis=0, keepdims=True)
                for j in range(2)
            ]
            for at in range(0, width, HD):
                found.append([line[:, at : at + HD] for line in picked])
        turned = []
        for j in range(2):
            heads = jnp.concatenate([head[j] for head in found[: GROUP + 1]], axis=0)
            swapped = jnp.concatenate([heads[:, half_dim:], heads[:, :half_dim]], axis=1)
            cosine = cosine_ref[pl.ds(2 * request + j, 1), :]
            sine = sine_ref[pl.ds(2 * request + j, 1), :]
            heads = heads * cosine + swapped * sine
            turned.append(heads.astype(jnp.bfloat16).astype(jnp.float32))
        return turned, [found[GROUP + 1][j] for j in range(2)]

    loads = []
    for slot, (source, at) in enumerate(late):
        page = pages_ref.at[order_ref[at]] if source == 0 else passed_ref.at[at]
        copy = pltpu.make_async_copy(page, stage.at[slot], load_sem.at[slot])
        copy.start()
        loads.append(copy)
    sums = jnp.zeros((QROWS, HD), jnp.float32)
    for slot in range(len(late)):
        page = ids_ref[slot]
        unit = page // PER_UNIT
        limit = lengths_ref[unit // KVH] - (page % PER_UNIT) * PAGE
        turned, _ = unit_rows(unit)
        query = jnp.concatenate([turned[0][:GROUP], turned[1][:GROUP]], axis=0)
        loads[slot].wait()
        weighted, total = attend(
            query.astype(jnp.bfloat16), stage[slot, :, :HD], stage[slot, :, HD:], limit
        )
        part_ref[slot * QROWS : (slot + 1) * QROWS, :] = weighted.astype(jnp.bfloat16)
        high = total.astype(jnp.bfloat16).astype(jnp.float32)
        sums = jnp.where(lane == 2 * slot, high, sums)
        sums = jnp.where(lane == 2 * slot + 1, total - high, sums)
    part_ref[len(late) * QROWS :, :] = sums.astype(jnp.bfloat16)
    for slot in range(U_DEV):
        turned, values = unit_rows(units_ref[slot])
        for j in range(2):
            at = 2 * slot + j
            queries_ref[slot, j * GROUP : (j + 1) * GROUP, :] = turned[j][:GROUP]
            fresh_ref[at : at + 1, :HD] = turned[j][GROUP:]
            fresh_ref[at : at + 1, HD:] = values[j]


def rows_and_parts(units, turn, order, ids, lengths, rows, cosine, sine, pages, passed, late):
    return pl.pallas_call(
        functools.partial(rows_kernel, late),
        out_shape=(
            jax.ShapeDtypeStruct((U_DEV, QROWS, HD), jnp.float32),
            jax.ShapeDtypeStruct((2 * U_DEV, 2 * HD), jnp.float32),
            jax.ShapeDtypeStruct(((len(late) + 1) * QROWS, HD), jnp.bfloat16),
        ),
        in_specs=[smem_spec()] * 5 + [vmem_spec()] * 3 + [any_spec()] * 2,
        out_specs=(vmem_spec(),) * 3,
        scratch_shapes=[
            pltpu.VMEM((len(late),) + pages.shape[1:], pages.dtype),
            pltpu.SemaphoreType.DMA((len(late),)),
        ],
        compiler_params=pltpu.CompilerParams(vmem_limit_bytes=VMEM_LIMIT),
        name="rows_and_parts",
    )(units, turn, order, ids, lengths, rows, cosine, sine, pages, passed)


def swap(values, key, devices):
    return lax.ppermute(values, "tp", [(i, i ^ key) for i in range(devices)])


def gather_line(values, devices):
    values = values[None]
    step = devices // 2
    keys = [step // 2, step, step + step // 2]
    found = [swap(values, k, devices) for k in keys]
    return jnp.concatenate([values] + found, axis=0), [0] + keys


def gather_more(values, span, step, devices):
    values = jnp.concatenate([values, swap(values, step, devices)], axis=0)
    return values, span + [s ^ step for s in span]


def after(value, *others):
    return lax.optimization_barrier((value,) + others)[0]


def body(hidden_states, qkv_weight, out_weight, cache_pages, context_lengths, new_units, old_pages):
    devices = lax.axis_size("tp")
    device = lax.axis_index("tp")
    requests = hidden_states.shape[0]
    pages_dev, page_rows, page_width = cache_pages.shape
    capacity = max(1, pages_dev // devices)
    total_units = new_units.shape[0]
    total_pages = old_pages.shape[0]
    pairwise = devices == 2 * KVH

    def own(*keys):
        return [(0, key, r) for key in keys for r in range(capacity)]

    def passed(source, piece):
        return [(source, 0, piece * capacity + r) for r in range(capacity)]

    def piece(chunk, n):
        return chunk[n * capacity : (n + 1) * capacity]

    def send(chunk, key):
        return swap(chunk, key, devices)

    if pairwise:
        half, quarter = devices // 2, devices // 4
        a, b = half, half + quarter
        c, d = a + 2, b + 2
        (chunk_a, cross_far), order = first_pack(
            new_units,
            old_pages,
            cache_pages,
            devices,
            capacity,
            [own(a), own(a + 1, b + 1, c + 1, d + 1)],
            True,
        )
        moved_a, cross_far = send(chunk_a, a), send(cross_far, 1)
        near = list(range(2, half, 2))
        chunk_b, cross_near = next_pack(
            order, [cache_pages], capacity, [own(b), own(1, *[k + 1 for k in near])]
        )
        moved_b, cross_near = send(chunk_b, b), send(cross_near, 1)
    else:
        (packed,), order = first_pack(
            new_units, old_pages, cache_pages, devices, capacity, [own(*range(devices))], False
        )
        arrived = lax.all_to_all(
            packed.reshape(devices, capacity, page_rows, page_width),
            "tp",
            split_axis=0,
            concat_axis=0,
            tiled=True,
        ).reshape(devices * capacity, page_rows, page_width)

    own_units = lax.dynamic_slice_in_dim(new_units, device * U_DEV, U_DEV)
    own_lengths = context_lengths[own_units // KVH]
    wanted = (
        own_units[:, None] * PER_UNIT + jnp.arange(PER_UNIT, dtype=jnp.int32)[None, :]
    ).reshape(pages_dev)
    source_pos = jnp.sum(
        jnp.where(
            wanted[:, None] == old_pages[None, :],
            jnp.arange(total_pages, dtype=jnp.int32)[None, :],
            0,
        ),
        axis=1,
    )
    source_dev = source_pos // pages_dev
    rank = jnp.sum(
        (
            (source_dev[:, None] == source_dev[None, :])
            & (source_pos[None, :] < source_pos[:, None])
        ).astype(jnp.int32),
        axis=1,
    )
    if pairwise:
        where = (source_dev ^ device) * capacity + rank
        spots = jnp.arange(devices * capacity, dtype=jnp.int32)
        slots = jnp.arange(pages_dev, dtype=jnp.int32)
        table = jnp.sum(jnp.where(where[None, :] == spots[:, None], slots[None, :], 0), axis=1)
    else:
        table = source_dev * capacity + rank

    slot_index = jnp.sum(
        jnp.where(
            new_units[None, :] == jnp.arange(total_units, dtype=jnp.int32)[:, None],
            jnp.arange(total_units, dtype=jnp.int32)[None, :],
            0,
        ),
        axis=1,
    )
    if pairwise:
        ids = old_pages.reshape(devices, 1, pages_dev)
        ids = jnp.concatenate([ids[device], ids[device ^ 1]], axis=0)
        reached = jnp.sum(
            jnp.where(
                (ids // PER_UNIT)[..., None] == new_units, jnp.arange(total_units) // U_DEV, 0
            ),
            axis=-1,
        )
        chosen = reached == (device ^ d)
        earlier = jnp.arange(pages_dev)[None, :] < jnp.arange(pages_dev)[:, None]
        ranks = jnp.sum((chosen[:, None, :] & earlier[None]).astype(jnp.int32), axis=-1)
        wants = jnp.arange(capacity, dtype=jnp.int32)[None, :, None]
        picked = chosen[:, None, :] & (ranks[:, None, :] == wants)
        late_ids = jnp.sum(jnp.where(picked, ids[:, None, :], 0), axis=-1)
        late_ids = late_ids.reshape(2 * capacity).astype(jnp.int32)
    flat_rows = hidden_states.reshape(requests * 2, D)
    if pairwise:
        flat_rows = after(flat_rows, cross_near, cross_far)
    own_part = lax.dot_general(
        flat_rows, qkv_weight, (((1,), (1,)), ((), ())), preferred_element_type=jnp.float32
    ).astype(jnp.bfloat16)
    if pairwise:
        positions = context_lengths[:, None] + jnp.arange(2, dtype=jnp.int32)[None, :]
        cosine, sine = rope_tables(positions.reshape(2 * requests))
        rows, span = gather_line(own_part, devices)
        moved_a2 = send(after(piece(cross_far, 0), own_part, moved_a), a)
        moved_b2 = send(after(piece(cross_far, 1), own_part), b)
        near_chunks = next_pack(
            order,
            [cache_pages, after(cross_near, rows)],
            capacity,
            [own(k) + passed(1, n + 1) for n, k in enumerate(near)],
        )
        rows, span = gather_more(after(rows, moved_a, moved_b), span, 2, devices)
        rows, span = gather_more(rows, span, 1, devices)
        moved_near = [
            send(after(near_chunks[0], rows), near[0]),
            send(near_chunks[1], near[1]),
            send(after(near_chunks[2], rows), near[2]),
        ]
        turn = jnp.array([span.index(i) for i in range(devices)], jnp.int32)
        late = [(0, d * capacity + r) for r in range(capacity)]
        late += [(1, 3 * capacity + r) for r in range(capacity)]
        places = [key * capacity + r for key in (d, d + 1) for r in range(capacity)]
        queries, fresh, sent = rows_and_parts(
            own_units,
            turn,
            order,
            late_ids,
            context_lengths,
            rows,
            cosine,
            sine,
            cache_pages,
            cross_far,
            late,
        )
        parts = [send(sent, d)]
        chunk_c, chunk_d = next_pack(
            order,
            [cache_pages, after(cross_far, rows)],
            capacity,
            [own(c) + passed(1, 2), own(d)],
        )
        moved_c = send(after(chunk_c, moved_a2, parts[0]), c)

        def place(groups, sums, cache, attends, parts, finish):
            entries, sources = [], []
            for array, keys, first in groups:
                for n, key in enumerate(keys):
                    for r in range(capacity):
                        at = (r,) if array is cache_pages else first + n * capacity + r
                        entries.append((len(sources), at, (key * capacity + r,)))
                sources.append(array)
            return place_pages(
                table,
                order,
                own_lengths,
                fresh,
                queries if attends else None,
                sums,
                parts,
                places if parts else [],
                sources,
                entries,
                cache,
                finish,
            )

        new_cache, sums, _ = place(
            [(cache_pages, [0], 0), (cross_near, [1], 0), (moved_a, [a], 0), (moved_b, [b], 0)],
            None,
            None,
            True,
            [],
            False,
        )
        moved_d = send(after(chunk_d, moved_b2, sums[0]), d)
        new_cache, sums, _ = place(
            [(moved_a2, [a + 1], 0), (moved_b2, [b + 1], 0), (moved_near[0], [2, 3], 0)],
            sums,
            new_cache,
            True,
            [],
            False,
        )
        new_cache, sums, _ = place(
            [(m, [k, k + 1], 0) for m, k in zip(moved_near[1:], near[1:])],
            sums,
            new_cache,
            True,
            [],
            False,
        )
        new_cache, sums, attended = place(
            [(moved_c, [c, c + 1], 0)], sums, new_cache, True, parts, True
        )
        attended = after(attended, moved_d)
        moved_d2 = send(after(piece(cross_far, 3), attended), d)
        new_cache, _, _ = place(
            [(moved_d, [d], 0), (moved_d2, [d + 1], 0)], None, new_cache, False, [], False
        )
    else:
        own_requests, own_heads = own_units // KVH, own_units % KVH
        positions = own_lengths[:, None] + jnp.arange(2, dtype=jnp.int32)[None, :]
        cosine, sine = rope_tables(positions.reshape(2 * U_DEV))
        rows = lax.all_gather(own_part, "tp", axis=1, tiled=True)
        rows = rows.reshape(requests, 2, KVH, GROUP + 2, HD)
        rows = rows[own_requests, :, own_heads].astype(jnp.float32)
        turned = rotate(
            rows[:, :, : GROUP + 1],
            cosine.reshape(U_DEV, 2, 1, HD),
            sine.reshape(U_DEV, 2, 1, HD),
        )
        queries = turned[:, :, :GROUP].reshape(U_DEV, QROWS, HD)
        fresh = jnp.concatenate([turned[:, :, GROUP], rows[:, :, GROUP + 1]], axis=-1)
        fresh = fresh.reshape(2 * U_DEV, 2 * HD).astype(jnp.bfloat16).astype(jnp.float32)
        queries = queries.astype(jnp.bfloat16).astype(jnp.float32)
        entries = [(0, (w,), w) for w in range(pages_dev)]
        new_cache, sums, attended = place_pages(
            table,
            table,
            own_lengths,
            fresh,
            queries,
            None,
            [],
            [],
            [arrived],
            entries,
            None,
            True,
        )

    attended = attended.reshape(U_DEV, 2, GROUP * HD)
    if pairwise:
        heads, span = gather_line(attended, devices)
        heads, span = gather_more(heads, span, 2, devices)
        heads, span = gather_more(heads, span, 1, devices)
        holder = turn[(slot_index // U_DEV) ^ device]
        heads = heads.reshape(total_units, 2, GROUP * HD)[holder * U_DEV + slot_index % U_DEV]
    else:
        heads = lax.all_gather(attended, "tp", axis=0, tiled=True)[slot_index]
    logical = (
        heads.reshape(requests, KVH, 2, GROUP * HD)
        .transpose(0, 2, 1, 3)
        .reshape(requests * 2, HEADS * HD)
    )
    mixed_rows = lax.dot_general(
        logical, out_weight, (((1,), (1,)), ((), ())), preferred_element_type=jnp.float32
    )
    mixed_rows = mixed_rows.astype(jnp.bfloat16).reshape(requests, 2, out_weight.shape[0])
    return (mixed_rows, new_cache)


def solution(mesh):
    in_specs = (
        P("group", None, None),
        P("tp", None),
        P("tp", None),
        P(("group", "tp"), None, None),
        P("group"),
        P("group"),
        P("group"),
    )
    out_specs = (P("group", None, "tp"), P(("group", "tp"), None, None))
    return jax.shard_map(body, mesh=mesh, in_specs=in_specs, out_specs=out_specs, check_vma=False)
```

```python
import functools
import math

import jax
import jax.numpy as jnp
from jax import lax
from jax.experimental import pallas as pl
from jax.experimental.pallas import tpu as pltpu
from jax.sharding import PartitionSpec as P

D = 8192
HEADS = 64
KVH = 8
HD = 128
U_DEV = 4
MAXCTX = 2048
PAGE = 128
GROUP = HEADS // KVH
QROWS = 2 * GROUP
PER_UNIT = MAXCTX // PAGE
VMEM_LIMIT = 56 * 1024 * 1024

rope_base = 10000.0


def rope_tables(positions):
    half_dim = HD // 2
    frequency = rope_base ** (-(jnp.arange(half_dim, dtype=jnp.float32) * 2.0 / HD))
    angles = positions.astype(jnp.float32)[..., None] * frequency
    cosine = jnp.concatenate([jnp.cos(angles), jnp.cos(angles)], axis=-1)
    sine = jnp.concatenate([-jnp.sin(angles), jnp.sin(angles)], axis=-1)
    return cosine, sine


def rotate(values, cosine, sine):
    half_dim = HD // 2
    turned = jnp.concatenate([values[..., half_dim:], values[..., :half_dim]], axis=-1)
    return values * cosine + turned * sine


def any_spec():
    return pl.BlockSpec(memory_space=pl.ANY)


def smem_spec():
    return pl.BlockSpec(memory_space=pltpu.SMEM)


def vmem_spec():
    return pl.BlockSpec(memory_space=pltpu.VMEM)


def load_order(devices, capacity, relative, units_ref, old_ref, order_ref, slots, count):
    device = lax.axis_index("tp")
    total_units = units_ref.shape[0]
    pages_dev = old_ref.shape[0] // devices

    def clear(t, carry):
        count[t] = 0
        return carry

    def empty(t, carry):
        order_ref[t] = 0
        return carry

    def invert(q, carry):
        slots[units_ref[q]] = q
        return carry

    def assign(i, carry):
        unit = old_ref[device * pages_dev + i] // PER_UNIT
        target = slots[unit] // U_DEV
        if relative:
            target = target ^ device
        rank = count[target]
        count[target] = rank + 1
        order_ref[target * capacity + rank] = i
        return carry

    lax.fori_loop(0, devices, clear, 0, unroll=8)
    if devices * capacity > pages_dev:
        lax.fori_loop(0, devices * capacity, empty, 0, unroll=8)
    lax.fori_loop(0, total_units, invert, 0, unroll=8)
    lax.fori_loop(0, pages_dev, assign, 0, unroll=8)


def move_pages(outs_pages, capacity, order_ref, sources, outs, stage, load_sem, store_sem):
    loads, stores = [], []
    for source, key, r in sum(outs_pages, []):
        slot = len(loads)
        index = order_ref[key * capacity + r] if source == 0 else r
        copy = pltpu.make_async_copy(
            sources[source].at[index], stage.at[slot], load_sem.at[slot]
        )
        copy.start()
        loads.append(copy)
    slot = 0
    for n, pages in enumerate(outs_pages):
        count = len(pages)
        for copy in loads[slot : slot + count]:
            copy.wait()
        copy = pltpu.make_async_copy(stage.at[pl.ds(slot, count)], outs[n], store_sem.at[n])
        copy.start()
        stores.append(copy)
        slot += count
    for copy in stores:
        copy.wait()


def first_pack_kernel(
    devices, capacity, outs_pages, relative, units_ref, old_ref, pages_ref, *rest
):
    outs = rest[:-6]
    order_ref, slots, count, stage, load_sem, store_sem = rest[-6:]
    load_order(devices, capacity, relative, units_ref, old_ref, order_ref, slots, count)
    move_pages(
        outs_pages, capacity, order_ref, [pages_ref], outs, stage, load_sem, store_sem
    )


def next_pack_kernel(capacity, outs_pages, sources, order_ref, *rest):
    source_refs, outs = rest[:sources], rest[sources:-3]
    stage, load_sem, store_sem = rest[-3:]
    move_pages(
        outs_pages, capacity, order_ref, source_refs, outs, stage, load_sem, store_sem
    )


def pack_shapes(outs_pages, pages):
    total = sum(len(p) for p in outs_pages)
    shapes = [jax.ShapeDtypeStruct((len(p),) + pages.shape[1:], pages.dtype) for p in outs_pages]
    scratch = [
        pltpu.VMEM((total,) + pages.shape[1:], pages.dtype),
        pltpu.SemaphoreType.DMA((total,)),
        pltpu.SemaphoreType.DMA((len(outs_pages),)),
    ]
    return shapes, scratch


def first_pack(new_units, old_pages, pages, devices, capacity, outs_pages, relative):
    outs, scratch = pack_shapes(outs_pages, pages)
    result = pl.pallas_call(
        functools.partial(first_pack_kernel, devices, capacity, outs_pages, relative),
        out_shape=tuple(outs) + (jax.ShapeDtypeStruct((devices * capacity,), jnp.int32),),
        in_specs=[smem_spec(), smem_spec(), any_spec()],
        out_specs=tuple(any_spec() for _ in outs) + (smem_spec(),),
        scratch_shapes=[
            pltpu.SMEM(new_units.shape, jnp.int32),
            pltpu.SMEM((devices,), jnp.int32),
        ]
        + scratch,
        compiler_params=pltpu.CompilerParams(vmem_limit_bytes=VMEM_LIMIT),
        name="first_pack",
    )(new_units, old_pages, pages)
    return result[:-1], result[-1]


def next_pack(order, sources, capacity, outs_pages):
    outs, scratch = pack_shapes(outs_pages, sources[0])
    return pl.pallas_call(
        functools.partial(next_pack_kernel, capacity, outs_pages, len(sources)),
        out_shape=tuple(outs),
        in_specs=[smem_spec()] + [any_spec()] * len(sources),
        out_specs=tuple(any_spec() for _ in outs),
        scratch_shapes=scratch,
        compiler_params=pltpu.CompilerParams(vmem_limit_bytes=VMEM_LIMIT),
        name="next_pack",
    )(order, *sources)


def attend(query, keys, values, limit):
    scale = 1.0 / math.sqrt(HD)
    scores = (
        lax.dot_general(query, keys, (((1,), (1,)), ((), ())), preferred_element_type=jnp.float32)
        * scale
    )
    lane = lax.broadcasted_iota(jnp.int32, scores.shape, 1)
    weights = jnp.where(lane < limit, jnp.exp(scores), 0.0)
    total = jnp.sum(weights, axis=1, keepdims=True)
    weighted = jnp.dot(weights.astype(jnp.bfloat16), values, preferred_element_type=jnp.float32)
    return weighted, total


ALIGN = 16


def place_kernel(entries, started, attends, finish, late, *refs):
    refs = list(refs)
    table_ref, order_ref, length_ref, fresh_ref = refs[:4]
    refs = refs[4:]
    if attends:
        queries_ref = refs.pop(0)
        if started:
            weighted_in, total_in = refs.pop(0), refs.pop(0)
        part_ref = refs.pop(0) if late else None
    sources = 1 + max(source for source, _, _ in entries)
    source_refs, refs = refs[:sources], refs[sources:]
    if started:
        refs.pop(0)
    out_ref = refs.pop(0)
    if attends:
        weighted_ref, total_ref = refs.pop(0), refs.pop(0)
    attended_ref = refs.pop(0) if finish else None
    stage, load_sem, store_sem = refs
    if attends and started:
        weighted_ref[...] = weighted_in[...]
        total_ref[...] = total_in[...]
    loads = []
    for n, (source, index, _) in enumerate(entries):
        index = order_ref[index[0]] if isinstance(index, tuple) else index
        copy = pltpu.make_async_copy(
            source_refs[source].at[index], stage.at[n], load_sem.at[n]
        )
        copy.start()
        loads.append(copy)
    row = lax.broadcasted_iota(jnp.int32, (ALIGN, 2 * HD), 0)
    stores = []
    for n, (_, _, key) in enumerate(entries):
        w = table_ref[key[0]] if isinstance(key, tuple) else key
        unit, part = w // PER_UNIT, w % PER_UNIT
        length = length_ref[unit]
        loads[n].wait()
        for j in range(2):
            position = length + j

            @pl.when(position // PAGE == part)
            def _():
                inside = position % PAGE
                rows = pl.ds(pl.multiple_of(inside // ALIGN * ALIGN, ALIGN), ALIGN)
                block = stage[n, rows, :].astype(jnp.float32)
                token = fresh_ref[pl.ds(2 * unit + j, 1), :]
                block = jnp.where(row == inside % ALIGN, token, block)
                stage[n, rows, :] = block.astype(jnp.bfloat16)

        copy = pltpu.make_async_copy(stage.at[n], out_ref.at[w], store_sem.at[n])
        copy.start()
        stores.append(copy)
    if attends and not started:
        own_terms(queries_ref, fresh_ref, weighted_ref, total_ref)
    lane = lax.broadcasted_iota(jnp.int32, (QROWS, HD), 1)
    if late:
        sums = part_ref[len(late) * QROWS :, :].astype(jnp.float32)
    for n, at in enumerate(late):
        unit = table_ref[at] // PER_UNIT
        mine = (lane == 2 * n) | (lane == 2 * n + 1)
        total = jnp.sum(jnp.where(mine, sums, 0.0), axis=1, keepdims=True)
        weighted_ref[unit] += part_ref[n * QROWS : (n + 1) * QROWS, :].astype(jnp.float32)
        total_ref[unit] += jnp.broadcast_to(total, (QROWS, HD))
    group = 4
    for first in range(0, len(entries) if attends else 0, group):
        found = []
        for n in range(first, min(first + group, len(entries))):
            key = entries[n][2]
            w = table_ref[key[0]] if isinstance(key, tuple) else key
            unit, part = w // PER_UNIT, w % PER_UNIT
            weighted, total = attend(
                queries_ref[unit].astype(jnp.bfloat16),
                stage[n, :, :HD],
                stage[n, :, HD:],
                length_ref[unit] - part * PAGE,
            )
            found.append((unit, weighted, total))
        for unit, weighted, total in found:
            weighted_ref[unit] += weighted
            total_ref[unit] += jnp.broadcast_to(total, (QROWS, HD))
    if finish:
        attended_ref[...] = (weighted_ref[...] / total_ref[...]).astype(jnp.bfloat16)
    for copy in stores:
        copy.wait()


def own_terms(queries_ref, fresh_ref, weighted_ref, total_ref):
    scale = 1.0 / math.sqrt(HD)
    row = lax.broadcasted_iota(jnp.int32, (QROWS, 1), 0)
    for unit in range(U_DEV):
        query = queries_ref[unit]
        weighted = jnp.zeros((QROWS, HD), jnp.float32)
        total = jnp.zeros((QROWS, 1), jnp.float32)
        for j in range(2):
            at = 2 * unit + j
            key = fresh_ref[at : at + 1, :HD]
            value = fresh_ref[at : at + 1, HD:]
            score = jnp.sum(query * key, axis=1, keepdims=True) * scale
            weight = jnp.where(row >= j * GROUP, jnp.exp(score), 0.0)
            total = total + weight
            weighted = weighted + weight.astype(jnp.bfloat16).astype(jnp.float32) * value
        weighted_ref[unit] = weighted
        total_ref[unit] = jnp.broadcast_to(total, (QROWS, HD))


def place_pages(
    table, order, lengths, fresh, queries, sums, parts, late, sources, entries, cache, finish
):
    started, attends = cache is not None, queries is not None
    page_shape = sources[0].shape[1:]
    pages_dev = U_DEV * PER_UNIT
    args = [table, order, lengths, fresh]
    specs = [smem_spec()] * 3 + [vmem_spec()]
    if attends:
        vmem_args = [queries] + (list(sums) if started else []) + list(parts)
        args += vmem_args
        specs += [vmem_spec()] * len(vmem_args)
    args += list(sources)
    specs += [any_spec()] * len(sources)
    aliases = {}
    if started:
        aliases = {len(args): 0}
        args.append(cache)
        specs.append(any_spec())
    outs = [jax.ShapeDtypeStruct((pages_dev,) + page_shape, jnp.bfloat16)]
    out_specs = [any_spec()]
    if attends:
        outs += [jax.ShapeDtypeStruct((U_DEV, QROWS, HD), jnp.float32)] * 2
        out_specs += [vmem_spec()] * 2
    if finish:
        outs.append(jax.ShapeDtypeStruct((U_DEV, QROWS, HD), jnp.bfloat16))
        out_specs.append(vmem_spec())
    count = len(entries)
    result = pl.pallas_call(
        functools.partial(place_kernel, entries, started, attends, finish, late),
        out_shape=tuple(outs),
        in_specs=specs,
        out_specs=tuple(out_specs),
        input_output_aliases=aliases,
        scratch_shapes=[
            pltpu.VMEM((count,) + page_shape, jnp.bfloat16),
            pltpu.SemaphoreType.DMA((count,)),
            pltpu.SemaphoreType.DMA((count,)),
        ],
        compiler_params=pltpu.CompilerParams(vmem_limit_bytes=VMEM_LIMIT),
        name="place_pages",
    )(*args)
    return result[0], result[1:3], result[3] if finish else None


def rows_kernel(
    late,
    units_ref,
    turn_ref,
    order_ref,
    ids_ref,
    lengths_ref,
    rows_ref,
    cosine_ref,
    sine_ref,
    pages_ref,
    passed_ref,
    queries_ref,
    fresh_ref,
    part_ref,
    stage,
    load_sem,
):
    device = lax.axis_index("tp")
    devices, _, width = rows_ref.shape
    pieces = (GROUP + 2) * HD // width
    half_dim = HD // 2
    row = lax.broadcasted_iota(jnp.int32, rows_ref.shape[1:], 0)
    lane = lax.broadcasted_iota(jnp.int32, (QROWS, HD), 1)

    def unit_rows(unit):
        request, head = unit // KVH, unit % KVH
        found = []
        for piece in range(pieces):
            place = turn_ref[(head * pieces + piece) ^ device]
            block = rows_ref[place].astype(jnp.float32)
            picked = [
                jnp.sum(jnp.where(row == 2 * request + j, block, 0.0), axis=0, keepdims=True)
                for j in range(2)
            ]
            for at in range(0, width, HD):
                found.append([line[:, at : at + HD] for line in picked])
        turned = []
        for j in range(2):
            heads = jnp.concatenate([head[j] for head in found[: GROUP + 1]], axis=0)
            swapped = jnp.concatenate([heads[:, half_dim:], heads[:, :half_dim]], axis=1)
            cosine = cosine_ref[pl.ds(2 * request + j, 1), :]
            sine = sine_ref[pl.ds(2 * request + j, 1), :]
            heads = heads * cosine + swapped * sine
            turned.append(heads.astype(jnp.bfloat16).astype(jnp.float32))
        return turned, [found[GROUP + 1][j] for j in range(2)]

    loads = []
    for slot, (source, at) in enumerate(late):
        page = pages_ref.at[order_ref[at]] if source == 0 else passed_ref.at[at]
        copy = pltpu.make_async_copy(page, stage.at[slot], load_sem.at[slot])
        copy.start()
        loads.append(copy)
    sums = jnp.zeros((QROWS, HD), jnp.float32)
    for slot in range(len(late)):
        page = ids_ref[slot]
        unit = page // PER_UNIT
        limit = lengths_ref[unit // KVH] - (page % PER_UNIT) * PAGE
        turned, _ = unit_rows(unit)
        query = jnp.concatenate([turned[0][:GROUP], turned[1][:GROUP]], axis=0)
        loads[slot].wait()
        weighted, total = attend(
            query.astype(jnp.bfloat16), stage[slot, :, :HD], stage[slot, :, HD:], limit
        )
        part_ref[slot * QROWS : (slot + 1) * QROWS, :] = weighted.astype(jnp.bfloat16)
        high = total.astype(jnp.bfloat16).astype(jnp.float32)
        sums = jnp.where(lane == 2 * slot, high, sums)
        sums = jnp.where(lane == 2 * slot + 1, total - high, sums)
    part_ref[len(late) * QROWS :, :] = sums.astype(jnp.bfloat16)
    for slot in range(U_DEV):
        turned, values = unit_rows(units_ref[slot])
        for j in range(2):
            at = 2 * slot + j
            queries_ref[slot, j * GROUP : (j + 1) * GROUP, :] = turned[j][:GROUP]
            fresh_ref[at : at + 1, :HD] = turned[j][GROUP:]
            fresh_ref[at : at + 1, HD:] = values[j]


def rows_and_parts(units, turn, order, ids, lengths, rows, cosine, sine, pages, passed, late):
    return pl.pallas_call(
        functools.partial(rows_kernel, late),
        out_shape=(
            jax.ShapeDtypeStruct((U_DEV, QROWS, HD), jnp.float32),
            jax.ShapeDtypeStruct((2 * U_DEV, 2 * HD), jnp.float32),
            jax.ShapeDtypeStruct(((len(late) + 1) * QROWS, HD), jnp.bfloat16),
        ),
        in_specs=[smem_spec()] * 5 + [vmem_spec()] * 3 + [any_spec()] * 2,
        out_specs=(vmem_spec(),) * 3,
        scratch_shapes=[
            pltpu.VMEM((len(late),) + pages.shape[1:], pages.dtype),
            pltpu.SemaphoreType.DMA((len(late),)),
        ],
        compiler_params=pltpu.CompilerParams(vmem_limit_bytes=VMEM_LIMIT),
        name="rows_and_parts",
    )(units, turn, order, ids, lengths, rows, cosine, sine, pages, passed)


def swap(values, key, devices):
    return lax.ppermute(values, "tp", [(i, i ^ key) for i in range(devices)])


def gather_line(values, devices):
    values = values[None]
    step = devices // 2
    keys = [step // 2, step, step + step // 2]
    found = [swap(values, k, devices) for k in keys]
    return jnp.concatenate([values] + found, axis=0), [0] + keys


def gather_more(values, span, step, devices):
    values = jnp.concatenate([values, swap(values, step, devices)], axis=0)
    return values, span + [s ^ step for s in span]


def after(value, *others):
    return lax.optimization_barrier((value,) + others)[0]


def body(hidden_states, qkv_weight, out_weight, cache_pages, context_lengths, new_units, old_pages):
    devices = lax.axis_size("tp")
    device = lax.axis_index("tp")
    requests = hidden_states.shape[0]
    pages_dev, page_rows, page_width = cache_pages.shape
    capacity = max(1, pages_dev // devices)
    total_units = new_units.shape[0]
    total_pages = old_pages.shape[0]
    pairwise = devices == 2 * KVH

    def own(*keys):
        return [(0, key, r) for key in keys for r in range(capacity)]

    def passed(source, piece):
        return [(source, 0, piece * capacity + r) for r in range(capacity)]

    def piece(chunk, n):
        return chunk[n * capacity : (n + 1) * capacity]

    def send(chunk, key):
        return swap(chunk, key, devices)

    if pairwise:
        half, quarter = devices // 2, devices // 4
        a, b = half, half + quarter
        c, d = a + 2, b + 2
        (chunk_a, cross_far), order = first_pack(
            new_units,
            old_pages,
            cache_pages,
            devices,
            capacity,
            [own(a), own(a + 1, b + 1, c + 1, d + 1)],
            True,
        )
        moved_a, cross_far = send(chunk_a, a), send(cross_far, 1)
        near = list(range(2, half, 2))
        chunk_b, cross_near = next_pack(
            after(order, cross_far), [cache_pages], capacity, [own(b), own(1, *[k + 1 for k in near])]
        )
        moved_b, cross_near = send(chunk_b, b), send(cross_near, 1)
    else:
        (packed,), order = first_pack(
            new_units, old_pages, cache_pages, devices, capacity, [own(*range(devices))], False
        )
        arrived = lax.all_to_all(
            packed.reshape(devices, capacity, page_rows, page_width),
            "tp",
            split_axis=0,
            concat_axis=0,
            tiled=True,
        ).reshape(devices * capacity, page_rows, page_width)

    own_units = lax.dynamic_slice_in_dim(new_units, device * U_DEV, U_DEV)
    own_lengths = context_lengths[own_units // KVH]
    wanted = (
        own_units[:, None] * PER_UNIT + jnp.arange(PER_UNIT, dtype=jnp.int32)[None, :]
    ).reshape(pages_dev)
    source_pos = jnp.sum(
        jnp.where(
            wanted[:, None] == old_pages[None, :],
            jnp.arange(total_pages, dtype=jnp.int32)[None, :],
            0,
        ),
        axis=1,
    )
    source_dev = source_pos // pages_dev
    rank = jnp.sum(
        (
            (source_dev[:, None] == source_dev[None, :])
            & (source_pos[None, :] < source_pos[:, None])
        ).astype(jnp.int32),
        axis=1,
    )
    if pairwise:
        where = (source_dev ^ device) * capacity + rank
        spots = jnp.arange(devices * capacity, dtype=jnp.int32)
        slots = jnp.arange(pages_dev, dtype=jnp.int32)
        table = jnp.sum(jnp.where(where[None, :] == spots[:, None], slots[None, :], 0), axis=1)
    else:
        table = source_dev * capacity + rank

    slot_index = jnp.sum(
        jnp.where(
            new_units[None, :] == jnp.arange(total_units, dtype=jnp.int32)[:, None],
            jnp.arange(total_units, dtype=jnp.int32)[None, :],
            0,
        ),
        axis=1,
    )
    if pairwise:
        ids = old_pages.reshape(devices, 1, pages_dev)
        ids = jnp.concatenate([ids[device], ids[device ^ 1]], axis=0)
        reached = jnp.sum(
            jnp.where(
                (ids // PER_UNIT)[..., None] == new_units, jnp.arange(total_units) // U_DEV, 0
            ),
            axis=-1,
        )
        chosen = reached == (device ^ d)
        earlier = jnp.arange(pages_dev)[None, :] < jnp.arange(pages_dev)[:, None]
        ranks = jnp.sum((chosen[:, None, :] & earlier[None]).astype(jnp.int32), axis=-1)
        wants = jnp.arange(capacity, dtype=jnp.int32)[None, :, None]
        picked = chosen[:, None, :] & (ranks[:, None, :] == wants)
        late_ids = jnp.sum(jnp.where(picked, ids[:, None, :], 0), axis=-1)
        late_ids = late_ids.reshape(2 * capacity).astype(jnp.int32)
    flat_rows = hidden_states.reshape(requests * 2, D)
    if pairwise:
        flat_rows = after(flat_rows, chunk_b)
    own_part = lax.dot_general(
        flat_rows, qkv_weight, (((1,), (1,)), ((), ())), preferred_element_type=jnp.float32
    ).astype(jnp.bfloat16)
    if pairwise:
        positions = context_lengths[:, None] + jnp.arange(2, dtype=jnp.int32)[None, :]
        cosine, sine = rope_tables(positions.reshape(2 * requests))
        rows, span = gather_line(own_part, devices)
        moved_a2 = send(after(piece(cross_far, 0), own_part, moved_a), a)
        moved_b2 = send(after(piece(cross_far, 1), own_part), b)
        near_chunks = next_pack(
            order,
            [cache_pages, after(cross_near, rows)],
            capacity,
            [own(k) + passed(1, n + 1) for n, k in enumerate(near)],
        )
        rows, span = gather_more(after(rows, moved_a, moved_b), span, 2, devices)
        rows_y = rows
        rows, span = gather_more(rows, span, 1, devices)
        moved_near = [
            send(after(near_chunks[0], rows_y), near[0]),
            send(near_chunks[1], near[1]),
            send(after(near_chunks[2], rows), near[2]),
        ]
        turn = jnp.array([span.index(i) for i in range(devices)], jnp.int32)
        late = [(0, d * capacity + r) for r in range(capacity)]
        late += [(1, 3 * capacity + r) for r in range(capacity)]
        places = [key * capacity + r for key in (d, d + 1) for r in range(capacity)]
        queries, fresh, sent = rows_and_parts(
            own_units,
            turn,
            order,
            late_ids,
            context_lengths,
            rows,
            cosine,
            sine,
            cache_pages,
            cross_far,
            late,
        )
        parts = [send(sent, d)]
        chunk_c, chunk_d = next_pack(
            order,
            [cache_pages, after(cross_far, rows)],
            capacity,
            [own(c) + passed(1, 2), own(d)],
        )
        moved_c = send(after(chunk_c, moved_a2), c)

        def place(groups, sums, cache, attends, parts, finish):
            entries, sources = [], []
            for array, keys, first in groups:
                for n, key in enumerate(keys):
                    for r in range(capacity):
                        at = (r,) if array is cache_pages else first + n * capacity + r
                        entries.append((len(sources), at, (key * capacity + r,)))
                sources.append(array)
            return place_pages(
                table,
                order,
                own_lengths,
                fresh,
                queries if attends else None,
                sums,
                parts,
                places if parts else [],
                sources,
                entries,
                cache,
                finish,
            )

        new_cache, sums, _ = place(
            [(cache_pages, [0], 0), (cross_near, [1], 0), (moved_a, [a], 0), (moved_b, [b], 0)],
            None,
            None,
            True,
            [],
            False,
        )
        new_cache, sums, _ = place(
            [(m, [k, k + 1], 0) for m, k in zip(moved_near, near)], sums, new_cache, True, [], False
        )
        moved_d = send(after(chunk_d, moved_b2, sums[0]), d)
        new_cache, sums, _ = place(
            [(moved_a2, [a + 1], 0), (moved_b2, [b + 1], 0)], sums, new_cache, True, parts, False
        )
        new_cache, sums, attended = place(
            [(moved_c, [c, c + 1], 0)], sums, new_cache, True, [], True
        )
        attended = after(attended, moved_d)
        moved_d2 = send(after(piece(cross_far, 3), attended), d)
        new_cache, _, _ = place(
            [(moved_d, [d], 0), (moved_d2, [d + 1], 0)], None, new_cache, False, [], False
        )
    else:
        own_requests, own_heads = own_units // KVH, own_units % KVH
        positions = own_lengths[:, None] + jnp.arange(2, dtype=jnp.int32)[None, :]
        cosine, sine = rope_tables(positions.reshape(2 * U_DEV))
        rows = lax.all_gather(own_part, "tp", axis=1, tiled=True)
        rows = rows.reshape(requests, 2, KVH, GROUP + 2, HD)
        rows = rows[own_requests, :, own_heads].astype(jnp.float32)
        turned = rotate(
            rows[:, :, : GROUP + 1],
            cosine.reshape(U_DEV, 2, 1, HD),
            sine.reshape(U_DEV, 2, 1, HD),
        )
        queries = turned[:, :, :GROUP].reshape(U_DEV, QROWS, HD)
        fresh = jnp.concatenate([turned[:, :, GROUP], rows[:, :, GROUP + 1]], axis=-1)
        fresh = fresh.reshape(2 * U_DEV, 2 * HD).astype(jnp.bfloat16).astype(jnp.float32)
        queries = queries.astype(jnp.bfloat16).astype(jnp.float32)
        entries = [(0, (w,), w) for w in range(pages_dev)]
        new_cache, sums, attended = place_pages(
            table,
            table,
            own_lengths,
            fresh,
            queries,
            None,
            [],
            [],
            [arrived],
            entries,
            None,
            True,
        )

    attended = attended.reshape(U_DEV, 2, GROUP * HD)
    if pairwise:
        heads, span = gather_line(attended, devices)
        heads, span = gather_more(heads, span, 2, devices)
        heads, span = gather_more(heads, span, 1, devices)
        holder = turn[(slot_index // U_DEV) ^ device]
        heads = heads.reshape(total_units, 2, GROUP * HD)[holder * U_DEV + slot_index % U_DEV]
    else:
        heads = lax.all_gather(attended, "tp", axis=0, tiled=True)[slot_index]
    logical = (
        heads.reshape(requests, KVH, 2, GROUP * HD)
        .transpose(0, 2, 1, 3)
        .reshape(requests * 2, HEADS * HD)
    )
    mixed_rows = lax.dot_general(
        logical, out_weight, (((1,), (1,)), ((), ())), preferred_element_type=jnp.float32
    )
    mixed_rows = mixed_rows.astype(jnp.bfloat16).reshape(requests, 2, out_weight.shape[0])
    return (mixed_rows, new_cache)


def solution(mesh):
    in_specs = (
        P("group", None, None),
        P("tp", None),
        P("tp", None),
        P(("group", "tp"), None, None),
        P("group"),
        P("group"),
        P("group"),
    )
    out_specs = (P("group", None, "tp"), P(("group", "tp"), None, None))
    return jax.shard_map(body, mesh=mesh, in_specs=in_specs, out_specs=out_specs, check_vma=False)
```

```python
import functools
import math

import jax
import jax.numpy as jnp
from jax import lax
from jax.experimental import pallas as pl
from jax.experimental.pallas import tpu as pltpu
from jax.sharding import PartitionSpec as P

D = 8192
HEADS = 64
KVH = 8
HD = 128
U_DEV = 4
MAXCTX = 2048
PAGE = 128
GROUP = HEADS // KVH
QROWS = 2 * GROUP
PER_UNIT = MAXCTX // PAGE
VMEM_LIMIT = 56 * 1024 * 1024

rope_base = 10000.0


def rope_tables(positions):
    half_dim = HD // 2
    frequency = rope_base ** (-(jnp.arange(half_dim, dtype=jnp.float32) * 2.0 / HD))
    angles = positions.astype(jnp.float32)[..., None] * frequency
    cosine = jnp.concatenate([jnp.cos(angles), jnp.cos(angles)], axis=-1)
    sine = jnp.concatenate([-jnp.sin(angles), jnp.sin(angles)], axis=-1)
    return cosine, sine


def rotate(values, cosine, sine):
    half_dim = HD // 2
    turned = jnp.concatenate([values[..., half_dim:], values[..., :half_dim]], axis=-1)
    return values * cosine + turned * sine


def any_spec():
    return pl.BlockSpec(memory_space=pl.ANY)


def smem_spec():
    return pl.BlockSpec(memory_space=pltpu.SMEM)


def vmem_spec():
    return pl.BlockSpec(memory_space=pltpu.VMEM)


def load_order(devices, capacity, relative, units_ref, old_ref, order_ref, slots, count):
    device = lax.axis_index("tp")
    total_units = units_ref.shape[0]
    pages_dev = old_ref.shape[0] // devices

    def clear(t, carry):
        count[t] = 0
        return carry

    def empty(t, carry):
        order_ref[t] = 0
        return carry

    def invert(q, carry):
        slots[units_ref[q]] = q
        return carry

    def assign(i, carry):
        unit = old_ref[device * pages_dev + i] // PER_UNIT
        target = slots[unit] // U_DEV
        if relative:
            target = target ^ device
        rank = count[target]
        count[target] = rank + 1
        order_ref[target * capacity + rank] = i
        return carry

    lax.fori_loop(0, devices, clear, 0, unroll=8)
    if devices * capacity > pages_dev:
        lax.fori_loop(0, devices * capacity, empty, 0, unroll=8)
    lax.fori_loop(0, total_units, invert, 0, unroll=8)
    lax.fori_loop(0, pages_dev, assign, 0, unroll=8)


def move_pages(outs_pages, capacity, order_ref, sources, outs, stage, load_sem, store_sem):
    loads, stores = [], []
    for source, key, r in sum(outs_pages, []):
        slot = len(loads)
        index = order_ref[key * capacity + r] if source == 0 else r
        copy = pltpu.make_async_copy(
            sources[source].at[index], stage.at[slot], load_sem.at[slot]
        )
        copy.start()
        loads.append(copy)
    slot = 0
    for n, pages in enumerate(outs_pages):
        count = len(pages)
        for copy in loads[slot : slot + count]:
            copy.wait()
        copy = pltpu.make_async_copy(stage.at[pl.ds(slot, count)], outs[n], store_sem.at[n])
        copy.start()
        stores.append(copy)
        slot += count
    for copy in stores:
        copy.wait()


def first_pack_kernel(
    devices, capacity, outs_pages, relative, units_ref, old_ref, pages_ref, *rest
):
    outs = rest[:-6]
    order_ref, slots, count, stage, load_sem, store_sem = rest[-6:]
    load_order(devices, capacity, relative, units_ref, old_ref, order_ref, slots, count)
    move_pages(
        outs_pages, capacity, order_ref, [pages_ref], outs, stage, load_sem, store_sem
    )


def next_pack_kernel(capacity, outs_pages, sources, order_ref, *rest):
    source_refs, outs = rest[:sources], rest[sources:-3]
    stage, load_sem, store_sem = rest[-3:]
    move_pages(
        outs_pages, capacity, order_ref, source_refs, outs, stage, load_sem, store_sem
    )


def pack_shapes(outs_pages, pages):
    total = sum(len(p) for p in outs_pages)
    shapes = [jax.ShapeDtypeStruct((len(p),) + pages.shape[1:], pages.dtype) for p in outs_pages]
    scratch = [
        pltpu.VMEM((total,) + pages.shape[1:], pages.dtype),
        pltpu.SemaphoreType.DMA((total,)),
        pltpu.SemaphoreType.DMA((len(outs_pages),)),
    ]
    return shapes, scratch


def first_pack(new_units, old_pages, pages, devices, capacity, outs_pages, relative):
    outs, scratch = pack_shapes(outs_pages, pages)
    result = pl.pallas_call(
        functools.partial(first_pack_kernel, devices, capacity, outs_pages, relative),
        out_shape=tuple(outs) + (jax.ShapeDtypeStruct((devices * capacity,), jnp.int32),),
        in_specs=[smem_spec(), smem_spec(), any_spec()],
        out_specs=tuple(any_spec() for _ in outs) + (smem_spec(),),
        scratch_shapes=[
            pltpu.SMEM(new_units.shape, jnp.int32),
            pltpu.SMEM((devices,), jnp.int32),
        ]
        + scratch,
        compiler_params=pltpu.CompilerParams(vmem_limit_bytes=VMEM_LIMIT),
        name="first_pack",
    )(new_units, old_pages, pages)
    return result[:-1], result[-1]


def next_pack(order, sources, capacity, outs_pages):
    outs, scratch = pack_shapes(outs_pages, sources[0])
    return pl.pallas_call(
        functools.partial(next_pack_kernel, capacity, outs_pages, len(sources)),
        out_shape=tuple(outs),
        in_specs=[smem_spec()] + [any_spec()] * len(sources),
        out_specs=tuple(any_spec() for _ in outs),
        scratch_shapes=scratch,
        compiler_params=pltpu.CompilerParams(vmem_limit_bytes=VMEM_LIMIT),
        name="next_pack",
    )(order, *sources)


def attend(query, keys, values, limit):
    scale = 1.0 / math.sqrt(HD)
    scores = (
        lax.dot_general(query, keys, (((1,), (1,)), ((), ())), preferred_element_type=jnp.float32)
        * scale
    )
    lane = lax.broadcasted_iota(jnp.int32, scores.shape, 1)
    weights = jnp.where(lane < limit, jnp.exp(scores), 0.0)
    total = jnp.sum(weights, axis=1, keepdims=True)
    weighted = jnp.dot(weights.astype(jnp.bfloat16), values, preferred_element_type=jnp.float32)
    return weighted, total


ALIGN = 16


def place_kernel(entries, started, attends, finish, late, *refs):
    refs = list(refs)
    table_ref, order_ref, length_ref, fresh_ref = refs[:4]
    refs = refs[4:]
    if attends:
        queries_ref = refs.pop(0)
        if started:
            weighted_in, total_in = refs.pop(0), refs.pop(0)
        part_ref = refs.pop(0) if late else None
    sources = 1 + max(source for source, _, _ in entries)
    source_refs, refs = refs[:sources], refs[sources:]
    if started:
        refs.pop(0)
    out_ref = refs.pop(0)
    if attends:
        weighted_ref, total_ref = refs.pop(0), refs.pop(0)
    attended_ref = refs.pop(0) if finish else None
    stage, load_sem, store_sem = refs
    if attends and started:
        weighted_ref[...] = weighted_in[...]
        total_ref[...] = total_in[...]
    loads = []
    for n, (source, index, _) in enumerate(entries):
        index = order_ref[index[0]] if isinstance(index, tuple) else index
        copy = pltpu.make_async_copy(
            source_refs[source].at[index], stage.at[n], load_sem.at[n]
        )
        copy.start()
        loads.append(copy)
    row = lax.broadcasted_iota(jnp.int32, (ALIGN, 2 * HD), 0)
    stores = []
    for n, (_, _, key) in enumerate(entries):
        w = table_ref[key[0]] if isinstance(key, tuple) else key
        unit, part = w // PER_UNIT, w % PER_UNIT
        length = length_ref[unit]
        loads[n].wait()
        for j in range(2):
            position = length + j

            @pl.when(position // PAGE == part)
            def _():
                inside = position % PAGE
                rows = pl.ds(pl.multiple_of(inside // ALIGN * ALIGN, ALIGN), ALIGN)
                block = stage[n, rows, :].astype(jnp.float32)
                token = fresh_ref[pl.ds(2 * unit + j, 1), :]
                block = jnp.where(row == inside % ALIGN, token, block)
                stage[n, rows, :] = block.astype(jnp.bfloat16)

        copy = pltpu.make_async_copy(stage.at[n], out_ref.at[w], store_sem.at[n])
        copy.start()
        stores.append(copy)
    if attends and not started:
        own_terms(queries_ref, fresh_ref, weighted_ref, total_ref)
    lane = lax.broadcasted_iota(jnp.int32, (QROWS, HD), 1)
    if late:
        sums = part_ref[len(late) * QROWS :, :].astype(jnp.float32)
    for n, at in enumerate(late):
        unit = table_ref[at] // PER_UNIT
        mine = (lane == 2 * n) | (lane == 2 * n + 1)
        total = jnp.sum(jnp.where(mine, sums, 0.0), axis=1, keepdims=True)
        weighted_ref[unit] += part_ref[n * QROWS : (n + 1) * QROWS, :].astype(jnp.float32)
        total_ref[unit] += jnp.broadcast_to(total, (QROWS, HD))
    group = 4
    for first in range(0, len(entries) if attends else 0, group):
        found = []
        for n in range(first, min(first + group, len(entries))):
            key = entries[n][2]
            w = table_ref[key[0]] if isinstance(key, tuple) else key
            unit, part = w // PER_UNIT, w % PER_UNIT
            weighted, total = attend(
                queries_ref[unit].astype(jnp.bfloat16),
                stage[n, :, :HD],
                stage[n, :, HD:],
                length_ref[unit] - part * PAGE,
            )
            found.append((unit, weighted, total))
        for unit, weighted, total in found:
            weighted_ref[unit] += weighted
            total_ref[unit] += jnp.broadcast_to(total, (QROWS, HD))
    if finish:
        attended_ref[...] = (weighted_ref[...] / total_ref[...]).astype(jnp.bfloat16)
    for copy in stores:
        copy.wait()


def own_terms(queries_ref, fresh_ref, weighted_ref, total_ref):
    scale = 1.0 / math.sqrt(HD)
    row = lax.broadcasted_iota(jnp.int32, (QROWS, 1), 0)
    for unit in range(U_DEV):
        query = queries_ref[unit]
        weighted = jnp.zeros((QROWS, HD), jnp.float32)
        total = jnp.zeros((QROWS, 1), jnp.float32)
        for j in range(2):
            at = 2 * unit + j
            key = fresh_ref[at : at + 1, :HD]
            value = fresh_ref[at : at + 1, HD:]
            score = jnp.sum(query * key, axis=1, keepdims=True) * scale
            weight = jnp.where(row >= j * GROUP, jnp.exp(score), 0.0)
            total = total + weight
            weighted = weighted + weight.astype(jnp.bfloat16).astype(jnp.float32) * value
        weighted_ref[unit] = weighted
        total_ref[unit] = jnp.broadcast_to(total, (QROWS, HD))


def place_pages(
    table, order, lengths, fresh, queries, sums, parts, late, sources, entries, cache, finish
):
    started, attends = cache is not None, queries is not None
    page_shape = sources[0].shape[1:]
    pages_dev = U_DEV * PER_UNIT
    args = [table, order, lengths, fresh]
    specs = [smem_spec()] * 3 + [vmem_spec()]
    if attends:
        vmem_args = [queries] + (list(sums) if started else []) + list(parts)
        args += vmem_args
        specs += [vmem_spec()] * len(vmem_args)
    args += list(sources)
    specs += [any_spec()] * len(sources)
    aliases = {}
    if started:
        aliases = {len(args): 0}
        args.append(cache)
        specs.append(any_spec())
    outs = [jax.ShapeDtypeStruct((pages_dev,) + page_shape, jnp.bfloat16)]
    out_specs = [any_spec()]
    if attends:
        outs += [jax.ShapeDtypeStruct((U_DEV, QROWS, HD), jnp.float32)] * 2
        out_specs += [vmem_spec()] * 2
    if finish:
        outs.append(jax.ShapeDtypeStruct((U_DEV, QROWS, HD), jnp.bfloat16))
        out_specs.append(vmem_spec())
    count = len(entries)
    result = pl.pallas_call(
        functools.partial(place_kernel, entries, started, attends, finish, late),
        out_shape=tuple(outs),
        in_specs=specs,
        out_specs=tuple(out_specs),
        input_output_aliases=aliases,
        scratch_shapes=[
            pltpu.VMEM((count,) + page_shape, jnp.bfloat16),
            pltpu.SemaphoreType.DMA((count,)),
            pltpu.SemaphoreType.DMA((count,)),
        ],
        compiler_params=pltpu.CompilerParams(vmem_limit_bytes=VMEM_LIMIT),
        name="place_pages",
    )(*args)
    return result[0], result[1:3], result[3] if finish else None


def rows_kernel(
    late,
    units_ref,
    turn_ref,
    order_ref,
    ids_ref,
    lengths_ref,
    rows_ref,
    cosine_ref,
    sine_ref,
    pages_ref,
    passed_ref,
    queries_ref,
    fresh_ref,
    part_ref,
    stage,
    load_sem,
):
    device = lax.axis_index("tp")
    devices, _, width = rows_ref.shape
    pieces = (GROUP + 2) * HD // width
    half_dim = HD // 2
    row = lax.broadcasted_iota(jnp.int32, rows_ref.shape[1:], 0)
    lane = lax.broadcasted_iota(jnp.int32, (QROWS, HD), 1)

    def unit_rows(unit):
        request, head = unit // KVH, unit % KVH
        found = []
        for piece in range(pieces):
            place = turn_ref[(head * pieces + piece) ^ device]
            block = rows_ref[place].astype(jnp.float32)
            picked = [
                jnp.sum(jnp.where(row == 2 * request + j, block, 0.0), axis=0, keepdims=True)
                for j in range(2)
            ]
            for at in range(0, width, HD):
                found.append([line[:, at : at + HD] for line in picked])
        turned = []
        for j in range(2):
            heads = jnp.concatenate([head[j] for head in found[: GROUP + 1]], axis=0)
            swapped = jnp.concatenate([heads[:, half_dim:], heads[:, :half_dim]], axis=1)
            cosine = cosine_ref[pl.ds(2 * request + j, 1), :]
            sine = sine_ref[pl.ds(2 * request + j, 1), :]
            heads = heads * cosine + swapped * sine
            turned.append(heads.astype(jnp.bfloat16).astype(jnp.float32))
        return turned, [found[GROUP + 1][j] for j in range(2)]

    loads = []
    for slot, (source, at) in enumerate(late):
        page = pages_ref.at[order_ref[at]] if source == 0 else passed_ref.at[at]
        copy = pltpu.make_async_copy(page, stage.at[slot], load_sem.at[slot])
        copy.start()
        loads.append(copy)
    sums = jnp.zeros((QROWS, HD), jnp.float32)
    for slot in range(len(late)):
        page = ids_ref[slot]
        unit = page // PER_UNIT
        limit = lengths_ref[unit // KVH] - (page % PER_UNIT) * PAGE
        turned, _ = unit_rows(unit)
        query = jnp.concatenate([turned[0][:GROUP], turned[1][:GROUP]], axis=0)
        loads[slot].wait()
        weighted, total = attend(
            query.astype(jnp.bfloat16), stage[slot, :, :HD], stage[slot, :, HD:], limit
        )
        part_ref[slot * QROWS : (slot + 1) * QROWS, :] = weighted.astype(jnp.bfloat16)
        high = total.astype(jnp.bfloat16).astype(jnp.float32)
        sums = jnp.where(lane == 2 * slot, high, sums)
        sums = jnp.where(lane == 2 * slot + 1, total - high, sums)
    part_ref[len(late) * QROWS :, :] = sums.astype(jnp.bfloat16)
    for slot in range(U_DEV):
        turned, values = unit_rows(units_ref[slot])
        for j in range(2):
            at = 2 * slot + j
            queries_ref[slot, j * GROUP : (j + 1) * GROUP, :] = turned[j][:GROUP]
            fresh_ref[at : at + 1, :HD] = turned[j][GROUP:]
            fresh_ref[at : at + 1, HD:] = values[j]


def rows_and_parts(units, turn, order, ids, lengths, rows, cosine, sine, pages, passed, late):
    return pl.pallas_call(
        functools.partial(rows_kernel, late),
        out_shape=(
            jax.ShapeDtypeStruct((U_DEV, QROWS, HD), jnp.float32),
            jax.ShapeDtypeStruct((2 * U_DEV, 2 * HD), jnp.float32),
            jax.ShapeDtypeStruct(((len(late) + 1) * QROWS, HD), jnp.bfloat16),
        ),
        in_specs=[smem_spec()] * 5 + [vmem_spec()] * 3 + [any_spec()] * 2,
        out_specs=(vmem_spec(),) * 3,
        scratch_shapes=[
            pltpu.VMEM((len(late),) + pages.shape[1:], pages.dtype),
            pltpu.SemaphoreType.DMA((len(late),)),
        ],
        compiler_params=pltpu.CompilerParams(vmem_limit_bytes=VMEM_LIMIT),
        name="rows_and_parts",
    )(units, turn, order, ids, lengths, rows, cosine, sine, pages, passed)


def swap(values, key, devices):
    return lax.ppermute(values, "tp", [(i, i ^ key) for i in range(devices)])


def gather_line(values, devices):
    values = values[None]
    step = devices // 2
    keys = [step // 2, step, step + step // 2]
    found = [swap(values, k, devices) for k in keys]
    return jnp.concatenate([values] + found, axis=0), [0] + keys


def gather_more(values, span, step, devices):
    values = jnp.concatenate([values, swap(values, step, devices)], axis=0)
    return values, span + [s ^ step for s in span]


def after(value, *others):
    return lax.optimization_barrier((value,) + others)[0]


def body(hidden_states, qkv_weight, out_weight, cache_pages, context_lengths, new_units, old_pages):
    devices = lax.axis_size("tp")
    device = lax.axis_index("tp")
    requests = hidden_states.shape[0]
    pages_dev, page_rows, page_width = cache_pages.shape
    capacity = max(1, pages_dev // devices)
    total_units = new_units.shape[0]
    total_pages = old_pages.shape[0]
    pairwise = devices == 2 * KVH

    def own(*keys):
        return [(0, key, r) for key in keys for r in range(capacity)]

    def passed(source, piece):
        return [(source, 0, piece * capacity + r) for r in range(capacity)]

    def piece(chunk, n):
        return chunk[n * capacity : (n + 1) * capacity]

    def send(chunk, key):
        return swap(chunk, key, devices)

    if pairwise:
        half, quarter = devices // 2, devices // 4
        a, b = half, half + quarter
        c, d = a + 2, b + 2
        near = list(range(2, half, 2))
        (chunk_a, cross_near), order = first_pack(
            new_units,
            old_pages,
            cache_pages,
            devices,
            capacity,
            [own(a), own(1, *[k + 1 for k in near])],
            True,
        )
        moved_a, cross_near = send(chunk_a, a), send(cross_near, 1)
        chunk_4, chunk_6, chunk_b, cross_far = next_pack(
            order,
            [cache_pages, cross_near],
            capacity,
            [
                own(near[1]) + passed(1, 2),
                own(near[2]) + passed(1, 3),
                own(b),
                own(a + 1, b + 1, c + 1, d + 1),
            ],
        )
        moved_4, moved_6 = send(chunk_4, near[1]), send(chunk_6, near[2])
        moved_b, cross_far = send(chunk_b, b), send(cross_far, 1)
    else:
        (packed,), order = first_pack(
            new_units, old_pages, cache_pages, devices, capacity, [own(*range(devices))], False
        )
        arrived = lax.all_to_all(
            packed.reshape(devices, capacity, page_rows, page_width),
            "tp",
            split_axis=0,
            concat_axis=0,
            tiled=True,
        ).reshape(devices * capacity, page_rows, page_width)

    own_units = lax.dynamic_slice_in_dim(new_units, device * U_DEV, U_DEV)
    own_lengths = context_lengths[own_units // KVH]
    wanted = (
        own_units[:, None] * PER_UNIT + jnp.arange(PER_UNIT, dtype=jnp.int32)[None, :]
    ).reshape(pages_dev)
    source_pos = jnp.sum(
        jnp.where(
            wanted[:, None] == old_pages[None, :],
            jnp.arange(total_pages, dtype=jnp.int32)[None, :],
            0,
        ),
        axis=1,
    )
    source_dev = source_pos // pages_dev
    rank = jnp.sum(
        (
            (source_dev[:, None] == source_dev[None, :])
            & (source_pos[None, :] < source_pos[:, None])
        ).astype(jnp.int32),
        axis=1,
    )
    if pairwise:
        where = (source_dev ^ device) * capacity + rank
        spots = jnp.arange(devices * capacity, dtype=jnp.int32)
        slots = jnp.arange(pages_dev, dtype=jnp.int32)
        table = jnp.sum(jnp.where(where[None, :] == spots[:, None], slots[None, :], 0), axis=1)
    else:
        table = source_dev * capacity + rank

    slot_index = jnp.sum(
        jnp.where(
            new_units[None, :] == jnp.arange(total_units, dtype=jnp.int32)[:, None],
            jnp.arange(total_units, dtype=jnp.int32)[None, :],
            0,
        ),
        axis=1,
    )
    if pairwise:
        ids = old_pages.reshape(devices, 1, pages_dev)
        ids = jnp.concatenate([ids[device], ids[device ^ 1]], axis=0)
        reached = jnp.sum(
            jnp.where(
                (ids // PER_UNIT)[..., None] == new_units, jnp.arange(total_units) // U_DEV, 0
            ),
            axis=-1,
        )
        chosen = reached == (device ^ d)
        earlier = jnp.arange(pages_dev)[None, :] < jnp.arange(pages_dev)[:, None]
        ranks = jnp.sum((chosen[:, None, :] & earlier[None]).astype(jnp.int32), axis=-1)
        wants = jnp.arange(capacity, dtype=jnp.int32)[None, :, None]
        picked = chosen[:, None, :] & (ranks[:, None, :] == wants)
        late_ids = jnp.sum(jnp.where(picked, ids[:, None, :], 0), axis=-1)
        late_ids = late_ids.reshape(2 * capacity).astype(jnp.int32)
    flat_rows = hidden_states.reshape(requests * 2, D)
    if pairwise:
        flat_rows = after(flat_rows, cross_far)
    own_part = lax.dot_general(
        flat_rows, qkv_weight, (((1,), (1,)), ((), ())), preferred_element_type=jnp.float32
    ).astype(jnp.bfloat16)
    if pairwise:
        positions = context_lengths[:, None] + jnp.arange(2, dtype=jnp.int32)[None, :]
        cosine, sine = rope_tables(positions.reshape(2 * requests))
        rows, span = gather_line(own_part, devices)
        moved_a2 = send(after(piece(cross_far, 0), own_part, moved_a), a)
        moved_b2 = send(after(piece(cross_far, 1), own_part), b)
        rows, span = gather_more(after(rows, moved_a, moved_b), span, 2, devices)
        rows, span = gather_more(rows, span, 1, devices)
        turn = jnp.array([span.index(i) for i in range(devices)], jnp.int32)
        late = [(0, d * capacity + r) for r in range(capacity)]
        late += [(1, 3 * capacity + r) for r in range(capacity)]
        places = [key * capacity + r for key in (d, d + 1) for r in range(capacity)]
        queries, fresh, sent = rows_and_parts(
            own_units,
            turn,
            order,
            late_ids,
            context_lengths,
            rows,
            cosine,
            sine,
            cache_pages,
            cross_far,
            late,
        )
        parts = [send(sent, d)]
        chunk_c, chunk_d, chunk_2 = next_pack(
            order,
            [cache_pages, after(cross_far, rows), cross_near],
            capacity,
            [own(c) + passed(1, 2), own(d), own(near[0]) + passed(2, 1)],
        )
        moved_2 = send(chunk_2, near[0])
        moved_c = send(after(chunk_c, moved_a2, sent), c)

        def place(groups, sums, cache, attends, parts, finish):
            entries, sources = [], []
            for array, keys, first in groups:
                for n, key in enumerate(keys):
                    for r in range(capacity):
                        at = (r,) if array is cache_pages else first + n * capacity + r
                        entries.append((len(sources), at, (key * capacity + r,)))
                sources.append(array)
            return place_pages(
                table,
                order,
                own_lengths,
                fresh,
                queries if attends else None,
                sums,
                parts,
                places if parts else [],
                sources,
                entries,
                cache,
                finish,
            )

        new_cache, sums, _ = place(
            [(cache_pages, [0], 0), (cross_near, [1], 0), (moved_a, [a], 0), (moved_b, [b], 0)],
            None,
            None,
            True,
            [],
            False,
        )
        new_cache, sums, _ = place(
            [(moved_4, [near[1], near[1] + 1], 0), (moved_6, [near[2], near[2] + 1], 0)],
            sums,
            new_cache,
            True,
            [],
            False,
        )
        new_cache, sums, _ = place(
            [(moved_a2, [a + 1], 0), (moved_b2, [b + 1], 0), (moved_2, [near[0], near[0] + 1], 0)],
            sums,
            new_cache,
            True,
            [],
            False,
        )
        moved_d = send(after(chunk_d, moved_b2, sums[0], parts[0]), d)
        new_cache, sums, attended = place(
            [(moved_c, [c, c + 1], 0)], sums, new_cache, True, parts, True
        )
        attended = after(attended, moved_d)
        moved_d2 = send(after(piece(cross_far, 3), attended), d)
        new_cache, _, _ = place(
            [(moved_d, [d], 0), (moved_d2, [d + 1], 0)], None, new_cache, False, [], False
        )
    else:
        own_requests, own_heads = own_units // KVH, own_units % KVH
        positions = own_lengths[:, None] + jnp.arange(2, dtype=jnp.int32)[None, :]
        cosine, sine = rope_tables(positions.reshape(2 * U_DEV))
        rows = lax.all_gather(own_part, "tp", axis=1, tiled=True)
        rows = rows.reshape(requests, 2, KVH, GROUP + 2, HD)
        rows = rows[own_requests, :, own_heads].astype(jnp.float32)
        turned = rotate(
            rows[:, :, : GROUP + 1],
            cosine.reshape(U_DEV, 2, 1, HD),
            sine.reshape(U_DEV, 2, 1, HD),
        )
        queries = turned[:, :, :GROUP].reshape(U_DEV, QROWS, HD)
        fresh = jnp.concatenate([turned[:, :, GROUP], rows[:, :, GROUP + 1]], axis=-1)
        fresh = fresh.reshape(2 * U_DEV, 2 * HD).astype(jnp.bfloat16).astype(jnp.float32)
        queries = queries.astype(jnp.bfloat16).astype(jnp.float32)
        entries = [(0, (w,), w) for w in range(pages_dev)]
        new_cache, sums, attended = place_pages(
            table,
            table,
            own_lengths,
            fresh,
            queries,
            None,
            [],
            [],
            [arrived],
            entries,
            None,
            True,
        )

    attended = attended.reshape(U_DEV, 2, GROUP * HD)
    if pairwise:
        heads, span = gather_line(attended, devices)
        heads, span = gather_more(heads, span, 2, devices)
        heads, span = gather_more(heads, span, 1, devices)
        holder = turn[(slot_index // U_DEV) ^ device]
        heads = heads.reshape(total_units, 2, GROUP * HD)[holder * U_DEV + slot_index % U_DEV]
    else:
        heads = lax.all_gather(attended, "tp", axis=0, tiled=True)[slot_index]
    logical = (
        heads.reshape(requests, KVH, 2, GROUP * HD)
        .transpose(0, 2, 1, 3)
        .reshape(requests * 2, HEADS * HD)
    )
    mixed_rows = lax.dot_general(
        logical, out_weight, (((1,), (1,)), ((), ())), preferred_element_type=jnp.float32
    )
    mixed_rows = mixed_rows.astype(jnp.bfloat16).reshape(requests, 2, out_weight.shape[0])
    return (mixed_rows, new_cache)


def solution(mesh):
    in_specs = (
        P("group", None, None),
        P("tp", None),
        P("tp", None),
        P(("group", "tp"), None, None),
        P("group"),
        P("group"),
        P("group"),
    )
    out_specs = (P("group", None, "tp"), P(("group", "tp"), None, None))
    return jax.shard_map(body, mesh=mesh, in_specs=in_specs, out_specs=out_specs, check_vma=False)
```

```python
import functools
import math

import jax
import jax.numpy as jnp
from jax import lax
from jax.experimental import pallas as pl
from jax.experimental.pallas import tpu as pltpu
from jax.sharding import PartitionSpec as P

D = 8192
HEADS = 64
KVH = 8
HD = 128
U_DEV = 4
MAXCTX = 2048
PAGE = 128
GROUP = HEADS // KVH
QROWS = 2 * GROUP
PER_UNIT = MAXCTX // PAGE
VMEM_LIMIT = 56 * 1024 * 1024

rope_base = 10000.0


def rope_tables(positions):
    half_dim = HD // 2
    frequency = rope_base ** (-(jnp.arange(half_dim, dtype=jnp.float32) * 2.0 / HD))
    angles = positions.astype(jnp.float32)[..., None] * frequency
    cosine = jnp.concatenate([jnp.cos(angles), jnp.cos(angles)], axis=-1)
    sine = jnp.concatenate([-jnp.sin(angles), jnp.sin(angles)], axis=-1)
    return cosine, sine


def rotate(values, cosine, sine):
    half_dim = HD // 2
    turned = jnp.concatenate([values[..., half_dim:], values[..., :half_dim]], axis=-1)
    return values * cosine + turned * sine


def any_spec():
    return pl.BlockSpec(memory_space=pl.ANY)


def smem_spec():
    return pl.BlockSpec(memory_space=pltpu.SMEM)


def vmem_spec():
    return pl.BlockSpec(memory_space=pltpu.VMEM)


def load_order(devices, capacity, relative, units_ref, old_ref, order_ref, slots, count):
    device = lax.axis_index("tp")
    total_units = units_ref.shape[0]
    pages_dev = old_ref.shape[0] // devices

    def clear(t, carry):
        count[t] = 0
        return carry

    def empty(t, carry):
        order_ref[t] = 0
        return carry

    def invert(q, carry):
        slots[units_ref[q]] = q
        return carry

    def assign(i, carry):
        unit = old_ref[device * pages_dev + i] // PER_UNIT
        target = slots[unit] // U_DEV
        if relative:
            target = target ^ device
        rank = count[target]
        count[target] = rank + 1
        order_ref[target * capacity + rank] = i
        return carry

    lax.fori_loop(0, devices, clear, 0, unroll=8)
    if devices * capacity > pages_dev:
        lax.fori_loop(0, devices * capacity, empty, 0, unroll=8)
    lax.fori_loop(0, total_units, invert, 0, unroll=8)
    lax.fori_loop(0, pages_dev, assign, 0, unroll=8)


def move_pages(outs_pages, capacity, order_ref, sources, outs, stage, load_sem, store_sem):
    loads, stores = [], []
    for source, key, r in sum(outs_pages, []):
        slot = len(loads)
        index = order_ref[key * capacity + r] if source == 0 else r
        copy = pltpu.make_async_copy(
            sources[source].at[index], stage.at[slot], load_sem.at[slot]
        )
        copy.start()
        loads.append(copy)
    slot = 0
    for n, pages in enumerate(outs_pages):
        count = len(pages)
        for copy in loads[slot : slot + count]:
            copy.wait()
        copy = pltpu.make_async_copy(stage.at[pl.ds(slot, count)], outs[n], store_sem.at[n])
        copy.start()
        stores.append(copy)
        slot += count
    for copy in stores:
        copy.wait()


def first_pack_kernel(
    devices, capacity, outs_pages, relative, units_ref, old_ref, pages_ref, *rest
):
    outs = rest[:-6]
    order_ref, slots, count, stage, load_sem, store_sem = rest[-6:]
    load_order(devices, capacity, relative, units_ref, old_ref, order_ref, slots, count)
    move_pages(
        outs_pages, capacity, order_ref, [pages_ref], outs, stage, load_sem, store_sem
    )


def next_pack_kernel(capacity, outs_pages, sources, order_ref, *rest):
    source_refs, outs = rest[:sources], rest[sources:-3]
    stage, load_sem, store_sem = rest[-3:]
    move_pages(
        outs_pages, capacity, order_ref, source_refs, outs, stage, load_sem, store_sem
    )


def pack_shapes(outs_pages, pages):
    total = sum(len(p) for p in outs_pages)
    shapes = [jax.ShapeDtypeStruct((len(p),) + pages.shape[1:], pages.dtype) for p in outs_pages]
    scratch = [
        pltpu.VMEM((total,) + pages.shape[1:], pages.dtype),
        pltpu.SemaphoreType.DMA((total,)),
        pltpu.SemaphoreType.DMA((len(outs_pages),)),
    ]
    return shapes, scratch


def first_pack(new_units, old_pages, pages, devices, capacity, outs_pages, relative):
    outs, scratch = pack_shapes(outs_pages, pages)
    result = pl.pallas_call(
        functools.partial(first_pack_kernel, devices, capacity, outs_pages, relative),
        out_shape=tuple(outs) + (jax.ShapeDtypeStruct((devices * capacity,), jnp.int32),),
        in_specs=[smem_spec(), smem_spec(), any_spec()],
        out_specs=tuple(any_spec() for _ in outs) + (smem_spec(),),
        scratch_shapes=[
            pltpu.SMEM(new_units.shape, jnp.int32),
            pltpu.SMEM((devices,), jnp.int32),
        ]
        + scratch,
        compiler_params=pltpu.CompilerParams(vmem_limit_bytes=VMEM_LIMIT),
        name="first_pack",
    )(new_units, old_pages, pages)
    return result[:-1], result[-1]


def next_pack(order, sources, capacity, outs_pages):
    outs, scratch = pack_shapes(outs_pages, sources[0])
    return pl.pallas_call(
        functools.partial(next_pack_kernel, capacity, outs_pages, len(sources)),
        out_shape=tuple(outs),
        in_specs=[smem_spec()] + [any_spec()] * len(sources),
        out_specs=tuple(any_spec() for _ in outs),
        scratch_shapes=scratch,
        compiler_params=pltpu.CompilerParams(vmem_limit_bytes=VMEM_LIMIT),
        name="next_pack",
    )(order, *sources)


def attend(query, keys, values, limit):
    scale = 1.0 / math.sqrt(HD)
    scores = (
        lax.dot_general(query, keys, (((1,), (1,)), ((), ())), preferred_element_type=jnp.float32)
        * scale
    )
    lane = lax.broadcasted_iota(jnp.int32, scores.shape, 1)
    weights = jnp.where(lane < limit, jnp.exp(scores), 0.0)
    total = jnp.sum(weights, axis=1, keepdims=True)
    weighted = jnp.dot(weights.astype(jnp.bfloat16), values, preferred_element_type=jnp.float32)
    return weighted, total


ALIGN = 16


def place_kernel(entries, started, attends, finish, late, *refs):
    refs = list(refs)
    table_ref, order_ref, length_ref, fresh_ref = refs[:4]
    refs = refs[4:]
    if attends:
        queries_ref = refs.pop(0)
        if started:
            weighted_in, total_in = refs.pop(0), refs.pop(0)
        part_ref = refs.pop(0) if late else None
    sources = 1 + max(source for source, _, _ in entries)
    source_refs, refs = refs[:sources], refs[sources:]
    if started:
        refs.pop(0)
    out_ref = refs.pop(0)
    if attends:
        weighted_ref, total_ref = refs.pop(0), refs.pop(0)
    attended_ref = refs.pop(0) if finish else None
    stage, load_sem, store_sem = refs
    if attends and started:
        weighted_ref[...] = weighted_in[...]
        total_ref[...] = total_in[...]
    loads = []
    for n, (source, index, _) in enumerate(entries):
        index = order_ref[index[0]] if isinstance(index, tuple) else index
        copy = pltpu.make_async_copy(
            source_refs[source].at[index], stage.at[n], load_sem.at[n]
        )
        copy.start()
        loads.append(copy)
    row = lax.broadcasted_iota(jnp.int32, (ALIGN, 2 * HD), 0)
    stores = []
    for n, (_, _, key) in enumerate(entries):
        w = table_ref[key[0]] if isinstance(key, tuple) else key
        unit, part = w // PER_UNIT, w % PER_UNIT
        length = length_ref[unit]
        loads[n].wait()
        for j in range(2):
            position = length + j

            @pl.when(position // PAGE == part)
            def _():
                inside = position % PAGE
                rows = pl.ds(pl.multiple_of(inside // ALIGN * ALIGN, ALIGN), ALIGN)
                block = stage[n, rows, :].astype(jnp.float32)
                token = fresh_ref[pl.ds(2 * unit + j, 1), :]
                block = jnp.where(row == inside % ALIGN, token, block)
                stage[n, rows, :] = block.astype(jnp.bfloat16)

        copy = pltpu.make_async_copy(stage.at[n], out_ref.at[w], store_sem.at[n])
        copy.start()
        stores.append(copy)
    if attends and not started:
        own_terms(queries_ref, fresh_ref, weighted_ref, total_ref)
    lane = lax.broadcasted_iota(jnp.int32, (QROWS, HD), 1)
    if late:
        sums = part_ref[len(late) * QROWS :, :].astype(jnp.float32)
    for n, at in enumerate(late):
        unit = table_ref[at] // PER_UNIT
        mine = (lane == 2 * n) | (lane == 2 * n + 1)
        total = jnp.sum(jnp.where(mine, sums, 0.0), axis=1, keepdims=True)
        weighted_ref[unit] += part_ref[n * QROWS : (n + 1) * QROWS, :].astype(jnp.float32)
        total_ref[unit] += jnp.broadcast_to(total, (QROWS, HD))
    group = 4
    for first in range(0, len(entries) if attends else 0, group):
        found = []
        for n in range(first, min(first + group, len(entries))):
            key = entries[n][2]
            w = table_ref[key[0]] if isinstance(key, tuple) else key
            unit, part = w // PER_UNIT, w % PER_UNIT
            weighted, total = attend(
                queries_ref[unit].astype(jnp.bfloat16),
                stage[n, :, :HD],
                stage[n, :, HD:],
                length_ref[unit] - part * PAGE,
            )
            found.append((unit, weighted, total))
        for unit, weighted, total in found:
            weighted_ref[unit] += weighted
            total_ref[unit] += jnp.broadcast_to(total, (QROWS, HD))
    if finish:
        attended_ref[...] = (weighted_ref[...] / total_ref[...]).astype(jnp.bfloat16)
    for copy in stores:
        copy.wait()


def own_terms(queries_ref, fresh_ref, weighted_ref, total_ref):
    scale = 1.0 / math.sqrt(HD)
    row = lax.broadcasted_iota(jnp.int32, (QROWS, 1), 0)
    for unit in range(U_DEV):
        query = queries_ref[unit]
        weighted = jnp.zeros((QROWS, HD), jnp.float32)
        total = jnp.zeros((QROWS, 1), jnp.float32)
        for j in range(2):
            at = 2 * unit + j
            key = fresh_ref[at : at + 1, :HD]
            value = fresh_ref[at : at + 1, HD:]
            score = jnp.sum(query * key, axis=1, keepdims=True) * scale
            weight = jnp.where(row >= j * GROUP, jnp.exp(score), 0.0)
            total = total + weight
            weighted = weighted + weight.astype(jnp.bfloat16).astype(jnp.float32) * value
        weighted_ref[unit] = weighted
        total_ref[unit] = jnp.broadcast_to(total, (QROWS, HD))


def place_pages(
    table, order, lengths, fresh, queries, sums, parts, late, sources, entries, cache, finish
):
    started, attends = cache is not None, queries is not None
    page_shape = sources[0].shape[1:]
    pages_dev = U_DEV * PER_UNIT
    args = [table, order, lengths, fresh]
    specs = [smem_spec()] * 3 + [vmem_spec()]
    if attends:
        vmem_args = [queries] + (list(sums) if started else []) + list(parts)
        args += vmem_args
        specs += [vmem_spec()] * len(vmem_args)
    args += list(sources)
    specs += [any_spec()] * len(sources)
    aliases = {}
    if started:
        aliases = {len(args): 0}
        args.append(cache)
        specs.append(any_spec())
    outs = [jax.ShapeDtypeStruct((pages_dev,) + page_shape, jnp.bfloat16)]
    out_specs = [any_spec()]
    if attends:
        outs += [jax.ShapeDtypeStruct((U_DEV, QROWS, HD), jnp.float32)] * 2
        out_specs += [vmem_spec()] * 2
    if finish:
        outs.append(jax.ShapeDtypeStruct((U_DEV, QROWS, HD), jnp.bfloat16))
        out_specs.append(vmem_spec())
    count = len(entries)
    result = pl.pallas_call(
        functools.partial(place_kernel, entries, started, attends, finish, late),
        out_shape=tuple(outs),
        in_specs=specs,
        out_specs=tuple(out_specs),
        input_output_aliases=aliases,
        scratch_shapes=[
            pltpu.VMEM((count,) + page_shape, jnp.bfloat16),
            pltpu.SemaphoreType.DMA((count,)),
            pltpu.SemaphoreType.DMA((count,)),
        ],
        compiler_params=pltpu.CompilerParams(vmem_limit_bytes=VMEM_LIMIT),
        name="place_pages",
    )(*args)
    return result[0], result[1:3], result[3] if finish else None


def rows_kernel(
    late,
    units_ref,
    turn_ref,
    order_ref,
    ids_ref,
    lengths_ref,
    rows_ref,
    cosine_ref,
    sine_ref,
    pages_ref,
    passed_ref,
    queries_ref,
    fresh_ref,
    part_ref,
    stage,
    load_sem,
):
    device = lax.axis_index("tp")
    devices, _, width = rows_ref.shape
    pieces = (GROUP + 2) * HD // width
    half_dim = HD // 2
    row = lax.broadcasted_iota(jnp.int32, rows_ref.shape[1:], 0)
    lane = lax.broadcasted_iota(jnp.int32, (QROWS, HD), 1)

    def unit_rows(unit):
        request, head = unit // KVH, unit % KVH
        found = []
        for piece in range(pieces):
            place = turn_ref[(head * pieces + piece) ^ device]
            block = rows_ref[place].astype(jnp.float32)
            picked = [
                jnp.sum(jnp.where(row == 2 * request + j, block, 0.0), axis=0, keepdims=True)
                for j in range(2)
            ]
            for at in range(0, width, HD):
                found.append([line[:, at : at + HD] for line in picked])
        turned = []
        for j in range(2):
            heads = jnp.concatenate([head[j] for head in found[: GROUP + 1]], axis=0)
            swapped = jnp.concatenate([heads[:, half_dim:], heads[:, :half_dim]], axis=1)
            cosine = cosine_ref[pl.ds(2 * request + j, 1), :]
            sine = sine_ref[pl.ds(2 * request + j, 1), :]
            heads = heads * cosine + swapped * sine
            turned.append(heads.astype(jnp.bfloat16).astype(jnp.float32))
        return turned, [found[GROUP + 1][j] for j in range(2)]

    loads = []
    for slot, (source, at) in enumerate(late):
        page = pages_ref.at[order_ref[at]] if source == 0 else passed_ref.at[at]
        copy = pltpu.make_async_copy(page, stage.at[slot], load_sem.at[slot])
        copy.start()
        loads.append(copy)
    sums = jnp.zeros((QROWS, HD), jnp.float32)
    for slot in range(len(late)):
        page = ids_ref[slot]
        unit = page // PER_UNIT
        limit = lengths_ref[unit // KVH] - (page % PER_UNIT) * PAGE
        turned, _ = unit_rows(unit)
        query = jnp.concatenate([turned[0][:GROUP], turned[1][:GROUP]], axis=0)
        loads[slot].wait()
        weighted, total = attend(
            query.astype(jnp.bfloat16), stage[slot, :, :HD], stage[slot, :, HD:], limit
        )
        part_ref[slot * QROWS : (slot + 1) * QROWS, :] = weighted.astype(jnp.bfloat16)
        high = total.astype(jnp.bfloat16).astype(jnp.float32)
        sums = jnp.where(lane == 2 * slot, high, sums)
        sums = jnp.where(lane == 2 * slot + 1, total - high, sums)
    part_ref[len(late) * QROWS :, :] = sums.astype(jnp.bfloat16)
    for slot in range(U_DEV):
        turned, values = unit_rows(units_ref[slot])
        for j in range(2):
            at = 2 * slot + j
            queries_ref[slot, j * GROUP : (j + 1) * GROUP, :] = turned[j][:GROUP]
            fresh_ref[at : at + 1, :HD] = turned[j][GROUP:]
            fresh_ref[at : at + 1, HD:] = values[j]


def rows_and_parts(units, turn, order, ids, lengths, rows, cosine, sine, pages, passed, late):
    return pl.pallas_call(
        functools.partial(rows_kernel, late),
        out_shape=(
            jax.ShapeDtypeStruct((U_DEV, QROWS, HD), jnp.float32),
            jax.ShapeDtypeStruct((2 * U_DEV, 2 * HD), jnp.float32),
            jax.ShapeDtypeStruct(((len(late) + 1) * QROWS, HD), jnp.bfloat16),
        ),
        in_specs=[smem_spec()] * 5 + [vmem_spec()] * 3 + [any_spec()] * 2,
        out_specs=(vmem_spec(),) * 3,
        scratch_shapes=[
            pltpu.VMEM((len(late),) + pages.shape[1:], pages.dtype),
            pltpu.SemaphoreType.DMA((len(late),)),
        ],
        compiler_params=pltpu.CompilerParams(vmem_limit_bytes=VMEM_LIMIT),
        name="rows_and_parts",
    )(units, turn, order, ids, lengths, rows, cosine, sine, pages, passed)


def swap(values, key, devices):
    return lax.ppermute(values, "tp", [(i, i ^ key) for i in range(devices)])


def gather_line(values, devices):
    values = values[None]
    step = devices // 2
    keys = [step // 2, step, step + step // 2]
    found = [swap(values, k, devices) for k in keys]
    return jnp.concatenate([values] + found, axis=0), [0] + keys


def gather_more(values, span, step, devices):
    values = jnp.concatenate([values, swap(values, step, devices)], axis=0)
    return values, span + [s ^ step for s in span]


def after(value, *others):
    return lax.optimization_barrier((value,) + others)[0]


def body(hidden_states, qkv_weight, out_weight, cache_pages, context_lengths, new_units, old_pages):
    devices = lax.axis_size("tp")
    device = lax.axis_index("tp")
    requests = hidden_states.shape[0]
    pages_dev, page_rows, page_width = cache_pages.shape
    capacity = max(1, pages_dev // devices)
    total_units = new_units.shape[0]
    total_pages = old_pages.shape[0]
    pairwise = devices == 2 * KVH

    def own(*keys):
        return [(0, key, r) for key in keys for r in range(capacity)]

    def passed(source, piece):
        return [(source, 0, piece * capacity + r) for r in range(capacity)]

    def piece(chunk, n):
        return chunk[n * capacity : (n + 1) * capacity]

    def send(chunk, key):
        return swap(chunk, key, devices)

    if pairwise:
        half, quarter = devices // 2, devices // 4
        a, b = half, half + quarter
        c, d = a + 2, b + 2
        near = list(range(2, half, 2))
        (chunk_a, cross_near), order = first_pack(
            new_units,
            old_pages,
            cache_pages,
            devices,
            capacity,
            [own(a), own(1, *[k + 1 for k in near])],
            True,
        )
        moved_a, cross_near = send(chunk_a, a), send(cross_near, 1)
        chunk_4, chunk_6, chunk_b, cross_far = next_pack(
            order,
            [cache_pages, cross_near],
            capacity,
            [
                own(near[1]) + passed(1, 2),
                own(near[2]) + passed(1, 3),
                own(b),
                own(a + 1, b + 1, c + 1, d + 1),
            ],
        )
        moved_b, cross_far = send(chunk_b, b), send(cross_far, 1)
    else:
        (packed,), order = first_pack(
            new_units, old_pages, cache_pages, devices, capacity, [own(*range(devices))], False
        )
        arrived = lax.all_to_all(
            packed.reshape(devices, capacity, page_rows, page_width),
            "tp",
            split_axis=0,
            concat_axis=0,
            tiled=True,
        ).reshape(devices * capacity, page_rows, page_width)

    slot_index = jnp.sum(
        jnp.where(
            new_units[None, :] == jnp.arange(total_units, dtype=jnp.int32)[:, None],
            jnp.arange(total_units, dtype=jnp.int32)[None, :],
            0,
        ),
        axis=1,
    )
    if pairwise:
        ids = old_pages.reshape(devices, 1, pages_dev)
        ids = jnp.concatenate([ids[device], ids[device ^ 1]], axis=0)
        reached = jnp.sum(
            jnp.where(
                (ids // PER_UNIT)[..., None] == new_units, jnp.arange(total_units) // U_DEV, 0
            ),
            axis=-1,
        )
        chosen = reached == (device ^ d)
        earlier = jnp.arange(pages_dev)[None, :] < jnp.arange(pages_dev)[:, None]
        ranks = jnp.sum((chosen[:, None, :] & earlier[None]).astype(jnp.int32), axis=-1)
        wants = jnp.arange(capacity, dtype=jnp.int32)[None, :, None]
        picked = chosen[:, None, :] & (ranks[:, None, :] == wants)
        late_ids = jnp.sum(jnp.where(picked, ids[:, None, :], 0), axis=-1)
        late_ids = late_ids.reshape(2 * capacity).astype(jnp.int32)
    flat_rows = hidden_states.reshape(requests * 2, D)
    if pairwise:
        flat_rows = after(flat_rows, cross_far)
    own_part = lax.dot_general(
        flat_rows, qkv_weight, (((1,), (1,)), ((), ())), preferred_element_type=jnp.float32
    ).astype(jnp.bfloat16)
    if pairwise:
        new_units, old_pages, _ = lax.optimization_barrier((new_units, old_pages, own_part))
    own_units = lax.dynamic_slice_in_dim(new_units, device * U_DEV, U_DEV)
    own_lengths = context_lengths[own_units // KVH]
    wanted = (
        own_units[:, None] * PER_UNIT + jnp.arange(PER_UNIT, dtype=jnp.int32)[None, :]
    ).reshape(pages_dev)
    source_pos = jnp.sum(
        jnp.where(
            wanted[:, None] == old_pages[None, :],
            jnp.arange(total_pages, dtype=jnp.int32)[None, :],
            0,
        ),
        axis=1,
    )
    source_dev = source_pos // pages_dev
    rank = jnp.sum(
        (
            (source_dev[:, None] == source_dev[None, :])
            & (source_pos[None, :] < source_pos[:, None])
        ).astype(jnp.int32),
        axis=1,
    )
    if pairwise:
        where = (source_dev ^ device) * capacity + rank
        spots = jnp.arange(devices * capacity, dtype=jnp.int32)
        slots = jnp.arange(pages_dev, dtype=jnp.int32)
        table = jnp.sum(jnp.where(where[None, :] == spots[:, None], slots[None, :], 0), axis=1)
    else:
        table = source_dev * capacity + rank

    if pairwise:
        positions = context_lengths[:, None] + jnp.arange(2, dtype=jnp.int32)[None, :]
        cosine, sine = rope_tables(positions.reshape(2 * requests))
        rows, span = gather_line(own_part, devices)
        moved_a2 = send(after(piece(cross_far, 0), own_part, moved_a), a)
        moved_4 = send(after(chunk_4, rows), near[1])
        moved_6 = send(after(chunk_6, rows), near[2])
        moved_b2 = send(after(piece(cross_far, 1), own_part), b)
        rows, span = gather_more(after(rows, moved_a, moved_b), span, 2, devices)
        rows, span = gather_more(rows, span, 1, devices)
        turn = jnp.array([span.index(i) for i in range(devices)], jnp.int32)
        late = [(0, d * capacity + r) for r in range(capacity)]
        late += [(1, 3 * capacity + r) for r in range(capacity)]
        places = [key * capacity + r for key in (d, d + 1) for r in range(capacity)]
        queries, fresh, sent = rows_and_parts(
            own_units,
            turn,
            order,
            late_ids,
            context_lengths,
            rows,
            cosine,
            sine,
            cache_pages,
            cross_far,
            late,
        )
        parts = [send(sent, d)]
        chunk_c, chunk_d, chunk_2 = next_pack(
            order,
            [cache_pages, after(cross_far, rows), cross_near],
            capacity,
            [own(c) + passed(1, 2), own(d), own(near[0]) + passed(2, 1)],
        )
        moved_2 = send(after(chunk_2, sent), near[0])
        moved_c = send(after(chunk_c, sent, moved_a2), c)

        def place(groups, sums, cache, attends, parts, finish):
            entries, sources = [], []
            for array, keys, first in groups:
                for n, key in enumerate(keys):
                    for r in range(capacity):
                        at = (r,) if array is cache_pages else first + n * capacity + r
                        entries.append((len(sources), at, (key * capacity + r,)))
                sources.append(array)
            return place_pages(
                table,
                order,
                own_lengths,
                fresh,
                queries if attends else None,
                sums,
                parts,
                places if parts else [],
                sources,
                entries,
                cache,
                finish,
            )

        new_cache, sums, _ = place(
            [(cache_pages, [0], 0), (cross_near, [1], 0), (moved_a, [a], 0), (moved_b, [b], 0)],
            None,
            None,
            True,
            [],
            False,
        )
        new_cache, sums, _ = place(
            [(moved_4, [near[1], near[1] + 1], 0), (moved_6, [near[2], near[2] + 1], 0)],
            sums,
            new_cache,
            True,
            [],
            False,
        )
        new_cache, sums, _ = place(
            [(moved_a2, [a + 1], 0), (moved_b2, [b + 1], 0), (moved_2, [near[0], near[0] + 1], 0)],
            sums,
            new_cache,
            True,
            [],
            False,
        )
        moved_d = send(after(chunk_d, moved_b2, sums[0], parts[0]), d)
        new_cache, sums, attended = place(
            [(moved_c, [c, c + 1], 0)], sums, new_cache, True, parts, True
        )
        attended = after(attended, moved_d)
        moved_d2 = send(after(piece(cross_far, 3), attended), d)
        new_cache, _, _ = place(
            [(moved_d, [d], 0), (moved_d2, [d + 1], 0)], None, new_cache, False, [], False
        )
    else:
        own_requests, own_heads = own_units // KVH, own_units % KVH
        positions = own_lengths[:, None] + jnp.arange(2, dtype=jnp.int32)[None, :]
        cosine, sine = rope_tables(positions.reshape(2 * U_DEV))
        rows = lax.all_gather(own_part, "tp", axis=1, tiled=True)
        rows = rows.reshape(requests, 2, KVH, GROUP + 2, HD)
        rows = rows[own_requests, :, own_heads].astype(jnp.float32)
        turned = rotate(
            rows[:, :, : GROUP + 1],
            cosine.reshape(U_DEV, 2, 1, HD),
            sine.reshape(U_DEV, 2, 1, HD),
        )
        queries = turned[:, :, :GROUP].reshape(U_DEV, QROWS, HD)
        fresh = jnp.concatenate([turned[:, :, GROUP], rows[:, :, GROUP + 1]], axis=-1)
        fresh = fresh.reshape(2 * U_DEV, 2 * HD).astype(jnp.bfloat16).astype(jnp.float32)
        queries = queries.astype(jnp.bfloat16).astype(jnp.float32)
        entries = [(0, (w,), w) for w in range(pages_dev)]
        new_cache, sums, attended = place_pages(
            table,
            table,
            own_lengths,
            fresh,
            queries,
            None,
            [],
            [],
            [arrived],
            entries,
            None,
            True,
        )

    attended = attended.reshape(U_DEV, 2, GROUP * HD)
    if pairwise:
        heads, span = gather_line(attended, devices)
        heads, span = gather_more(heads, span, 2, devices)
        heads, span = gather_more(heads, span, 1, devices)
        holder = turn[(slot_index // U_DEV) ^ device]
        heads = heads.reshape(total_units, 2, GROUP * HD)[holder * U_DEV + slot_index % U_DEV]
    else:
        heads = lax.all_gather(attended, "tp", axis=0, tiled=True)[slot_index]
    logical = (
        heads.reshape(requests, KVH, 2, GROUP * HD)
        .transpose(0, 2, 1, 3)
        .reshape(requests * 2, HEADS * HD)
    )
    if pairwise:
        logical = after(logical, moved_d2)
    mixed_rows = lax.dot_general(
        logical, out_weight, (((1,), (1,)), ((), ())), preferred_element_type=jnp.float32
    )
    mixed_rows = mixed_rows.astype(jnp.bfloat16).reshape(requests, 2, out_weight.shape[0])
    return (mixed_rows, new_cache)


def solution(mesh):
    in_specs = (
        P("group", None, None),
        P("tp", None),
        P("tp", None),
        P(("group", "tp"), None, None),
        P("group"),
        P("group"),
        P("group"),
    )
    out_specs = (P("group", None, "tp"), P(("group", "tp"), None, None))
    return jax.shard_map(body, mesh=mesh, in_specs=in_specs, out_specs=out_specs, check_vma=False)
```

```python
import functools
import math

import jax
import jax.numpy as jnp
from jax import lax
from jax.experimental import pallas as pl
from jax.experimental.pallas import tpu as pltpu
from jax.sharding import PartitionSpec as P

D = 8192
HEADS = 64
KVH = 8
HD = 128
U_DEV = 4
MAXCTX = 2048
PAGE = 128
GROUP = HEADS // KVH
QROWS = 2 * GROUP
PER_UNIT = MAXCTX // PAGE
VMEM_LIMIT = 56 * 1024 * 1024

rope_base = 10000.0


def rope_tables(positions):
    half_dim = HD // 2
    frequency = rope_base ** (-(jnp.arange(half_dim, dtype=jnp.float32) * 2.0 / HD))
    angles = positions.astype(jnp.float32)[..., None] * frequency
    cosine = jnp.concatenate([jnp.cos(angles), jnp.cos(angles)], axis=-1)
    sine = jnp.concatenate([-jnp.sin(angles), jnp.sin(angles)], axis=-1)
    return cosine, sine


def rotate(values, cosine, sine):
    half_dim = HD // 2
    turned = jnp.concatenate([values[..., half_dim:], values[..., :half_dim]], axis=-1)
    return values * cosine + turned * sine


def any_spec():
    return pl.BlockSpec(memory_space=pl.ANY)


def smem_spec():
    return pl.BlockSpec(memory_space=pltpu.SMEM)


def vmem_spec():
    return pl.BlockSpec(memory_space=pltpu.VMEM)


def load_order(devices, capacity, relative, units_ref, old_ref, order_ref, slots, count):
    device = lax.axis_index("tp")
    total_units = units_ref.shape[0]
    pages_dev = old_ref.shape[0] // devices

    def clear(t, carry):
        count[t] = 0
        return carry

    def empty(t, carry):
        order_ref[t] = 0
        return carry

    def invert(q, carry):
        slots[units_ref[q]] = q
        return carry

    def assign(i, carry):
        unit = old_ref[device * pages_dev + i] // PER_UNIT
        target = slots[unit] // U_DEV
        if relative:
            target = target ^ device
        rank = count[target]
        count[target] = rank + 1
        order_ref[target * capacity + rank] = i
        return carry

    lax.fori_loop(0, devices, clear, 0, unroll=8)
    if devices * capacity > pages_dev:
        lax.fori_loop(0, devices * capacity, empty, 0, unroll=8)
    lax.fori_loop(0, total_units, invert, 0, unroll=8)
    lax.fori_loop(0, pages_dev, assign, 0, unroll=8)


def move_pages(outs_pages, capacity, order_ref, sources, outs, stage, load_sem, store_sem):
    loads, stores = [], []
    for source, key, r in sum(outs_pages, []):
        slot = len(loads)
        index = order_ref[key * capacity + r] if source == 0 else r
        copy = pltpu.make_async_copy(
            sources[source].at[index], stage.at[slot], load_sem.at[slot]
        )
        copy.start()
        loads.append(copy)
    slot = 0
    for n, pages in enumerate(outs_pages):
        count = len(pages)
        for copy in loads[slot : slot + count]:
            copy.wait()
        copy = pltpu.make_async_copy(stage.at[pl.ds(slot, count)], outs[n], store_sem.at[n])
        copy.start()
        stores.append(copy)
        slot += count
    for copy in stores:
        copy.wait()


def first_pack_kernel(
    devices, capacity, outs_pages, relative, units_ref, old_ref, pages_ref, *rest
):
    outs = rest[:-6]
    order_ref, slots, count, stage, load_sem, store_sem = rest[-6:]
    load_order(devices, capacity, relative, units_ref, old_ref, order_ref, slots, count)
    move_pages(
        outs_pages, capacity, order_ref, [pages_ref], outs, stage, load_sem, store_sem
    )


def next_pack_kernel(capacity, outs_pages, sources, order_ref, *rest):
    source_refs, outs = rest[:sources], rest[sources:-3]
    stage, load_sem, store_sem = rest[-3:]
    move_pages(
        outs_pages, capacity, order_ref, source_refs, outs, stage, load_sem, store_sem
    )


def pack_shapes(outs_pages, pages):
    total = sum(len(p) for p in outs_pages)
    shapes = [jax.ShapeDtypeStruct((len(p),) + pages.shape[1:], pages.dtype) for p in outs_pages]
    scratch = [
        pltpu.VMEM((total,) + pages.shape[1:], pages.dtype),
        pltpu.SemaphoreType.DMA((total,)),
        pltpu.SemaphoreType.DMA((len(outs_pages),)),
    ]
    return shapes, scratch


def first_pack(new_units, old_pages, pages, devices, capacity, outs_pages, relative):
    outs, scratch = pack_shapes(outs_pages, pages)
    result = pl.pallas_call(
        functools.partial(first_pack_kernel, devices, capacity, outs_pages, relative),
        out_shape=tuple(outs) + (jax.ShapeDtypeStruct((devices * capacity,), jnp.int32),),
        in_specs=[smem_spec(), smem_spec(), any_spec()],
        out_specs=tuple(any_spec() for _ in outs) + (smem_spec(),),
        scratch_shapes=[
            pltpu.SMEM(new_units.shape, jnp.int32),
            pltpu.SMEM((devices,), jnp.int32),
        ]
        + scratch,
        compiler_params=pltpu.CompilerParams(vmem_limit_bytes=VMEM_LIMIT),
        name="first_pack",
    )(new_units, old_pages, pages)
    return result[:-1], result[-1]


def next_pack(order, sources, capacity, outs_pages):
    outs, scratch = pack_shapes(outs_pages, sources[0])
    return pl.pallas_call(
        functools.partial(next_pack_kernel, capacity, outs_pages, len(sources)),
        out_shape=tuple(outs),
        in_specs=[smem_spec()] + [any_spec()] * len(sources),
        out_specs=tuple(any_spec() for _ in outs),
        scratch_shapes=scratch,
        compiler_params=pltpu.CompilerParams(vmem_limit_bytes=VMEM_LIMIT),
        name="next_pack",
    )(order, *sources)


def attend(query, keys, values, limit):
    scale = 1.0 / math.sqrt(HD)
    scores = (
        lax.dot_general(query, keys, (((1,), (1,)), ((), ())), preferred_element_type=jnp.float32)
        * scale
    )
    lane = lax.broadcasted_iota(jnp.int32, scores.shape, 1)
    weights = jnp.where(lane < limit, jnp.exp(scores), 0.0)
    total = jnp.sum(weights, axis=1, keepdims=True)
    weighted = jnp.dot(weights.astype(jnp.bfloat16), values, preferred_element_type=jnp.float32)
    return weighted, total


ALIGN = 16


def place_kernel(entries, started, attends, finish, late, *refs):
    refs = list(refs)
    table_ref, order_ref, length_ref, fresh_ref = refs[:4]
    refs = refs[4:]
    if attends:
        queries_ref = refs.pop(0)
        if started:
            weighted_in, total_in = refs.pop(0), refs.pop(0)
        part_ref = refs.pop(0) if late else None
    sources = 1 + max(source for source, _, _ in entries)
    source_refs, refs = refs[:sources], refs[sources:]
    if started:
        refs.pop(0)
    out_ref = refs.pop(0)
    if attends:
        weighted_ref, total_ref = refs.pop(0), refs.pop(0)
    attended_ref = refs.pop(0) if finish else None
    stage, load_sem, store_sem = refs
    if attends and started:
        weighted_ref[...] = weighted_in[...]
        total_ref[...] = total_in[...]
    loads = []
    for n, (source, index, _) in enumerate(entries):
        index = order_ref[index[0]] if isinstance(index, tuple) else index
        copy = pltpu.make_async_copy(
            source_refs[source].at[index], stage.at[n], load_sem.at[n]
        )
        copy.start()
        loads.append(copy)
    row = lax.broadcasted_iota(jnp.int32, (ALIGN, 2 * HD), 0)
    stores = []
    for n, (_, _, key) in enumerate(entries):
        w = table_ref[key[0]] if isinstance(key, tuple) else key
        unit, part = w // PER_UNIT, w % PER_UNIT
        length = length_ref[unit]
        loads[n].wait()
        for j in range(2):
            position = length + j

            @pl.when(position // PAGE == part)
            def _():
                inside = position % PAGE
                rows = pl.ds(pl.multiple_of(inside // ALIGN * ALIGN, ALIGN), ALIGN)
                block = stage[n, rows, :].astype(jnp.float32)
                token = fresh_ref[pl.ds(2 * unit + j, 1), :]
                block = jnp.where(row == inside % ALIGN, token, block)
                stage[n, rows, :] = block.astype(jnp.bfloat16)

        copy = pltpu.make_async_copy(stage.at[n], out_ref.at[w], store_sem.at[n])
        copy.start()
        stores.append(copy)
    if attends and not started:
        own_terms(queries_ref, fresh_ref, weighted_ref, total_ref)
    lane = lax.broadcasted_iota(jnp.int32, (QROWS, HD), 1)
    if late:
        sums = part_ref[len(late) * QROWS :, :].astype(jnp.float32)
    for n, at in enumerate(late):
        unit = table_ref[at] // PER_UNIT
        mine = (lane == 2 * n) | (lane == 2 * n + 1)
        total = jnp.sum(jnp.where(mine, sums, 0.0), axis=1, keepdims=True)
        weighted_ref[unit] += part_ref[n * QROWS : (n + 1) * QROWS, :].astype(jnp.float32)
        total_ref[unit] += jnp.broadcast_to(total, (QROWS, HD))
    group = 8
    for first in range(0, len(entries) if attends else 0, group):
        found = []
        for n in range(first, min(first + group, len(entries))):
            key = entries[n][2]
            w = table_ref[key[0]] if isinstance(key, tuple) else key
            unit, part = w // PER_UNIT, w % PER_UNIT
            weighted, total = attend(
                queries_ref[unit].astype(jnp.bfloat16),
                stage[n, :, :HD],
                stage[n, :, HD:],
                length_ref[unit] - part * PAGE,
            )
            found.append((unit, weighted, total))
        for unit, weighted, total in found:
            weighted_ref[unit] += weighted
            total_ref[unit] += jnp.broadcast_to(total, (QROWS, HD))
    if finish:
        attended_ref[...] = (weighted_ref[...] / total_ref[...]).astype(jnp.bfloat16)
    for copy in stores:
        copy.wait()


def own_terms(queries_ref, fresh_ref, weighted_ref, total_ref):
    scale = 1.0 / math.sqrt(HD)
    row = lax.broadcasted_iota(jnp.int32, (QROWS, 1), 0)
    for unit in range(U_DEV):
        query = queries_ref[unit]
        weighted = jnp.zeros((QROWS, HD), jnp.float32)
        total = jnp.zeros((QROWS, 1), jnp.float32)
        for j in range(2):
            at = 2 * unit + j
            key = fresh_ref[at : at + 1, :HD]
            value = fresh_ref[at : at + 1, HD:]
            score = jnp.sum(query * key, axis=1, keepdims=True) * scale
            weight = jnp.where(row >= j * GROUP, jnp.exp(score), 0.0)
            total = total + weight
            weighted = weighted + weight.astype(jnp.bfloat16).astype(jnp.float32) * value
        weighted_ref[unit] = weighted
        total_ref[unit] = jnp.broadcast_to(total, (QROWS, HD))


def place_pages(
    table, order, lengths, fresh, queries, sums, parts, late, sources, entries, cache, finish
):
    started, attends = cache is not None, queries is not None
    page_shape = sources[0].shape[1:]
    pages_dev = U_DEV * PER_UNIT
    args = [table, order, lengths, fresh]
    specs = [smem_spec()] * 3 + [vmem_spec()]
    if attends:
        vmem_args = [queries] + (list(sums) if started else []) + list(parts)
        args += vmem_args
        specs += [vmem_spec()] * len(vmem_args)
    args += list(sources)
    specs += [any_spec()] * len(sources)
    aliases = {}
    if started:
        aliases = {len(args): 0}
        args.append(cache)
        specs.append(any_spec())
    outs = [jax.ShapeDtypeStruct((pages_dev,) + page_shape, jnp.bfloat16)]
    out_specs = [any_spec()]
    if attends:
        outs += [jax.ShapeDtypeStruct((U_DEV, QROWS, HD), jnp.float32)] * 2
        out_specs += [vmem_spec()] * 2
    if finish:
        outs.append(jax.ShapeDtypeStruct((U_DEV, QROWS, HD), jnp.bfloat16))
        out_specs.append(vmem_spec())
    count = len(entries)
    result = pl.pallas_call(
        functools.partial(place_kernel, entries, started, attends, finish, late),
        out_shape=tuple(outs),
        in_specs=specs,
        out_specs=tuple(out_specs),
        input_output_aliases=aliases,
        scratch_shapes=[
            pltpu.VMEM((count,) + page_shape, jnp.bfloat16),
            pltpu.SemaphoreType.DMA((count,)),
            pltpu.SemaphoreType.DMA((count,)),
        ],
        compiler_params=pltpu.CompilerParams(vmem_limit_bytes=VMEM_LIMIT),
        name="place_pages",
    )(*args)
    return result[0], result[1:3], result[3] if finish else None


def rows_kernel(
    late,
    units_ref,
    turn_ref,
    order_ref,
    ids_ref,
    lengths_ref,
    rows_ref,
    cosine_ref,
    sine_ref,
    pages_ref,
    passed_ref,
    queries_ref,
    fresh_ref,
    part_ref,
    stage,
    load_sem,
):
    device = lax.axis_index("tp")
    devices, _, width = rows_ref.shape
    pieces = (GROUP + 2) * HD // width
    half_dim = HD // 2
    row = lax.broadcasted_iota(jnp.int32, rows_ref.shape[1:], 0)
    lane = lax.broadcasted_iota(jnp.int32, (QROWS, HD), 1)

    def unit_rows(unit):
        request, head = unit // KVH, unit % KVH
        found = []
        for piece in range(pieces):
            place = turn_ref[(head * pieces + piece) ^ device]
            block = rows_ref[place].astype(jnp.float32)
            picked = [
                jnp.sum(jnp.where(row == 2 * request + j, block, 0.0), axis=0, keepdims=True)
                for j in range(2)
            ]
            for at in range(0, width, HD):
                found.append([line[:, at : at + HD] for line in picked])
        turned = []
        for j in range(2):
            heads = jnp.concatenate([head[j] for head in found[: GROUP + 1]], axis=0)
            swapped = jnp.concatenate([heads[:, half_dim:], heads[:, :half_dim]], axis=1)
            cosine = cosine_ref[pl.ds(2 * request + j, 1), :]
            sine = sine_ref[pl.ds(2 * request + j, 1), :]
            heads = heads * cosine + swapped * sine
            turned.append(heads.astype(jnp.bfloat16).astype(jnp.float32))
        return turned, [found[GROUP + 1][j] for j in range(2)]

    loads = []
    for slot, (source, at) in enumerate(late):
        page = pages_ref.at[order_ref[at]] if source == 0 else passed_ref.at[at]
        copy = pltpu.make_async_copy(page, stage.at[slot], load_sem.at[slot])
        copy.start()
        loads.append(copy)
    sums = jnp.zeros((QROWS, HD), jnp.float32)
    for slot in range(len(late)):
        page = ids_ref[slot]
        unit = page // PER_UNIT
        limit = lengths_ref[unit // KVH] - (page % PER_UNIT) * PAGE
        turned, _ = unit_rows(unit)
        query = jnp.concatenate([turned[0][:GROUP], turned[1][:GROUP]], axis=0)
        loads[slot].wait()
        weighted, total = attend(
            query.astype(jnp.bfloat16), stage[slot, :, :HD], stage[slot, :, HD:], limit
        )
        part_ref[slot * QROWS : (slot + 1) * QROWS, :] = weighted.astype(jnp.bfloat16)
        high = total.astype(jnp.bfloat16).astype(jnp.float32)
        sums = jnp.where(lane == 2 * slot, high, sums)
        sums = jnp.where(lane == 2 * slot + 1, total - high, sums)
    part_ref[len(late) * QROWS :, :] = sums.astype(jnp.bfloat16)
    for slot in range(U_DEV):
        turned, values = unit_rows(units_ref[slot])
        for j in range(2):
            at = 2 * slot + j
            queries_ref[slot, j * GROUP : (j + 1) * GROUP, :] = turned[j][:GROUP]
            fresh_ref[at : at + 1, :HD] = turned[j][GROUP:]
            fresh_ref[at : at + 1, HD:] = values[j]


def rows_and_parts(units, turn, order, ids, lengths, rows, cosine, sine, pages, passed, late):
    return pl.pallas_call(
        functools.partial(rows_kernel, late),
        out_shape=(
            jax.ShapeDtypeStruct((U_DEV, QROWS, HD), jnp.float32),
            jax.ShapeDtypeStruct((2 * U_DEV, 2 * HD), jnp.float32),
            jax.ShapeDtypeStruct(((len(late) + 1) * QROWS, HD), jnp.bfloat16),
        ),
        in_specs=[smem_spec()] * 5 + [vmem_spec()] * 3 + [any_spec()] * 2,
        out_specs=(vmem_spec(),) * 3,
        scratch_shapes=[
            pltpu.VMEM((len(late),) + pages.shape[1:], pages.dtype),
            pltpu.SemaphoreType.DMA((len(late),)),
        ],
        compiler_params=pltpu.CompilerParams(vmem_limit_bytes=VMEM_LIMIT),
        name="rows_and_parts",
    )(units, turn, order, ids, lengths, rows, cosine, sine, pages, passed)


def swap(values, key, devices):
    return lax.ppermute(values, "tp", [(i, i ^ key) for i in range(devices)])


def gather_line(values, devices):
    values = values[None]
    step = devices // 2
    keys = [step // 2, step, step + step // 2]
    found = [swap(values, k, devices) for k in keys]
    return jnp.concatenate([values] + found, axis=0), [0] + keys


def gather_more(values, span, step, devices):
    values = jnp.concatenate([values, swap(values, step, devices)], axis=0)
    return values, span + [s ^ step for s in span]


def after(value, *others):
    return lax.optimization_barrier((value,) + others)[0]


def body(hidden_states, qkv_weight, out_weight, cache_pages, context_lengths, new_units, old_pages):
    devices = lax.axis_size("tp")
    device = lax.axis_index("tp")
    requests = hidden_states.shape[0]
    pages_dev, page_rows, page_width = cache_pages.shape
    capacity = max(1, pages_dev // devices)
    total_units = new_units.shape[0]
    total_pages = old_pages.shape[0]
    pairwise = devices == 2 * KVH

    def own(*keys):
        return [(0, key, r) for key in keys for r in range(capacity)]

    def passed(source, piece):
        return [(source, 0, piece * capacity + r) for r in range(capacity)]

    def piece(chunk, n):
        return chunk[n * capacity : (n + 1) * capacity]

    def send(chunk, key):
        return swap(chunk, key, devices)

    if pairwise:
        half, quarter = devices // 2, devices // 4
        a, b = half, half + quarter
        c, d = a + 2, b + 2
        near = list(range(2, half, 2))
        (chunk_a, cross_near), order = first_pack(
            new_units,
            old_pages,
            cache_pages,
            devices,
            capacity,
            [own(a), own(1, *[k + 1 for k in near])],
            True,
        )
        moved_a, cross_near = send(chunk_a, a), send(cross_near, 1)
        chunk_4, chunk_6, chunk_b, cross_far = next_pack(
            order,
            [cache_pages, cross_near],
            capacity,
            [
                own(near[1]) + passed(1, 2),
                own(near[2]) + passed(1, 3),
                own(b),
                own(a + 1, b + 1, c + 1, d + 1),
            ],
        )
        moved_b, cross_far = send(chunk_b, b), send(cross_far, 1)
    else:
        (packed,), order = first_pack(
            new_units, old_pages, cache_pages, devices, capacity, [own(*range(devices))], False
        )
        arrived = lax.all_to_all(
            packed.reshape(devices, capacity, page_rows, page_width),
            "tp",
            split_axis=0,
            concat_axis=0,
            tiled=True,
        ).reshape(devices * capacity, page_rows, page_width)

    slot_index = jnp.sum(
        jnp.where(
            new_units[None, :] == jnp.arange(total_units, dtype=jnp.int32)[:, None],
            jnp.arange(total_units, dtype=jnp.int32)[None, :],
            0,
        ),
        axis=1,
    )
    if pairwise:
        ids = old_pages.reshape(devices, 1, pages_dev)
        ids = jnp.concatenate([ids[device], ids[device ^ 1]], axis=0)
        reached = jnp.sum(
            jnp.where(
                (ids // PER_UNIT)[..., None] == new_units, jnp.arange(total_units) // U_DEV, 0
            ),
            axis=-1,
        )
        chosen = reached == (device ^ d)
        earlier = jnp.arange(pages_dev)[None, :] < jnp.arange(pages_dev)[:, None]
        ranks = jnp.sum((chosen[:, None, :] & earlier[None]).astype(jnp.int32), axis=-1)
        wants = jnp.arange(capacity, dtype=jnp.int32)[None, :, None]
        picked = chosen[:, None, :] & (ranks[:, None, :] == wants)
        late_ids = jnp.sum(jnp.where(picked, ids[:, None, :], 0), axis=-1)
        late_ids = late_ids.reshape(2 * capacity).astype(jnp.int32)
    flat_rows = hidden_states.reshape(requests * 2, D)
    if pairwise:
        flat_rows = after(flat_rows, cross_far)
    own_part = lax.dot_general(
        flat_rows, qkv_weight, (((1,), (1,)), ((), ())), preferred_element_type=jnp.float32
    ).astype(jnp.bfloat16)
    if pairwise:
        new_units, old_pages, _ = lax.optimization_barrier((new_units, old_pages, own_part))
    own_units = lax.dynamic_slice_in_dim(new_units, device * U_DEV, U_DEV)
    own_lengths = context_lengths[own_units // KVH]
    wanted = (
        own_units[:, None] * PER_UNIT + jnp.arange(PER_UNIT, dtype=jnp.int32)[None, :]
    ).reshape(pages_dev)
    source_pos = jnp.sum(
        jnp.where(
            wanted[:, None] == old_pages[None, :],
            jnp.arange(total_pages, dtype=jnp.int32)[None, :],
            0,
        ),
        axis=1,
    )
    source_dev = source_pos // pages_dev
    rank = jnp.sum(
        (
            (source_dev[:, None] == source_dev[None, :])
            & (source_pos[None, :] < source_pos[:, None])
        ).astype(jnp.int32),
        axis=1,
    )
    if pairwise:
        where = (source_dev ^ device) * capacity + rank
        spots = jnp.arange(devices * capacity, dtype=jnp.int32)
        slots = jnp.arange(pages_dev, dtype=jnp.int32)
        table = jnp.sum(jnp.where(where[None, :] == spots[:, None], slots[None, :], 0), axis=1)
    else:
        table = source_dev * capacity + rank

    if pairwise:
        positions = context_lengths[:, None] + jnp.arange(2, dtype=jnp.int32)[None, :]
        cosine, sine = rope_tables(positions.reshape(2 * requests))
        rows, span = gather_line(own_part, devices)
        moved_a2 = send(after(piece(cross_far, 0), own_part, moved_a), a)
        moved_4 = send(after(chunk_4, rows), near[1])
        moved_6 = send(after(chunk_6, rows), near[2])
        moved_b2 = send(after(piece(cross_far, 1), own_part), b)
        rows, span = gather_more(after(rows, moved_a, moved_b), span, 2, devices)
        rows, span = gather_more(rows, span, 1, devices)
        turn = jnp.array([span.index(i) for i in range(devices)], jnp.int32)
        late = [(0, d * capacity + r) for r in range(capacity)]
        late += [(1, 3 * capacity + r) for r in range(capacity)]
        places = [key * capacity + r for key in (d, d + 1) for r in range(capacity)]
        queries, fresh, sent = rows_and_parts(
            own_units,
            turn,
            order,
            late_ids,
            context_lengths,
            rows,
            cosine,
            sine,
            cache_pages,
            cross_far,
            late,
        )
        parts = [send(sent, d)]
        chunk_c, chunk_d, chunk_2 = next_pack(
            order,
            [cache_pages, after(cross_far, rows), cross_near],
            capacity,
            [own(c) + passed(1, 2), own(d), own(near[0]) + passed(2, 1)],
        )
        moved_2 = send(after(chunk_2, sent), near[0])
        moved_c = send(after(chunk_c, sent, moved_a2), c)

        def place(groups, sums, cache, attends, parts, finish):
            entries, sources = [], []
            for array, keys, first in groups:
                for n, key in enumerate(keys):
                    for r in range(capacity):
                        at = (r,) if array is cache_pages else first + n * capacity + r
                        entries.append((len(sources), at, (key * capacity + r,)))
                sources.append(array)
            return place_pages(
                table,
                order,
                own_lengths,
                fresh,
                queries if attends else None,
                sums,
                parts,
                places if parts else [],
                sources,
                entries,
                cache,
                finish,
            )

        new_cache, sums, _ = place(
            [(cache_pages, [0], 0), (cross_near, [1], 0), (moved_a, [a], 0), (moved_b, [b], 0)],
            None,
            None,
            True,
            [],
            False,
        )
        moved_d = send(after(chunk_d, moved_b2, sums[0], parts[0]), d)
        new_cache, sums, _ = place(
            [(moved_a2, [a + 1], 0), (moved_b2, [b + 1], 0), (moved_2, [near[0], near[0] + 1], 0)],
            sums,
            new_cache,
            True,
            [],
            False,
        )
        new_cache, sums, _ = place(
            [(moved_4, [near[1], near[1] + 1], 0), (moved_6, [near[2], near[2] + 1], 0)],
            sums,
            new_cache,
            True,
            [],
            False,
        )
        new_cache, sums, attended = place(
            [(moved_c, [c, c + 1], 0)], sums, new_cache, True, parts, True
        )
        attended = after(attended, moved_d)
        moved_d2 = send(after(piece(cross_far, 3), attended), d)
        new_cache, _, _ = place(
            [(moved_d, [d], 0), (moved_d2, [d + 1], 0)], None, new_cache, False, [], False
        )
    else:
        own_requests, own_heads = own_units // KVH, own_units % KVH
        positions = own_lengths[:, None] + jnp.arange(2, dtype=jnp.int32)[None, :]
        cosine, sine = rope_tables(positions.reshape(2 * U_DEV))
        rows = lax.all_gather(own_part, "tp", axis=1, tiled=True)
        rows = rows.reshape(requests, 2, KVH, GROUP + 2, HD)
        rows = rows[own_requests, :, own_heads].astype(jnp.float32)
        turned = rotate(
            rows[:, :, : GROUP + 1],
            cosine.reshape(U_DEV, 2, 1, HD),
            sine.reshape(U_DEV, 2, 1, HD),
        )
        queries = turned[:, :, :GROUP].reshape(U_DEV, QROWS, HD)
        fresh = jnp.concatenate([turned[:, :, GROUP], rows[:, :, GROUP + 1]], axis=-1)
        fresh = fresh.reshape(2 * U_DEV, 2 * HD).astype(jnp.bfloat16).astype(jnp.float32)
        queries = queries.astype(jnp.bfloat16).astype(jnp.float32)
        entries = [(0, (w,), w) for w in range(pages_dev)]
        new_cache, sums, attended = place_pages(
            table,
            table,
            own_lengths,
            fresh,
            queries,
            None,
            [],
            [],
            [arrived],
            entries,
            None,
            True,
        )

    attended = attended.reshape(U_DEV, 2, GROUP * HD)
    if pairwise:
        heads, span = gather_line(attended, devices)
        heads, span = gather_more(heads, span, 2, devices)
        heads, span = gather_more(heads, span, 1, devices)
        holder = turn[(slot_index // U_DEV) ^ device]
        heads = heads.reshape(total_units, 2, GROUP * HD)[holder * U_DEV + slot_index % U_DEV]
    else:
        heads = lax.all_gather(attended, "tp", axis=0, tiled=True)[slot_index]
    logical = (
        heads.reshape(requests, KVH, 2, GROUP * HD)
        .transpose(0, 2, 1, 3)
        .reshape(requests * 2, HEADS * HD)
    )
    if pairwise:
        logical = after(logical, moved_d2)
    mixed_rows = lax.dot_general(
        logical, out_weight, (((1,), (1,)), ((), ())), preferred_element_type=jnp.float32
    )
    mixed_rows = mixed_rows.astype(jnp.bfloat16).reshape(requests, 2, out_weight.shape[0])
    return (mixed_rows, new_cache)


def solution(mesh):
    in_specs = (
        P("group", None, None),
        P("tp", None),
        P("tp", None),
        P(("group", "tp"), None, None),
        P("group"),
        P("group"),
        P("group"),
    )
    out_specs = (P("group", None, "tp"), P(("group", "tp"), None, None))
    return jax.shard_map(body, mesh=mesh, in_specs=in_specs, out_specs=out_specs, check_vma=False)
```

```python
import functools
import math

import jax
import jax.numpy as jnp
from jax import lax
from jax.experimental import pallas as pl
from jax.experimental.pallas import tpu as pltpu
from jax.sharding import PartitionSpec as P

D = 8192
HEADS = 64
KVH = 8
HD = 128
U_DEV = 4
MAXCTX = 2048
PAGE = 128
GROUP = HEADS // KVH
QROWS = 2 * GROUP
PER_UNIT = MAXCTX // PAGE
VMEM_LIMIT = 56 * 1024 * 1024

rope_base = 10000.0


def rope_tables(positions):
    half_dim = HD // 2
    frequency = rope_base ** (-(jnp.arange(half_dim, dtype=jnp.float32) * 2.0 / HD))
    angles = positions.astype(jnp.float32)[..., None] * frequency
    cosine = jnp.concatenate([jnp.cos(angles), jnp.cos(angles)], axis=-1)
    sine = jnp.concatenate([-jnp.sin(angles), jnp.sin(angles)], axis=-1)
    return cosine, sine


def rotate(values, cosine, sine):
    half_dim = HD // 2
    turned = jnp.concatenate([values[..., half_dim:], values[..., :half_dim]], axis=-1)
    return values * cosine + turned * sine


def any_spec():
    return pl.BlockSpec(memory_space=pl.ANY)


def smem_spec():
    return pl.BlockSpec(memory_space=pltpu.SMEM)


def vmem_spec():
    return pl.BlockSpec(memory_space=pltpu.VMEM)


def load_order(devices, capacity, relative, units_ref, old_ref, order_ref, slots, count):
    device = lax.axis_index("tp")
    total_units = units_ref.shape[0]
    pages_dev = old_ref.shape[0] // devices

    def clear(t, carry):
        count[t] = 0
        return carry

    def empty(t, carry):
        order_ref[t] = 0
        return carry

    def invert(q, carry):
        slots[units_ref[q]] = q
        return carry

    def assign(i, carry):
        unit = old_ref[device * pages_dev + i] // PER_UNIT
        target = slots[unit] // U_DEV
        if relative:
            target = target ^ device
        rank = count[target]
        count[target] = rank + 1
        order_ref[target * capacity + rank] = i
        return carry

    lax.fori_loop(0, devices, clear, 0, unroll=8)
    if devices * capacity > pages_dev:
        lax.fori_loop(0, devices * capacity, empty, 0, unroll=8)
    lax.fori_loop(0, total_units, invert, 0, unroll=8)
    lax.fori_loop(0, pages_dev, assign, 0, unroll=8)


def move_pages(outs_pages, capacity, order_ref, sources, outs, stage, load_sem, store_sem):
    loads, stores = [], []
    for source, key, r in sum(outs_pages, []):
        slot = len(loads)
        index = order_ref[key * capacity + r] if source == 0 else r
        copy = pltpu.make_async_copy(
            sources[source].at[index], stage.at[slot], load_sem.at[slot]
        )
        copy.start()
        loads.append(copy)
    slot = 0
    for n, pages in enumerate(outs_pages):
        count = len(pages)
        for copy in loads[slot : slot + count]:
            copy.wait()
        copy = pltpu.make_async_copy(stage.at[pl.ds(slot, count)], outs[n], store_sem.at[n])
        copy.start()
        stores.append(copy)
        slot += count
    for copy in stores:
        copy.wait()


def first_pack_kernel(
    devices, capacity, outs_pages, relative, units_ref, old_ref, pages_ref, *rest
):
    outs = rest[:-6]
    order_ref, slots, count, stage, load_sem, store_sem = rest[-6:]
    load_order(devices, capacity, relative, units_ref, old_ref, order_ref, slots, count)
    move_pages(
        outs_pages, capacity, order_ref, [pages_ref], outs, stage, load_sem, store_sem
    )


def next_pack_kernel(capacity, outs_pages, sources, order_ref, *rest):
    source_refs, outs = rest[:sources], rest[sources:-3]
    stage, load_sem, store_sem = rest[-3:]
    move_pages(
        outs_pages, capacity, order_ref, source_refs, outs, stage, load_sem, store_sem
    )


def pack_shapes(outs_pages, pages):
    total = sum(len(p) for p in outs_pages)
    shapes = [jax.ShapeDtypeStruct((len(p),) + pages.shape[1:], pages.dtype) for p in outs_pages]
    scratch = [
        pltpu.VMEM((total,) + pages.shape[1:], pages.dtype),
        pltpu.SemaphoreType.DMA((total,)),
        pltpu.SemaphoreType.DMA((len(outs_pages),)),
    ]
    return shapes, scratch


def first_pack(new_units, old_pages, pages, devices, capacity, outs_pages, relative):
    outs, scratch = pack_shapes(outs_pages, pages)
    result = pl.pallas_call(
        functools.partial(first_pack_kernel, devices, capacity, outs_pages, relative),
        out_shape=tuple(outs) + (jax.ShapeDtypeStruct((devices * capacity,), jnp.int32),),
        in_specs=[smem_spec(), smem_spec(), any_spec()],
        out_specs=tuple(any_spec() for _ in outs) + (smem_spec(),),
        scratch_shapes=[
            pltpu.SMEM(new_units.shape, jnp.int32),
            pltpu.SMEM((devices,), jnp.int32),
        ]
        + scratch,
        compiler_params=pltpu.CompilerParams(vmem_limit_bytes=VMEM_LIMIT),
        name="first_pack",
    )(new_units, old_pages, pages)
    return result[:-1], result[-1]


def next_pack(order, sources, capacity, outs_pages):
    outs, scratch = pack_shapes(outs_pages, sources[0])
    return pl.pallas_call(
        functools.partial(next_pack_kernel, capacity, outs_pages, len(sources)),
        out_shape=tuple(outs),
        in_specs=[smem_spec()] + [any_spec()] * len(sources),
        out_specs=tuple(any_spec() for _ in outs),
        scratch_shapes=scratch,
        compiler_params=pltpu.CompilerParams(vmem_limit_bytes=VMEM_LIMIT),
        name="next_pack",
    )(order, *sources)


def attend(query, keys, values, limit):
    scale = 1.0 / math.sqrt(HD)
    scores = (
        lax.dot_general(query, keys, (((1,), (1,)), ((), ())), preferred_element_type=jnp.float32)
        * scale
    )
    lane = lax.broadcasted_iota(jnp.int32, scores.shape, 1)
    weights = jnp.where(lane < limit, jnp.exp(scores), 0.0)
    total = jnp.sum(weights, axis=1, keepdims=True)
    weighted = jnp.dot(weights.astype(jnp.bfloat16), values, preferred_element_type=jnp.float32)
    return weighted, total


ALIGN = 16


def place_kernel(entries, started, attends, finish, late, *refs):
    refs = list(refs)
    table_ref, order_ref, length_ref, fresh_ref = refs[:4]
    refs = refs[4:]
    if attends:
        queries_ref = refs.pop(0)
        if started:
            weighted_in, total_in = refs.pop(0), refs.pop(0)
        part_ref = refs.pop(0) if late else None
    sources = 1 + max(source for source, _, _ in entries)
    source_refs, refs = refs[:sources], refs[sources:]
    if started:
        refs.pop(0)
    out_ref = refs.pop(0)
    if attends:
        weighted_ref, total_ref = refs.pop(0), refs.pop(0)
    attended_ref = refs.pop(0) if finish else None
    stage, load_sem, store_sem = refs
    if attends and started:
        weighted_ref[...] = weighted_in[...]
        total_ref[...] = total_in[...]
    loads = []
    for n, (source, index, _) in enumerate(entries):
        index = order_ref[index[0]] if isinstance(index, tuple) else index
        copy = pltpu.make_async_copy(
            source_refs[source].at[index], stage.at[n], load_sem.at[n]
        )
        copy.start()
        loads.append(copy)
    row = lax.broadcasted_iota(jnp.int32, (ALIGN, 2 * HD), 0)
    stores = []
    for n, (_, _, key) in enumerate(entries):
        w = table_ref[key[0]] if isinstance(key, tuple) else key
        unit, part = w // PER_UNIT, w % PER_UNIT
        length = length_ref[unit]
        loads[n].wait()
        for j in range(2):
            position = length + j

            @pl.when(position // PAGE == part)
            def _():
                inside = position % PAGE
                rows = pl.ds(pl.multiple_of(inside // ALIGN * ALIGN, ALIGN), ALIGN)
                block = stage[n, rows, :].astype(jnp.float32)
                token = fresh_ref[pl.ds(2 * unit + j, 1), :]
                block = jnp.where(row == inside % ALIGN, token, block)
                stage[n, rows, :] = block.astype(jnp.bfloat16)

        copy = pltpu.make_async_copy(stage.at[n], out_ref.at[w], store_sem.at[n])
        copy.start()
        stores.append(copy)
    if attends and not started:
        own_terms(queries_ref, fresh_ref, weighted_ref, total_ref)
    lane = lax.broadcasted_iota(jnp.int32, (QROWS, HD), 1)
    if late:
        sums = part_ref[len(late) * QROWS :, :].astype(jnp.float32)
    for n, at in enumerate(late):
        unit = table_ref[at] // PER_UNIT
        mine = (lane == 2 * n) | (lane == 2 * n + 1)
        total = jnp.sum(jnp.where(mine, sums, 0.0), axis=1, keepdims=True)
        weighted_ref[unit] += part_ref[n * QROWS : (n + 1) * QROWS, :].astype(jnp.float32)
        total_ref[unit] += jnp.broadcast_to(total, (QROWS, HD))
    group = 4
    for first in range(0, len(entries) if attends else 0, group):
        found = []
        for n in range(first, min(first + group, len(entries))):
            key = entries[n][2]
            w = table_ref[key[0]] if isinstance(key, tuple) else key
            unit, part = w // PER_UNIT, w % PER_UNIT
            weighted, total = attend(
                queries_ref[unit].astype(jnp.bfloat16),
                stage[n, :, :HD],
                stage[n, :, HD:],
                length_ref[unit] - part * PAGE,
            )
            found.append((unit, weighted, total))
        for unit, weighted, total in found:
            weighted_ref[unit] += weighted
            total_ref[unit] += jnp.broadcast_to(total, (QROWS, HD))
    if finish:
        attended_ref[...] = (weighted_ref[...] / total_ref[...]).astype(jnp.bfloat16)
    for copy in stores:
        copy.wait()


def own_terms(queries_ref, fresh_ref, weighted_ref, total_ref):
    scale = 1.0 / math.sqrt(HD)
    row = lax.broadcasted_iota(jnp.int32, (QROWS, 1), 0)
    for unit in range(U_DEV):
        query = queries_ref[unit]
        weighted = jnp.zeros((QROWS, HD), jnp.float32)
        total = jnp.zeros((QROWS, 1), jnp.float32)
        for j in range(2):
            at = 2 * unit + j
            key = fresh_ref[at : at + 1, :HD]
            value = fresh_ref[at : at + 1, HD:]
            score = jnp.sum(query * key, axis=1, keepdims=True) * scale
            weight = jnp.where(row >= j * GROUP, jnp.exp(score), 0.0)
            total = total + weight
            weighted = weighted + weight.astype(jnp.bfloat16).astype(jnp.float32) * value
        weighted_ref[unit] = weighted
        total_ref[unit] = jnp.broadcast_to(total, (QROWS, HD))


def place_pages(
    table, order, lengths, fresh, queries, sums, parts, late, sources, entries, cache, finish
):
    started, attends = cache is not None, queries is not None
    page_shape = sources[0].shape[1:]
    pages_dev = U_DEV * PER_UNIT
    args = [table, order, lengths, fresh]
    specs = [smem_spec()] * 3 + [vmem_spec()]
    if attends:
        vmem_args = [queries] + (list(sums) if started else []) + list(parts)
        args += vmem_args
        specs += [vmem_spec()] * len(vmem_args)
    args += list(sources)
    specs += [any_spec()] * len(sources)
    aliases = {}
    if started:
        aliases = {len(args): 0}
        args.append(cache)
        specs.append(any_spec())
    outs = [jax.ShapeDtypeStruct((pages_dev,) + page_shape, jnp.bfloat16)]
    out_specs = [any_spec()]
    if attends:
        outs += [jax.ShapeDtypeStruct((U_DEV, QROWS, HD), jnp.float32)] * 2
        out_specs += [vmem_spec()] * 2
    if finish:
        outs.append(jax.ShapeDtypeStruct((U_DEV, QROWS, HD), jnp.bfloat16))
        out_specs.append(vmem_spec())
    count = len(entries)
    result = pl.pallas_call(
        functools.partial(place_kernel, entries, started, attends, finish, late),
        out_shape=tuple(outs),
        in_specs=specs,
        out_specs=tuple(out_specs),
        input_output_aliases=aliases,
        scratch_shapes=[
            pltpu.VMEM((count,) + page_shape, jnp.bfloat16),
            pltpu.SemaphoreType.DMA((count,)),
            pltpu.SemaphoreType.DMA((count,)),
        ],
        compiler_params=pltpu.CompilerParams(vmem_limit_bytes=VMEM_LIMIT),
        name="place_pages",
    )(*args)
    return result[0], result[1:3], result[3] if finish else None


def rows_kernel(
    late,
    units_ref,
    turn_ref,
    order_ref,
    ids_ref,
    lengths_ref,
    rows_ref,
    cosine_ref,
    sine_ref,
    pages_ref,
    passed_ref,
    queries_ref,
    fresh_ref,
    part_ref,
    stage,
    load_sem,
):
    device = lax.axis_index("tp")
    devices, _, width = rows_ref.shape
    pieces = (GROUP + 2) * HD // width
    half_dim = HD // 2
    row = lax.broadcasted_iota(jnp.int32, rows_ref.shape[1:], 0)
    lane = lax.broadcasted_iota(jnp.int32, (QROWS, HD), 1)

    def unit_rows(unit):
        request, head = unit // KVH, unit % KVH
        found = []
        for piece in range(pieces):
            place = turn_ref[(head * pieces + piece) ^ device]
            block = rows_ref[place].astype(jnp.float32)
            picked = [
                jnp.sum(jnp.where(row == 2 * request + j, block, 0.0), axis=0, keepdims=True)
                for j in range(2)
            ]
            for at in range(0, width, HD):
                found.append([line[:, at : at + HD] for line in picked])
        turned = []
        for j in range(2):
            heads = jnp.concatenate([head[j] for head in found[: GROUP + 1]], axis=0)
            swapped = jnp.concatenate([heads[:, half_dim:], heads[:, :half_dim]], axis=1)
            cosine = cosine_ref[pl.ds(2 * request + j, 1), :]
            sine = sine_ref[pl.ds(2 * request + j, 1), :]
            heads = heads * cosine + swapped * sine
            turned.append(heads.astype(jnp.bfloat16).astype(jnp.float32))
        return turned, [found[GROUP + 1][j] for j in range(2)]

    loads = []
    for slot, (source, at) in enumerate(late):
        page = pages_ref.at[order_ref[at]] if source == 0 else passed_ref.at[at]
        copy = pltpu.make_async_copy(page, stage.at[slot], load_sem.at[slot])
        copy.start()
        loads.append(copy)
    sums = jnp.zeros((QROWS, HD), jnp.float32)
    for slot in range(len(late)):
        page = ids_ref[slot]
        unit = page // PER_UNIT
        limit = lengths_ref[unit // KVH] - (page % PER_UNIT) * PAGE
        turned, _ = unit_rows(unit)
        query = jnp.concatenate([turned[0][:GROUP], turned[1][:GROUP]], axis=0)
        loads[slot].wait()
        weighted, total = attend(
            query.astype(jnp.bfloat16), stage[slot, :, :HD], stage[slot, :, HD:], limit
        )
        part_ref[slot * QROWS : (slot + 1) * QROWS, :] = weighted.astype(jnp.bfloat16)
        high = total.astype(jnp.bfloat16).astype(jnp.float32)
        sums = jnp.where(lane == 2 * slot, high, sums)
        sums = jnp.where(lane == 2 * slot + 1, total - high, sums)
    part_ref[len(late) * QROWS :, :] = sums.astype(jnp.bfloat16)
    for slot in range(U_DEV):
        turned, values = unit_rows(units_ref[slot])
        for j in range(2):
            at = 2 * slot + j
            queries_ref[slot, j * GROUP : (j + 1) * GROUP, :] = turned[j][:GROUP]
            fresh_ref[at : at + 1, :HD] = turned[j][GROUP:]
            fresh_ref[at : at + 1, HD:] = values[j]


def rows_and_parts(units, turn, order, ids, lengths, rows, cosine, sine, pages, passed, late):
    return pl.pallas_call(
        functools.partial(rows_kernel, late),
        out_shape=(
            jax.ShapeDtypeStruct((U_DEV, QROWS, HD), jnp.float32),
            jax.ShapeDtypeStruct((2 * U_DEV, 2 * HD), jnp.float32),
            jax.ShapeDtypeStruct(((len(late) + 1) * QROWS, HD), jnp.bfloat16),
        ),
        in_specs=[smem_spec()] * 5 + [vmem_spec()] * 3 + [any_spec()] * 2,
        out_specs=(vmem_spec(),) * 3,
        scratch_shapes=[
            pltpu.VMEM((len(late),) + pages.shape[1:], pages.dtype),
            pltpu.SemaphoreType.DMA((len(late),)),
        ],
        compiler_params=pltpu.CompilerParams(vmem_limit_bytes=VMEM_LIMIT),
        name="rows_and_parts",
    )(units, turn, order, ids, lengths, rows, cosine, sine, pages, passed)


def swap(values, key, devices):
    return lax.ppermute(values, "tp", [(i, i ^ key) for i in range(devices)])


def gather_line(values, devices):
    values = values[None]
    step = devices // 2
    keys = [step // 2, step, step + step // 2]
    found = [swap(values, k, devices) for k in keys]
    return jnp.concatenate([values] + found, axis=0), [0] + keys


def gather_more(values, span, step, devices):
    values = jnp.concatenate([values, swap(values, step, devices)], axis=0)
    return values, span + [s ^ step for s in span]


def after(value, *others):
    return lax.optimization_barrier((value,) + others)[0]


def body(hidden_states, qkv_weight, out_weight, cache_pages, context_lengths, new_units, old_pages):
    devices = lax.axis_size("tp")
    device = lax.axis_index("tp")
    requests = hidden_states.shape[0]
    pages_dev, page_rows, page_width = cache_pages.shape
    capacity = max(1, pages_dev // devices)
    total_units = new_units.shape[0]
    total_pages = old_pages.shape[0]
    pairwise = devices == 2 * KVH

    def own(*keys):
        return [(0, key, r) for key in keys for r in range(capacity)]

    def passed(source, piece):
        return [(source, 0, piece * capacity + r) for r in range(capacity)]

    def piece(chunk, n):
        return chunk[n * capacity : (n + 1) * capacity]

    def send(chunk, key):
        return swap(chunk, key, devices)

    if pairwise:
        half, quarter = devices // 2, devices // 4
        a, b = half, half + quarter
        c, d, b = a + 2, b, b + 2
        near = list(range(2, half, 2))
        (chunk_a, cross_near), order = first_pack(
            new_units,
            old_pages,
            cache_pages,
            devices,
            capacity,
            [own(a), own(1, *[k + 1 for k in near])],
            True,
        )
        moved_a, cross_near = send(chunk_a, a), send(cross_near, 1)
        chunk_4, chunk_6, chunk_b, cross_far = next_pack(
            order,
            [cache_pages, cross_near],
            capacity,
            [
                own(near[1]) + passed(1, 2),
                own(near[2]) + passed(1, 3),
                own(b),
                own(a + 1, b + 1, c + 1, d + 1),
            ],
        )
        moved_4, moved_6 = send(chunk_4, near[1]), send(chunk_6, near[2])
        moved_b, cross_far = send(chunk_b, b), send(cross_far, 1)
    else:
        (packed,), order = first_pack(
            new_units, old_pages, cache_pages, devices, capacity, [own(*range(devices))], False
        )
        arrived = lax.all_to_all(
            packed.reshape(devices, capacity, page_rows, page_width),
            "tp",
            split_axis=0,
            concat_axis=0,
            tiled=True,
        ).reshape(devices * capacity, page_rows, page_width)

    own_units = lax.dynamic_slice_in_dim(new_units, device * U_DEV, U_DEV)
    own_lengths = context_lengths[own_units // KVH]
    wanted = (
        own_units[:, None] * PER_UNIT + jnp.arange(PER_UNIT, dtype=jnp.int32)[None, :]
    ).reshape(pages_dev)
    source_pos = jnp.sum(
        jnp.where(
            wanted[:, None] == old_pages[None, :],
            jnp.arange(total_pages, dtype=jnp.int32)[None, :],
            0,
        ),
        axis=1,
    )
    source_dev = source_pos // pages_dev
    rank = jnp.sum(
        (
            (source_dev[:, None] == source_dev[None, :])
            & (source_pos[None, :] < source_pos[:, None])
        ).astype(jnp.int32),
        axis=1,
    )
    if pairwise:
        where = (source_dev ^ device) * capacity + rank
        spots = jnp.arange(devices * capacity, dtype=jnp.int32)
        slots = jnp.arange(pages_dev, dtype=jnp.int32)
        table = jnp.sum(jnp.where(where[None, :] == spots[:, None], slots[None, :], 0), axis=1)
    else:
        table = source_dev * capacity + rank

    slot_index = jnp.sum(
        jnp.where(
            new_units[None, :] == jnp.arange(total_units, dtype=jnp.int32)[:, None],
            jnp.arange(total_units, dtype=jnp.int32)[None, :],
            0,
        ),
        axis=1,
    )
    if pairwise:
        ids = old_pages.reshape(devices, 1, pages_dev)
        ids = jnp.concatenate([ids[device], ids[device ^ 1]], axis=0)
        reached = jnp.sum(
            jnp.where(
                (ids // PER_UNIT)[..., None] == new_units, jnp.arange(total_units) // U_DEV, 0
            ),
            axis=-1,
        )
        chosen = reached == (device ^ d)
        earlier = jnp.arange(pages_dev)[None, :] < jnp.arange(pages_dev)[:, None]
        ranks = jnp.sum((chosen[:, None, :] & earlier[None]).astype(jnp.int32), axis=-1)
        wants = jnp.arange(capacity, dtype=jnp.int32)[None, :, None]
        picked = chosen[:, None, :] & (ranks[:, None, :] == wants)
        late_ids = jnp.sum(jnp.where(picked, ids[:, None, :], 0), axis=-1)
        late_ids = late_ids.reshape(2 * capacity).astype(jnp.int32)
    flat_rows = hidden_states.reshape(requests * 2, D)
    if pairwise:
        flat_rows = after(flat_rows, cross_far)
    own_part = lax.dot_general(
        flat_rows, qkv_weight, (((1,), (1,)), ((), ())), preferred_element_type=jnp.float32
    ).astype(jnp.bfloat16)
    if pairwise:
        positions = context_lengths[:, None] + jnp.arange(2, dtype=jnp.int32)[None, :]
        cosine, sine = rope_tables(positions.reshape(2 * requests))
        rows, span = gather_line(own_part, devices)
        moved_a2 = send(after(piece(cross_far, 0), own_part, moved_a), a)
        moved_b2 = send(after(piece(cross_far, 1), own_part), b)
        rows, span = gather_more(after(rows, moved_a, moved_b), span, 2, devices)
        rows, span = gather_more(rows, span, 1, devices)
        turn = jnp.array([span.index(i) for i in range(devices)], jnp.int32)
        late = [(0, d * capacity + r) for r in range(capacity)]
        late += [(1, 3 * capacity + r) for r in range(capacity)]
        places = [key * capacity + r for key in (d, d + 1) for r in range(capacity)]
        queries, fresh, sent = rows_and_parts(
            own_units,
            turn,
            order,
            late_ids,
            context_lengths,
            rows,
            cosine,
            sine,
            cache_pages,
            cross_far,
            late,
        )
        parts = [send(sent, d)]
        chunk_c, chunk_d, chunk_2 = next_pack(
            order,
            [cache_pages, after(cross_far, rows), cross_near],
            capacity,
            [own(c) + passed(1, 2), own(d), own(near[0]) + passed(2, 1)],
        )
        moved_2 = send(chunk_2, near[0])
        moved_c = send(after(chunk_c, moved_a2, sent), c)

        def place(groups, sums, cache, attends, parts, finish):
            entries, sources = [], []
            for array, keys, first in groups:
                for n, key in enumerate(keys):
                    for r in range(capacity):
                        at = (r,) if array is cache_pages else first + n * capacity + r
                        entries.append((len(sources), at, (key * capacity + r,)))
                sources.append(array)
            return place_pages(
                table,
                order,
                own_lengths,
                fresh,
                queries if attends else None,
                sums,
                parts,
                places if parts else [],
                sources,
                entries,
                cache,
                finish,
            )

        new_cache, sums, _ = place(
            [(cache_pages, [0], 0), (cross_near, [1], 0), (moved_a, [a], 0), (moved_b, [b], 0)],
            None,
            None,
            True,
            [],
            False,
        )
        new_cache, sums, _ = place(
            [(moved_4, [near[1], near[1] + 1], 0), (moved_6, [near[2], near[2] + 1], 0)],
            sums,
            new_cache,
            True,
            [],
            False,
        )
        new_cache, sums, _ = place(
            [(moved_a2, [a + 1], 0), (moved_b2, [b + 1], 0), (moved_2, [near[0], near[0] + 1], 0)],
            sums,
            new_cache,
            True,
            [],
            False,
        )
        moved_d = send(after(chunk_d, moved_b2, sums[0], parts[0]), d)
        new_cache, sums, attended = place(
            [(moved_c, [c, c + 1], 0)], sums, new_cache, True, parts, True
        )
        attended = after(attended, moved_d)
        moved_d2 = send(after(piece(cross_far, 3), attended), d)
        new_cache, _, _ = place(
            [(moved_d, [d], 0), (moved_d2, [d + 1], 0)], None, new_cache, False, [], False
        )
    else:
        own_requests, own_heads = own_units // KVH, own_units % KVH
        positions = own_lengths[:, None] + jnp.arange(2, dtype=jnp.int32)[None, :]
        cosine, sine = rope_tables(positions.reshape(2 * U_DEV))
        rows = lax.all_gather(own_part, "tp", axis=1, tiled=True)
        rows = rows.reshape(requests, 2, KVH, GROUP + 2, HD)
        rows = rows[own_requests, :, own_heads].astype(jnp.float32)
        turned = rotate(
            rows[:, :, : GROUP + 1],
            cosine.reshape(U_DEV, 2, 1, HD),
            sine.reshape(U_DEV, 2, 1, HD),
        )
        queries = turned[:, :, :GROUP].reshape(U_DEV, QROWS, HD)
        fresh = jnp.concatenate([turned[:, :, GROUP], rows[:, :, GROUP + 1]], axis=-1)
        fresh = fresh.reshape(2 * U_DEV, 2 * HD).astype(jnp.bfloat16).astype(jnp.float32)
        queries = queries.astype(jnp.bfloat16).astype(jnp.float32)
        entries = [(0, (w,), w) for w in range(pages_dev)]
        new_cache, sums, attended = place_pages(
            table,
            table,
            own_lengths,
            fresh,
            queries,
            None,
            [],
            [],
            [arrived],
            entries,
            None,
            True,
        )

    attended = attended.reshape(U_DEV, 2, GROUP * HD)
    if pairwise:
        heads, span = gather_line(attended, devices)
        heads, span = gather_more(heads, span, 2, devices)
        heads, span = gather_more(heads, span, 1, devices)
        holder = turn[(slot_index // U_DEV) ^ device]
        heads = heads.reshape(total_units, 2, GROUP * HD)[holder * U_DEV + slot_index % U_DEV]
    else:
        heads = lax.all_gather(attended, "tp", axis=0, tiled=True)[slot_index]
    logical = (
        heads.reshape(requests, KVH, 2, GROUP * HD)
        .transpose(0, 2, 1, 3)
        .reshape(requests * 2, HEADS * HD)
    )
    if pairwise:
        logical = after(logical, moved_d2)
    mixed_rows = lax.dot_general(
        logical, out_weight, (((1,), (1,)), ((), ())), preferred_element_type=jnp.float32
    )
    mixed_rows = mixed_rows.astype(jnp.bfloat16).reshape(requests, 2, out_weight.shape[0])
    return (mixed_rows, new_cache)


def solution(mesh):
    in_specs = (
        P("group", None, None),
        P("tp", None),
        P("tp", None),
        P(("group", "tp"), None, None),
        P("group"),
        P("group"),
        P("group"),
    )
    out_specs = (P("group", None, "tp"), P(("group", "tp"), None, None))
    return jax.shard_map(body, mesh=mesh, in_specs=in_specs, out_specs=out_specs, check_vma=False)
```

```python
import functools
import math

import jax
import jax.numpy as jnp
from jax import lax
from jax.experimental import pallas as pl
from jax.experimental.pallas import tpu as pltpu
from jax.sharding import PartitionSpec as P

D = 8192
HEADS = 64
KVH = 8
HD = 128
U_DEV = 4
MAXCTX = 2048
PAGE = 128
GROUP = HEADS // KVH
QROWS = 2 * GROUP
PER_UNIT = MAXCTX // PAGE
VMEM_LIMIT = 56 * 1024 * 1024

rope_base = 10000.0


def rope_tables(positions):
    half_dim = HD // 2
    frequency = rope_base ** (-(jnp.arange(half_dim, dtype=jnp.float32) * 2.0 / HD))
    angles = positions.astype(jnp.float32)[..., None] * frequency
    cosine = jnp.concatenate([jnp.cos(angles), jnp.cos(angles)], axis=-1)
    sine = jnp.concatenate([-jnp.sin(angles), jnp.sin(angles)], axis=-1)
    return cosine, sine


def rotate(values, cosine, sine):
    half_dim = HD // 2
    turned = jnp.concatenate([values[..., half_dim:], values[..., :half_dim]], axis=-1)
    return values * cosine + turned * sine


def any_spec():
    return pl.BlockSpec(memory_space=pl.ANY)


def smem_spec():
    return pl.BlockSpec(memory_space=pltpu.SMEM)


def vmem_spec():
    return pl.BlockSpec(memory_space=pltpu.VMEM)


def load_order(devices, capacity, relative, units_ref, old_ref, order_ref, slots, count):
    device = lax.axis_index("tp")
    total_units = units_ref.shape[0]
    pages_dev = old_ref.shape[0] // devices

    def clear(t, carry):
        count[t] = 0
        return carry

    def empty(t, carry):
        order_ref[t] = 0
        return carry

    def invert(q, carry):
        slots[units_ref[q]] = q
        return carry

    def assign(i, carry):
        unit = old_ref[device * pages_dev + i] // PER_UNIT
        target = slots[unit] // U_DEV
        if relative:
            target = target ^ device
        rank = count[target]
        count[target] = rank + 1
        order_ref[target * capacity + rank] = i
        return carry

    lax.fori_loop(0, devices, clear, 0, unroll=8)
    if devices * capacity > pages_dev:
        lax.fori_loop(0, devices * capacity, empty, 0, unroll=8)
    lax.fori_loop(0, total_units, invert, 0, unroll=8)
    lax.fori_loop(0, pages_dev, assign, 0, unroll=8)


def move_pages(outs_pages, capacity, order_ref, sources, outs, stage, load_sem, store_sem):
    loads, stores = [], []
    for source, key, r in sum(outs_pages, []):
        slot = len(loads)
        index = order_ref[key * capacity + r] if source == 0 else r
        copy = pltpu.make_async_copy(
            sources[source].at[index], stage.at[slot], load_sem.at[slot]
        )
        copy.start()
        loads.append(copy)
    slot = 0
    for n, pages in enumerate(outs_pages):
        count = len(pages)
        for copy in loads[slot : slot + count]:
            copy.wait()
        copy = pltpu.make_async_copy(stage.at[pl.ds(slot, count)], outs[n], store_sem.at[n])
        copy.start()
        stores.append(copy)
        slot += count
    for copy in stores:
        copy.wait()


def first_pack_kernel(
    devices, capacity, outs_pages, relative, units_ref, old_ref, pages_ref, *rest
):
    outs = rest[:-6]
    order_ref, slots, count, stage, load_sem, store_sem = rest[-6:]
    load_order(devices, capacity, relative, units_ref, old_ref, order_ref, slots, count)
    move_pages(
        outs_pages, capacity, order_ref, [pages_ref], outs, stage, load_sem, store_sem
    )


def next_pack_kernel(capacity, outs_pages, sources, order_ref, *rest):
    source_refs, outs = rest[:sources], rest[sources:-3]
    stage, load_sem, store_sem = rest[-3:]
    move_pages(
        outs_pages, capacity, order_ref, source_refs, outs, stage, load_sem, store_sem
    )


def pack_shapes(outs_pages, pages):
    total = sum(len(p) for p in outs_pages)
    shapes = [jax.ShapeDtypeStruct((len(p),) + pages.shape[1:], pages.dtype) for p in outs_pages]
    scratch = [
        pltpu.VMEM((total,) + pages.shape[1:], pages.dtype),
        pltpu.SemaphoreType.DMA((total,)),
        pltpu.SemaphoreType.DMA((len(outs_pages),)),
    ]
    return shapes, scratch


def first_pack(new_units, old_pages, pages, devices, capacity, outs_pages, relative):
    outs, scratch = pack_shapes(outs_pages, pages)
    result = pl.pallas_call(
        functools.partial(first_pack_kernel, devices, capacity, outs_pages, relative),
        out_shape=tuple(outs) + (jax.ShapeDtypeStruct((devices * capacity,), jnp.int32),),
        in_specs=[smem_spec(), smem_spec(), any_spec()],
        out_specs=tuple(any_spec() for _ in outs) + (smem_spec(),),
        scratch_shapes=[
            pltpu.SMEM(new_units.shape, jnp.int32),
            pltpu.SMEM((devices,), jnp.int32),
        ]
        + scratch,
        compiler_params=pltpu.CompilerParams(vmem_limit_bytes=VMEM_LIMIT),
        name="first_pack",
    )(new_units, old_pages, pages)
    return result[:-1], result[-1]


def next_pack(order, sources, capacity, outs_pages):
    outs, scratch = pack_shapes(outs_pages, sources[0])
    return pl.pallas_call(
        functools.partial(next_pack_kernel, capacity, outs_pages, len(sources)),
        out_shape=tuple(outs),
        in_specs=[smem_spec()] + [any_spec()] * len(sources),
        out_specs=tuple(any_spec() for _ in outs),
        scratch_shapes=scratch,
        compiler_params=pltpu.CompilerParams(vmem_limit_bytes=VMEM_LIMIT),
        name="next_pack",
    )(order, *sources)


def attend(query, keys, values, limit):
    scale = 1.0 / math.sqrt(HD)
    scores = (
        lax.dot_general(query, keys, (((1,), (1,)), ((), ())), preferred_element_type=jnp.float32)
        * scale
    )
    lane = lax.broadcasted_iota(jnp.int32, scores.shape, 1)
    weights = jnp.where(lane < limit, jnp.exp(scores), 0.0)
    total = jnp.sum(weights, axis=1, keepdims=True)
    weighted = jnp.dot(weights.astype(jnp.bfloat16), values, preferred_element_type=jnp.float32)
    return weighted, total


ALIGN = 16


def place_kernel(entries, started, attends, finish, late, *refs):
    refs = list(refs)
    table_ref, order_ref, length_ref, fresh_ref = refs[:4]
    refs = refs[4:]
    if attends:
        queries_ref = refs.pop(0)
        if started:
            weighted_in, total_in = refs.pop(0), refs.pop(0)
        part_ref = refs.pop(0) if late else None
    sources = 1 + max(source for source, _, _ in entries)
    source_refs, refs = refs[:sources], refs[sources:]
    if started:
        refs.pop(0)
    out_ref = refs.pop(0)
    if attends:
        weighted_ref, total_ref = refs.pop(0), refs.pop(0)
    attended_ref = refs.pop(0) if finish else None
    stage, load_sem, store_sem = refs
    if attends and started:
        weighted_ref[...] = weighted_in[...]
        total_ref[...] = total_in[...]
    loads = []
    for n, (source, index, _) in enumerate(entries):
        index = order_ref[index[0]] if isinstance(index, tuple) else index
        copy = pltpu.make_async_copy(
            source_refs[source].at[index], stage.at[n], load_sem.at[n]
        )
        copy.start()
        loads.append(copy)
    row = lax.broadcasted_iota(jnp.int32, (ALIGN, 2 * HD), 0)
    stores = []
    for n, (_, _, key) in enumerate(entries):
        w = table_ref[key[0]] if isinstance(key, tuple) else key
        unit, part = w // PER_UNIT, w % PER_UNIT
        length = length_ref[unit]
        loads[n].wait()
        for j in range(2):
            position = length + j

            @pl.when(position // PAGE == part)
            def _():
                inside = position % PAGE
                rows = pl.ds(pl.multiple_of(inside // ALIGN * ALIGN, ALIGN), ALIGN)
                block = stage[n, rows, :].astype(jnp.float32)
                token = fresh_ref[pl.ds(2 * unit + j, 1), :]
                block = jnp.where(row == inside % ALIGN, token, block)
                stage[n, rows, :] = block.astype(jnp.bfloat16)

        copy = pltpu.make_async_copy(stage.at[n], out_ref.at[w], store_sem.at[n])
        copy.start()
        stores.append(copy)
    if attends and not started:
        own_terms(queries_ref, fresh_ref, weighted_ref, total_ref)
    lane = lax.broadcasted_iota(jnp.int32, (QROWS, HD), 1)
    if late:
        sums = part_ref[len(late) * QROWS :, :].astype(jnp.float32)
    for n, at in enumerate(late):
        unit = table_ref[at] // PER_UNIT
        mine = (lane == 2 * n) | (lane == 2 * n + 1)
        total = jnp.sum(jnp.where(mine, sums, 0.0), axis=1, keepdims=True)
        weighted_ref[unit] += part_ref[n * QROWS : (n + 1) * QROWS, :].astype(jnp.float32)
        total_ref[unit] += jnp.broadcast_to(total, (QROWS, HD))
    group = 4
    for first in range(0, len(entries) if attends else 0, group):
        found = []
        for n in range(first, min(first + group, len(entries))):
            key = entries[n][2]
            w = table_ref[key[0]] if isinstance(key, tuple) else key
            unit, part = w // PER_UNIT, w % PER_UNIT
            weighted, total = attend(
                queries_ref[unit].astype(jnp.bfloat16),
                stage[n, :, :HD],
                stage[n, :, HD:],
                length_ref[unit] - part * PAGE,
            )
            found.append((unit, weighted, total))
        for unit, weighted, total in found:
            weighted_ref[unit] += weighted
            total_ref[unit] += jnp.broadcast_to(total, (QROWS, HD))
    if finish:
        attended_ref[...] = (weighted_ref[...] / total_ref[...]).astype(jnp.bfloat16)
    for copy in stores:
        copy.wait()


def own_terms(queries_ref, fresh_ref, weighted_ref, total_ref):
    scale = 1.0 / math.sqrt(HD)
    row = lax.broadcasted_iota(jnp.int32, (QROWS, 1), 0)
    for unit in range(U_DEV):
        query = queries_ref[unit]
        weighted = jnp.zeros((QROWS, HD), jnp.float32)
        total = jnp.zeros((QROWS, 1), jnp.float32)
        for j in range(2):
            at = 2 * unit + j
            key = fresh_ref[at : at + 1, :HD]
            value = fresh_ref[at : at + 1, HD:]
            score = jnp.sum(query * key, axis=1, keepdims=True) * scale
            weight = jnp.where(row >= j * GROUP, jnp.exp(score), 0.0)
            total = total + weight
            weighted = weighted + weight.astype(jnp.bfloat16).astype(jnp.float32) * value
        weighted_ref[unit] = weighted
        total_ref[unit] = jnp.broadcast_to(total, (QROWS, HD))


def place_pages(
    table, order, lengths, fresh, queries, sums, parts, late, sources, entries, cache, finish
):
    started, attends = cache is not None, queries is not None
    page_shape = sources[0].shape[1:]
    pages_dev = U_DEV * PER_UNIT
    args = [table, order, lengths, fresh]
    specs = [smem_spec()] * 3 + [vmem_spec()]
    if attends:
        vmem_args = [queries] + (list(sums) if started else []) + list(parts)
        args += vmem_args
        specs += [vmem_spec()] * len(vmem_args)
    args += list(sources)
    specs += [any_spec()] * len(sources)
    aliases = {}
    if started:
        aliases = {len(args): 0}
        args.append(cache)
        specs.append(any_spec())
    outs = [jax.ShapeDtypeStruct((pages_dev,) + page_shape, jnp.bfloat16)]
    out_specs = [any_spec()]
    if attends:
        outs += [jax.ShapeDtypeStruct((U_DEV, QROWS, HD), jnp.float32)] * 2
        out_specs += [vmem_spec()] * 2
    if finish:
        outs.append(jax.ShapeDtypeStruct((U_DEV, QROWS, HD), jnp.bfloat16))
        out_specs.append(vmem_spec())
    count = len(entries)
    result = pl.pallas_call(
        functools.partial(place_kernel, entries, started, attends, finish, late),
        out_shape=tuple(outs),
        in_specs=specs,
        out_specs=tuple(out_specs),
        input_output_aliases=aliases,
        scratch_shapes=[
            pltpu.VMEM((count,) + page_shape, jnp.bfloat16),
            pltpu.SemaphoreType.DMA((count,)),
            pltpu.SemaphoreType.DMA((count,)),
        ],
        compiler_params=pltpu.CompilerParams(vmem_limit_bytes=VMEM_LIMIT),
        name="place_pages",
    )(*args)
    return result[0], result[1:3], result[3] if finish else None


def rows_kernel(
    late,
    units_ref,
    turn_ref,
    order_ref,
    ids_ref,
    lengths_ref,
    rows_ref,
    cosine_ref,
    sine_ref,
    pages_ref,
    passed_ref,
    queries_ref,
    fresh_ref,
    part_ref,
    stage,
    load_sem,
):
    device = lax.axis_index("tp")
    devices, _, width = rows_ref.shape
    pieces = (GROUP + 2) * HD // width
    half_dim = HD // 2
    row = lax.broadcasted_iota(jnp.int32, rows_ref.shape[1:], 0)
    lane = lax.broadcasted_iota(jnp.int32, (QROWS, HD), 1)

    def unit_rows(unit):
        request, head = unit // KVH, unit % KVH
        found = []
        for piece in range(pieces):
            place = turn_ref[(head * pieces + piece) ^ device]
            block = rows_ref[place].astype(jnp.float32)
            picked = [
                jnp.sum(jnp.where(row == 2 * request + j, block, 0.0), axis=0, keepdims=True)
                for j in range(2)
            ]
            for at in range(0, width, HD):
                found.append([line[:, at : at + HD] for line in picked])
        turned = []
        for j in range(2):
            heads = jnp.concatenate([head[j] for head in found[: GROUP + 1]], axis=0)
            swapped = jnp.concatenate([heads[:, half_dim:], heads[:, :half_dim]], axis=1)
            cosine = cosine_ref[pl.ds(2 * request + j, 1), :]
            sine = sine_ref[pl.ds(2 * request + j, 1), :]
            heads = heads * cosine + swapped * sine
            turned.append(heads.astype(jnp.bfloat16).astype(jnp.float32))
        return turned, [found[GROUP + 1][j] for j in range(2)]

    loads = []
    for slot, (source, at) in enumerate(late):
        page = pages_ref.at[order_ref[at]] if source == 0 else passed_ref.at[at]
        copy = pltpu.make_async_copy(page, stage.at[slot], load_sem.at[slot])
        copy.start()
        loads.append(copy)
    sums = jnp.zeros((QROWS, HD), jnp.float32)
    for slot in range(len(late)):
        page = ids_ref[slot]
        unit = page // PER_UNIT
        limit = lengths_ref[unit // KVH] - (page % PER_UNIT) * PAGE
        turned, _ = unit_rows(unit)
        query = jnp.concatenate([turned[0][:GROUP], turned[1][:GROUP]], axis=0)
        loads[slot].wait()
        weighted, total = attend(
            query.astype(jnp.bfloat16), stage[slot, :, :HD], stage[slot, :, HD:], limit
        )
        part_ref[slot * QROWS : (slot + 1) * QROWS, :] = weighted.astype(jnp.bfloat16)
        high = total.astype(jnp.bfloat16).astype(jnp.float32)
        sums = jnp.where(lane == 2 * slot, high, sums)
        sums = jnp.where(lane == 2 * slot + 1, total - high, sums)
    part_ref[len(late) * QROWS :, :] = sums.astype(jnp.bfloat16)
    for slot in range(U_DEV):
        turned, values = unit_rows(units_ref[slot])
        for j in range(2):
            at = 2 * slot + j
            queries_ref[slot, j * GROUP : (j + 1) * GROUP, :] = turned[j][:GROUP]
            fresh_ref[at : at + 1, :HD] = turned[j][GROUP:]
            fresh_ref[at : at + 1, HD:] = values[j]


def rows_and_parts(units, turn, order, ids, lengths, rows, cosine, sine, pages, passed, late):
    return pl.pallas_call(
        functools.partial(rows_kernel, late),
        out_shape=(
            jax.ShapeDtypeStruct((U_DEV, QROWS, HD), jnp.float32),
            jax.ShapeDtypeStruct((2 * U_DEV, 2 * HD), jnp.float32),
            jax.ShapeDtypeStruct(((len(late) + 1) * QROWS, HD), jnp.bfloat16),
        ),
        in_specs=[smem_spec()] * 5 + [vmem_spec()] * 3 + [any_spec()] * 2,
        out_specs=(vmem_spec(),) * 3,
        scratch_shapes=[
            pltpu.VMEM((len(late),) + pages.shape[1:], pages.dtype),
            pltpu.SemaphoreType.DMA((len(late),)),
        ],
        compiler_params=pltpu.CompilerParams(vmem_limit_bytes=VMEM_LIMIT),
        name="rows_and_parts",
    )(units, turn, order, ids, lengths, rows, cosine, sine, pages, passed)


def swap(values, key, devices):
    return lax.ppermute(values, "tp", [(i, i ^ key) for i in range(devices)])


def gather_line(values, devices):
    values = values[None]
    step = devices // 2
    keys = [step // 2, step, step + step // 2]
    found = [swap(values, k, devices) for k in keys]
    return jnp.concatenate([values] + found, axis=0), [0] + keys


def gather_more(values, span, step, devices):
    values = jnp.concatenate([values, swap(values, step, devices)], axis=0)
    return values, span + [s ^ step for s in span]


def after(value, *others):
    return lax.optimization_barrier((value,) + others)[0]


def body(hidden_states, qkv_weight, out_weight, cache_pages, context_lengths, new_units, old_pages):
    devices = lax.axis_size("tp")
    device = lax.axis_index("tp")
    requests = hidden_states.shape[0]
    pages_dev, page_rows, page_width = cache_pages.shape
    capacity = max(1, pages_dev // devices)
    total_units = new_units.shape[0]
    total_pages = old_pages.shape[0]
    pairwise = devices == 2 * KVH

    def own(*keys):
        return [(0, key, r) for key in keys for r in range(capacity)]

    def passed(source, piece):
        return [(source, 0, piece * capacity + r) for r in range(capacity)]

    def piece(chunk, n):
        return chunk[n * capacity : (n + 1) * capacity]

    def send(chunk, key):
        return swap(chunk, key, devices)

    if pairwise:
        half, quarter = devices // 2, devices // 4
        a, b = half, half + quarter
        c, d = a + 2, b + 2
        near = list(range(2, half, 2))
        (chunk_a, cross_near), order = first_pack(
            new_units,
            old_pages,
            cache_pages,
            devices,
            capacity,
            [own(a), own(1, *[k + 1 for k in near])],
            True,
        )
        moved_a, cross_near = send(chunk_a, a), send(cross_near, 1)
        chunk_4, chunk_6, chunk_b, cross_far = next_pack(
            order,
            [cache_pages, cross_near],
            capacity,
            [
                own(near[1]) + passed(1, 2),
                own(near[2]) + passed(1, 3),
                own(b),
                own(a + 1, b + 1, c + 1, d + 1),
            ],
        )
        moved_4, moved_6 = send(chunk_4, near[1]), send(chunk_6, near[2])
        moved_b, cross_far = send(chunk_b, b), send(cross_far, 1)
    else:
        (packed,), order = first_pack(
            new_units, old_pages, cache_pages, devices, capacity, [own(*range(devices))], False
        )
        arrived = lax.all_to_all(
            packed.reshape(devices, capacity, page_rows, page_width),
            "tp",
            split_axis=0,
            concat_axis=0,
            tiled=True,
        ).reshape(devices * capacity, page_rows, page_width)

    own_units = lax.dynamic_slice_in_dim(new_units, device * U_DEV, U_DEV)
    own_lengths = context_lengths[own_units // KVH]
    wanted = (
        own_units[:, None] * PER_UNIT + jnp.arange(PER_UNIT, dtype=jnp.int32)[None, :]
    ).reshape(pages_dev)
    source_pos = jnp.sum(
        jnp.where(
            wanted[:, None] == old_pages[None, :],
            jnp.arange(total_pages, dtype=jnp.int32)[None, :],
            0,
        ),
        axis=1,
    )
    source_dev = source_pos // pages_dev
    rank = jnp.sum(
        (
            (source_dev[:, None] == source_dev[None, :])
            & (source_pos[None, :] < source_pos[:, None])
        ).astype(jnp.int32),
        axis=1,
    )
    if pairwise:
        where = (source_dev ^ device) * capacity + rank
        spots = jnp.arange(devices * capacity, dtype=jnp.int32)
        slots = jnp.arange(pages_dev, dtype=jnp.int32)
        table = jnp.sum(jnp.where(where[None, :] == spots[:, None], slots[None, :], 0), axis=1)
    else:
        table = source_dev * capacity + rank

    slot_index = jnp.sum(
        jnp.where(
            new_units[None, :] == jnp.arange(total_units, dtype=jnp.int32)[:, None],
            jnp.arange(total_units, dtype=jnp.int32)[None, :],
            0,
        ),
        axis=1,
    )
    if pairwise:
        ids = old_pages.reshape(devices, 1, pages_dev)
        ids = jnp.concatenate([ids[device], ids[device ^ 1]], axis=0)
        reached = jnp.sum(
            jnp.where(
                (ids // PER_UNIT)[..., None] == new_units, jnp.arange(total_units) // U_DEV, 0
            ),
            axis=-1,
        )
        chosen = reached == (device ^ d)
        earlier = jnp.arange(pages_dev)[None, :] < jnp.arange(pages_dev)[:, None]
        ranks = jnp.sum((chosen[:, None, :] & earlier[None]).astype(jnp.int32), axis=-1)
        wants = jnp.arange(capacity, dtype=jnp.int32)[None, :, None]
        picked = chosen[:, None, :] & (ranks[:, None, :] == wants)
        late_ids = jnp.sum(jnp.where(picked, ids[:, None, :], 0), axis=-1)
        late_ids = late_ids.reshape(2 * capacity).astype(jnp.int32)
    flat_rows = hidden_states.reshape(requests * 2, D)
    if pairwise:
        flat_rows = after(flat_rows, cross_far)
    own_part = lax.dot_general(
        flat_rows, qkv_weight, (((1,), (1,)), ((), ())), preferred_element_type=jnp.float32
    ).astype(jnp.bfloat16)
    if pairwise:
        positions = context_lengths[:, None] + jnp.arange(2, dtype=jnp.int32)[None, :]
        cosine, sine = rope_tables(positions.reshape(2 * requests))
        rows, span = gather_line(own_part, devices)
        moved_a2 = send(after(piece(cross_far, 0), own_part, moved_a), a)
        moved_b2 = send(after(piece(cross_far, 1), own_part), b)
        rows, span = gather_more(after(rows, moved_a, moved_b), span, 2, devices)
        rows, span = gather_more(rows, span, 1, devices)
        turn = jnp.array([span.index(i) for i in range(devices)], jnp.int32)
        late = [(0, d * capacity + r) for r in range(capacity)]
        late += [(1, 3 * capacity + r) for r in range(capacity)]
        places = [key * capacity + r for key in (d, d + 1) for r in range(capacity)]
        queries, fresh, sent = rows_and_parts(
            own_units,
            turn,
            order,
            late_ids,
            context_lengths,
            rows,
            cosine,
            sine,
            cache_pages,
            cross_far,
            late,
        )
        parts = [send(sent, d)]
        chunk_c, chunk_d, chunk_2 = next_pack(
            order,
            [cache_pages, after(cross_far, rows), cross_near],
            capacity,
            [own(c) + passed(1, 2), own(d), own(near[0]) + passed(2, 1)],
        )
        moved_2 = send(after(chunk_2, sent), near[0])
        moved_c = send(after(chunk_c, moved_a2, sent), c)

        def place(groups, sums, cache, attends, parts, finish):
            entries, sources = [], []
            for array, keys, first in groups:
                for n, key in enumerate(keys):
                    for r in range(capacity):
                        at = (r,) if array is cache_pages else first + n * capacity + r
                        entries.append((len(sources), at, (key * capacity + r,)))
                sources.append(array)
            return place_pages(
                table,
                order,
                own_lengths,
                fresh,
                queries if attends else None,
                sums,
                parts,
                places if parts else [],
                sources,
                entries,
                cache,
                finish,
            )

        new_cache, sums, _ = place(
            [(cache_pages, [0], 0), (cross_near, [1], 0), (moved_a, [a], 0), (moved_b, [b], 0)],
            None,
            None,
            True,
            [],
            False,
        )
        new_cache, sums, _ = place(
            [(moved_4, [near[1], near[1] + 1], 0), (moved_6, [near[2], near[2] + 1], 0)],
            sums,
            new_cache,
            True,
            [],
            False,
        )
        new_cache, sums, _ = place(
            [(moved_a2, [a + 1], 0), (moved_b2, [b + 1], 0), (moved_2, [near[0], near[0] + 1], 0)],
            sums,
            new_cache,
            True,
            [],
            False,
        )
        moved_d = send(after(chunk_d, moved_b2, sums[0], parts[0]), d)
        new_cache, sums, attended = place(
            [(moved_c, [c, c + 1], 0)], sums, new_cache, True, parts, True
        )
        attended = after(attended, moved_d)
        moved_d2 = send(after(piece(cross_far, 3), attended), d)
        new_cache, _, _ = place(
            [(moved_d, [d], 0), (moved_d2, [d + 1], 0)], None, new_cache, False, [], False
        )
    else:
        own_requests, own_heads = own_units // KVH, own_units % KVH
        positions = own_lengths[:, None] + jnp.arange(2, dtype=jnp.int32)[None, :]
        cosine, sine = rope_tables(positions.reshape(2 * U_DEV))
        rows = lax.all_gather(own_part, "tp", axis=1, tiled=True)
        rows = rows.reshape(requests, 2, KVH, GROUP + 2, HD)
        rows = rows[own_requests, :, own_heads].astype(jnp.float32)
        turned = rotate(
            rows[:, :, : GROUP + 1],
            cosine.reshape(U_DEV, 2, 1, HD),
            sine.reshape(U_DEV, 2, 1, HD),
        )
        queries = turned[:, :, :GROUP].reshape(U_DEV, QROWS, HD)
        fresh = jnp.concatenate([turned[:, :, GROUP], rows[:, :, GROUP + 1]], axis=-1)
        fresh = fresh.reshape(2 * U_DEV, 2 * HD).astype(jnp.bfloat16).astype(jnp.float32)
        queries = queries.astype(jnp.bfloat16).astype(jnp.float32)
        entries = [(0, (w,), w) for w in range(pages_dev)]
        new_cache, sums, attended = place_pages(
            table,
            table,
            own_lengths,
            fresh,
            queries,
            None,
            [],
            [],
            [arrived],
            entries,
            None,
            True,
        )

    attended = attended.reshape(U_DEV, 2, GROUP * HD)
    if pairwise:
        heads, span = gather_line(attended, devices)
        heads, span = gather_more(heads, span, 2, devices)
        heads, span = gather_more(heads, span, 1, devices)
        holder = turn[(slot_index // U_DEV) ^ device]
        heads = heads.reshape(total_units, 2, GROUP * HD)[holder * U_DEV + slot_index % U_DEV]
    else:
        heads = lax.all_gather(attended, "tp", axis=0, tiled=True)[slot_index]
    logical = (
        heads.reshape(requests, KVH, 2, GROUP * HD)
        .transpose(0, 2, 1, 3)
        .reshape(requests * 2, HEADS * HD)
    )
    if pairwise:
        logical = after(logical, moved_d2)
    mixed_rows = lax.dot_general(
        logical, out_weight, (((1,), (1,)), ((), ())), preferred_element_type=jnp.float32
    )
    mixed_rows = mixed_rows.astype(jnp.bfloat16).reshape(requests, 2, out_weight.shape[0])
    return (mixed_rows, new_cache)


def solution(mesh):
    in_specs = (
        P("group", None, None),
        P("tp", None),
        P("tp", None),
        P(("group", "tp"), None, None),
        P("group"),
        P("group"),
        P("group"),
    )
    out_specs = (P("group", None, "tp"), P(("group", "tp"), None, None))
    return jax.shard_map(body, mesh=mesh, in_specs=in_specs, out_specs=out_specs, check_vma=False)
```

```python
import functools
import math

import jax
import jax.numpy as jnp
from jax import lax
from jax.experimental import pallas as pl
from jax.experimental.pallas import tpu as pltpu
from jax.sharding import PartitionSpec as P

D = 8192
HEADS = 64
KVH = 8
HD = 128
U_DEV = 4
MAXCTX = 2048
PAGE = 128
GROUP = HEADS // KVH
QROWS = 2 * GROUP
PER_UNIT = MAXCTX // PAGE
VMEM_LIMIT = 56 * 1024 * 1024
PLACE_LIMIT = 16 * 1024 * 1024

rope_base = 10000.0


def rope_tables(positions):
    half_dim = HD // 2
    frequency = rope_base ** (-(jnp.arange(half_dim, dtype=jnp.float32) * 2.0 / HD))
    angles = positions.astype(jnp.float32)[..., None] * frequency
    cosine = jnp.concatenate([jnp.cos(angles), jnp.cos(angles)], axis=-1)
    sine = jnp.concatenate([-jnp.sin(angles), jnp.sin(angles)], axis=-1)
    return cosine, sine


def rotate(values, cosine, sine):
    half_dim = HD // 2
    turned = jnp.concatenate([values[..., half_dim:], values[..., :half_dim]], axis=-1)
    return values * cosine + turned * sine


def any_spec():
    return pl.BlockSpec(memory_space=pl.ANY)


def smem_spec():
    return pl.BlockSpec(memory_space=pltpu.SMEM)


def vmem_spec():
    return pl.BlockSpec(memory_space=pltpu.VMEM)


def load_order(devices, capacity, relative, units_ref, old_ref, order_ref, slots, count):
    device = lax.axis_index("tp")
    total_units = units_ref.shape[0]
    pages_dev = old_ref.shape[0] // devices

    def clear(t, carry):
        count[t] = 0
        return carry

    def empty(t, carry):
        order_ref[t] = 0
        return carry

    def invert(q, carry):
        slots[units_ref[q]] = q
        return carry

    def assign(i, carry):
        unit = old_ref[device * pages_dev + i] // PER_UNIT
        target = slots[unit] // U_DEV
        if relative:
            target = target ^ device
        rank = count[target]
        count[target] = rank + 1
        order_ref[target * capacity + rank] = i
        return carry

    lax.fori_loop(0, devices, clear, 0, unroll=8)
    if devices * capacity > pages_dev:
        lax.fori_loop(0, devices * capacity, empty, 0, unroll=8)
    lax.fori_loop(0, total_units, invert, 0, unroll=8)
    lax.fori_loop(0, pages_dev, assign, 0, unroll=8)


def move_pages(outs_pages, capacity, order_ref, sources, outs, stage, load_sem, store_sem):
    loads, stores = [], []
    for source, key, r in sum(outs_pages, []):
        slot = len(loads)
        index = order_ref[key * capacity + r] if source == 0 else r
        copy = pltpu.make_async_copy(
            sources[source].at[index], stage.at[slot], load_sem.at[slot]
        )
        copy.start()
        loads.append(copy)
    slot = 0
    for n, pages in enumerate(outs_pages):
        count = len(pages)
        for copy in loads[slot : slot + count]:
            copy.wait()
        copy = pltpu.make_async_copy(stage.at[pl.ds(slot, count)], outs[n], store_sem.at[n])
        copy.start()
        stores.append(copy)
        slot += count
    for copy in stores:
        copy.wait()


def first_pack_kernel(
    devices, capacity, outs_pages, relative, units_ref, old_ref, pages_ref, *rest
):
    outs = rest[:-6]
    order_ref, slots, count, stage, load_sem, store_sem = rest[-6:]
    load_order(devices, capacity, relative, units_ref, old_ref, order_ref, slots, count)
    move_pages(
        outs_pages, capacity, order_ref, [pages_ref], outs, stage, load_sem, store_sem
    )


def next_pack_kernel(capacity, outs_pages, sources, order_ref, *rest):
    source_refs, outs = rest[:sources], rest[sources:-3]
    stage, load_sem, store_sem = rest[-3:]
    move_pages(
        outs_pages, capacity, order_ref, source_refs, outs, stage, load_sem, store_sem
    )


def pack_shapes(outs_pages, pages):
    total = sum(len(p) for p in outs_pages)
    shapes = [jax.ShapeDtypeStruct((len(p),) + pages.shape[1:], pages.dtype) for p in outs_pages]
    scratch = [
        pltpu.VMEM((total,) + pages.shape[1:], pages.dtype),
        pltpu.SemaphoreType.DMA((total,)),
        pltpu.SemaphoreType.DMA((len(outs_pages),)),
    ]
    return shapes, scratch


def first_pack(new_units, old_pages, pages, devices, capacity, outs_pages, relative):
    outs, scratch = pack_shapes(outs_pages, pages)
    result = pl.pallas_call(
        functools.partial(first_pack_kernel, devices, capacity, outs_pages, relative),
        out_shape=tuple(outs) + (jax.ShapeDtypeStruct((devices * capacity,), jnp.int32),),
        in_specs=[smem_spec(), smem_spec(), any_spec()],
        out_specs=tuple(any_spec() for _ in outs) + (smem_spec(),),
        scratch_shapes=[
            pltpu.SMEM(new_units.shape, jnp.int32),
            pltpu.SMEM((devices,), jnp.int32),
        ]
        + scratch,
        compiler_params=pltpu.CompilerParams(vmem_limit_bytes=VMEM_LIMIT),
        name="first_pack",
    )(new_units, old_pages, pages)
    return result[:-1], result[-1]


def next_pack(order, sources, capacity, outs_pages):
    outs, scratch = pack_shapes(outs_pages, sources[0])
    return pl.pallas_call(
        functools.partial(next_pack_kernel, capacity, outs_pages, len(sources)),
        out_shape=tuple(outs),
        in_specs=[smem_spec()] + [any_spec()] * len(sources),
        out_specs=tuple(any_spec() for _ in outs),
        scratch_shapes=scratch,
        compiler_params=pltpu.CompilerParams(vmem_limit_bytes=VMEM_LIMIT),
        name="next_pack",
    )(order, *sources)


def attend(query, keys, values, limit):
    scale = 1.0 / math.sqrt(HD)
    scores = (
        lax.dot_general(query, keys, (((1,), (1,)), ((), ())), preferred_element_type=jnp.float32)
        * scale
    )
    lane = lax.broadcasted_iota(jnp.int32, scores.shape, 1)
    weights = jnp.where(lane < limit, jnp.exp(scores), 0.0)
    total = jnp.sum(weights, axis=1, keepdims=True)
    weighted = jnp.dot(weights.astype(jnp.bfloat16), values, preferred_element_type=jnp.float32)
    return weighted, total


ALIGN = 16


def place_kernel(entries, started, attends, finish, late, *refs):
    refs = list(refs)
    table_ref, order_ref, length_ref, fresh_ref = refs[:4]
    refs = refs[4:]
    if attends:
        queries_ref = refs.pop(0)
        if started:
            weighted_in, total_in = refs.pop(0), refs.pop(0)
        part_ref = refs.pop(0) if late else None
    sources = 1 + max(source for source, _, _ in entries)
    source_refs, refs = refs[:sources], refs[sources:]
    if started:
        refs.pop(0)
    out_ref = refs.pop(0)
    if attends:
        weighted_ref, total_ref = refs.pop(0), refs.pop(0)
    attended_ref = refs.pop(0) if finish else None
    stage, load_sem, store_sem = refs
    if attends and started:
        weighted_ref[...] = weighted_in[...]
        total_ref[...] = total_in[...]
    loads = []
    for n, (source, index, _) in enumerate(entries):
        index = order_ref[index[0]] if isinstance(index, tuple) else index
        copy = pltpu.make_async_copy(
            source_refs[source].at[index], stage.at[n], load_sem.at[n]
        )
        copy.start()
        loads.append(copy)
    row = lax.broadcasted_iota(jnp.int32, (ALIGN, 2 * HD), 0)
    stores = []
    for n, (_, _, key) in enumerate(entries):
        w = table_ref[key[0]] if isinstance(key, tuple) else key
        unit, part = w // PER_UNIT, w % PER_UNIT
        length = length_ref[unit]
        loads[n].wait()
        for j in range(2):
            position = length + j

            @pl.when(position // PAGE == part)
            def _():
                inside = position % PAGE
                rows = pl.ds(pl.multiple_of(inside // ALIGN * ALIGN, ALIGN), ALIGN)
                block = stage[n, rows, :].astype(jnp.float32)
                token = fresh_ref[pl.ds(2 * unit + j, 1), :]
                block = jnp.where(row == inside % ALIGN, token, block)
                stage[n, rows, :] = block.astype(jnp.bfloat16)

        copy = pltpu.make_async_copy(stage.at[n], out_ref.at[w], store_sem.at[n])
        copy.start()
        stores.append(copy)
    if attends and not started:
        own_terms(queries_ref, fresh_ref, weighted_ref, total_ref)
    lane = lax.broadcasted_iota(jnp.int32, (QROWS, HD), 1)
    if late:
        sums = part_ref[len(late) * QROWS :, :].astype(jnp.float32)
    for n, at in enumerate(late):
        unit = table_ref[at] // PER_UNIT
        mine = (lane == 2 * n) | (lane == 2 * n + 1)
        total = jnp.sum(jnp.where(mine, sums, 0.0), axis=1, keepdims=True)
        weighted_ref[unit] += part_ref[n * QROWS : (n + 1) * QROWS, :].astype(jnp.float32)
        total_ref[unit] += jnp.broadcast_to(total, (QROWS, HD))
    group = 4
    for first in range(0, len(entries) if attends else 0, group):
        found = []
        for n in range(first, min(first + group, len(entries))):
            key = entries[n][2]
            w = table_ref[key[0]] if isinstance(key, tuple) else key
            unit, part = w // PER_UNIT, w % PER_UNIT
            weighted, total = attend(
                queries_ref[unit].astype(jnp.bfloat16),
                stage[n, :, :HD],
                stage[n, :, HD:],
                length_ref[unit] - part * PAGE,
            )
            found.append((unit, weighted, total))
        for unit, weighted, total in found:
            weighted_ref[unit] += weighted
            total_ref[unit] += jnp.broadcast_to(total, (QROWS, HD))
    if finish:
        attended_ref[...] = (weighted_ref[...] / total_ref[...]).astype(jnp.bfloat16)
    for copy in stores:
        copy.wait()


def own_terms(queries_ref, fresh_ref, weighted_ref, total_ref):
    scale = 1.0 / math.sqrt(HD)
    row = lax.broadcasted_iota(jnp.int32, (QROWS, 1), 0)
    for unit in range(U_DEV):
        query = queries_ref[unit]
        weighted = jnp.zeros((QROWS, HD), jnp.float32)
        total = jnp.zeros((QROWS, 1), jnp.float32)
        for j in range(2):
            at = 2 * unit + j
            key = fresh_ref[at : at + 1, :HD]
            value = fresh_ref[at : at + 1, HD:]
            score = jnp.sum(query * key, axis=1, keepdims=True) * scale
            weight = jnp.where(row >= j * GROUP, jnp.exp(score), 0.0)
            total = total + weight
            weighted = weighted + weight.astype(jnp.bfloat16).astype(jnp.float32) * value
        weighted_ref[unit] = weighted
        total_ref[unit] = jnp.broadcast_to(total, (QROWS, HD))


def place_pages(
    table, order, lengths, fresh, queries, sums, parts, late, sources, entries, cache, finish
):
    started, attends = cache is not None, queries is not None
    page_shape = sources[0].shape[1:]
    pages_dev = U_DEV * PER_UNIT
    args = [table, order, lengths, fresh]
    specs = [smem_spec()] * 3 + [vmem_spec()]
    if attends:
        vmem_args = [queries] + (list(sums) if started else []) + list(parts)
        args += vmem_args
        specs += [vmem_spec()] * len(vmem_args)
    args += list(sources)
    specs += [any_spec()] * len(sources)
    aliases = {}
    if started:
        aliases = {len(args): 0}
        args.append(cache)
        specs.append(any_spec())
    outs = [jax.ShapeDtypeStruct((pages_dev,) + page_shape, jnp.bfloat16)]
    out_specs = [any_spec()]
    if attends:
        outs += [jax.ShapeDtypeStruct((U_DEV, QROWS, HD), jnp.float32)] * 2
        out_specs += [vmem_spec()] * 2
    if finish:
        outs.append(jax.ShapeDtypeStruct((U_DEV, QROWS, HD), jnp.bfloat16))
        out_specs.append(vmem_spec())
    count = len(entries)
    result = pl.pallas_call(
        functools.partial(place_kernel, entries, started, attends, finish, late),
        out_shape=tuple(outs),
        in_specs=specs,
        out_specs=tuple(out_specs),
        input_output_aliases=aliases,
        scratch_shapes=[
            pltpu.VMEM((count,) + page_shape, jnp.bfloat16),
            pltpu.SemaphoreType.DMA((count,)),
            pltpu.SemaphoreType.DMA((count,)),
        ],
        compiler_params=pltpu.CompilerParams(vmem_limit_bytes=PLACE_LIMIT if started else VMEM_LIMIT),
        name="place_pages",
    )(*args)
    return result[0], result[1:3], result[3] if finish else None


def rows_kernel(
    late,
    units_ref,
    turn_ref,
    order_ref,
    ids_ref,
    lengths_ref,
    rows_ref,
    cosine_ref,
    sine_ref,
    pages_ref,
    passed_ref,
    queries_ref,
    fresh_ref,
    part_ref,
    stage,
    load_sem,
):
    device = lax.axis_index("tp")
    devices, _, width = rows_ref.shape
    pieces = (GROUP + 2) * HD // width
    half_dim = HD // 2
    row = lax.broadcasted_iota(jnp.int32, rows_ref.shape[1:], 0)
    lane = lax.broadcasted_iota(jnp.int32, (QROWS, HD), 1)

    def unit_rows(unit):
        request, head = unit // KVH, unit % KVH
        found = []
        for piece in range(pieces):
            place = turn_ref[(head * pieces + piece) ^ device]
            block = rows_ref[place].astype(jnp.float32)
            picked = [
                jnp.sum(jnp.where(row == 2 * request + j, block, 0.0), axis=0, keepdims=True)
                for j in range(2)
            ]
            for at in range(0, width, HD):
                found.append([line[:, at : at + HD] for line in picked])
        turned = []
        for j in range(2):
            heads = jnp.concatenate([head[j] for head in found[: GROUP + 1]], axis=0)
            swapped = jnp.concatenate([heads[:, half_dim:], heads[:, :half_dim]], axis=1)
            cosine = cosine_ref[pl.ds(2 * request + j, 1), :]
            sine = sine_ref[pl.ds(2 * request + j, 1), :]
            heads = heads * cosine + swapped * sine
            turned.append(heads.astype(jnp.bfloat16).astype(jnp.float32))
        return turned, [found[GROUP + 1][j] for j in range(2)]

    loads = []
    for slot, (source, at) in enumerate(late):
        page = pages_ref.at[order_ref[at]] if source == 0 else passed_ref.at[at]
        copy = pltpu.make_async_copy(page, stage.at[slot], load_sem.at[slot])
        copy.start()
        loads.append(copy)
    sums = jnp.zeros((QROWS, HD), jnp.float32)
    for slot in range(len(late)):
        page = ids_ref[slot]
        unit = page // PER_UNIT
        limit = lengths_ref[unit // KVH] - (page % PER_UNIT) * PAGE
        turned, _ = unit_rows(unit)
        query = jnp.concatenate([turned[0][:GROUP], turned[1][:GROUP]], axis=0)
        loads[slot].wait()
        weighted, total = attend(
            query.astype(jnp.bfloat16), stage[slot, :, :HD], stage[slot, :, HD:], limit
        )
        part_ref[slot * QROWS : (slot + 1) * QROWS, :] = weighted.astype(jnp.bfloat16)
        high = total.astype(jnp.bfloat16).astype(jnp.float32)
        sums = jnp.where(lane == 2 * slot, high, sums)
        sums = jnp.where(lane == 2 * slot + 1, total - high, sums)
    part_ref[len(late) * QROWS :, :] = sums.astype(jnp.bfloat16)
    for slot in range(U_DEV):
        turned, values = unit_rows(units_ref[slot])
        for j in range(2):
            at = 2 * slot + j
            queries_ref[slot, j * GROUP : (j + 1) * GROUP, :] = turned[j][:GROUP]
            fresh_ref[at : at + 1, :HD] = turned[j][GROUP:]
            fresh_ref[at : at + 1, HD:] = values[j]


def rows_and_parts(units, turn, order, ids, lengths, rows, cosine, sine, pages, passed, late):
    return pl.pallas_call(
        functools.partial(rows_kernel, late),
        out_shape=(
            jax.ShapeDtypeStruct((U_DEV, QROWS, HD), jnp.float32),
            jax.ShapeDtypeStruct((2 * U_DEV, 2 * HD), jnp.float32),
            jax.ShapeDtypeStruct(((len(late) + 1) * QROWS, HD), jnp.bfloat16),
        ),
        in_specs=[smem_spec()] * 5 + [vmem_spec()] * 3 + [any_spec()] * 2,
        out_specs=(vmem_spec(),) * 3,
        scratch_shapes=[
            pltpu.VMEM((len(late),) + pages.shape[1:], pages.dtype),
            pltpu.SemaphoreType.DMA((len(late),)),
        ],
        compiler_params=pltpu.CompilerParams(vmem_limit_bytes=VMEM_LIMIT),
        name="rows_and_parts",
    )(units, turn, order, ids, lengths, rows, cosine, sine, pages, passed)


def swap(values, key, devices):
    return lax.ppermute(values, "tp", [(i, i ^ key) for i in range(devices)])


def gather_line(values, devices):
    values = values[None]
    step = devices // 2
    keys = [step // 2, step, step + step // 2]
    found = [swap(values, k, devices) for k in keys]
    return jnp.concatenate([values] + found, axis=0), [0] + keys


def gather_more(values, span, step, devices):
    values = jnp.concatenate([values, swap(values, step, devices)], axis=0)
    return values, span + [s ^ step for s in span]


def after(value, *others):
    return lax.optimization_barrier((value,) + others)[0]


def body(hidden_states, qkv_weight, out_weight, cache_pages, context_lengths, new_units, old_pages):
    devices = lax.axis_size("tp")
    device = lax.axis_index("tp")
    requests = hidden_states.shape[0]
    pages_dev, page_rows, page_width = cache_pages.shape
    capacity = max(1, pages_dev // devices)
    total_units = new_units.shape[0]
    total_pages = old_pages.shape[0]
    pairwise = devices == 2 * KVH

    def own(*keys):
        return [(0, key, r) for key in keys for r in range(capacity)]

    def passed(source, piece):
        return [(source, 0, piece * capacity + r) for r in range(capacity)]

    def piece(chunk, n):
        return chunk[n * capacity : (n + 1) * capacity]

    def send(chunk, key):
        return swap(chunk, key, devices)

    if pairwise:
        half, quarter = devices // 2, devices // 4
        a, b = half, half + quarter
        c, d = a + 2, b + 2
        near = list(range(2, half, 2))
        (chunk_a, cross_near), order = first_pack(
            new_units,
            old_pages,
            cache_pages,
            devices,
            capacity,
            [own(a), own(1, *[k + 1 for k in near])],
            True,
        )
        moved_a, cross_near = send(chunk_a, a), send(cross_near, 1)
        chunk_4, chunk_6, chunk_b, cross_far = next_pack(
            order,
            [cache_pages, cross_near],
            capacity,
            [
                own(near[1]) + passed(1, 2),
                own(near[2]) + passed(1, 3),
                own(b),
                own(a + 1, b + 1, c + 1, d + 1),
            ],
        )
        moved_4, moved_6 = send(chunk_4, near[1]), send(chunk_6, near[2])
        moved_b, cross_far = send(chunk_b, b), send(cross_far, 1)
    else:
        (packed,), order = first_pack(
            new_units, old_pages, cache_pages, devices, capacity, [own(*range(devices))], False
        )
        arrived = lax.all_to_all(
            packed.reshape(devices, capacity, page_rows, page_width),
            "tp",
            split_axis=0,
            concat_axis=0,
            tiled=True,
        ).reshape(devices * capacity, page_rows, page_width)

    own_units = lax.dynamic_slice_in_dim(new_units, device * U_DEV, U_DEV)
    own_lengths = context_lengths[own_units // KVH]
    wanted = (
        own_units[:, None] * PER_UNIT + jnp.arange(PER_UNIT, dtype=jnp.int32)[None, :]
    ).reshape(pages_dev)
    source_pos = jnp.sum(
        jnp.where(
            wanted[:, None] == old_pages[None, :],
            jnp.arange(total_pages, dtype=jnp.int32)[None, :],
            0,
        ),
        axis=1,
    )
    source_dev = source_pos // pages_dev
    rank = jnp.sum(
        (
            (source_dev[:, None] == source_dev[None, :])
            & (source_pos[None, :] < source_pos[:, None])
        ).astype(jnp.int32),
        axis=1,
    )
    if pairwise:
        where = (source_dev ^ device) * capacity + rank
        spots = jnp.arange(devices * capacity, dtype=jnp.int32)
        slots = jnp.arange(pages_dev, dtype=jnp.int32)
        table = jnp.sum(jnp.where(where[None, :] == spots[:, None], slots[None, :], 0), axis=1)
    else:
        table = source_dev * capacity + rank

    slot_index = jnp.sum(
        jnp.where(
            new_units[None, :] == jnp.arange(total_units, dtype=jnp.int32)[:, None],
            jnp.arange(total_units, dtype=jnp.int32)[None, :],
            0,
        ),
        axis=1,
    )
    if pairwise:
        ids = old_pages.reshape(devices, 1, pages_dev)
        ids = jnp.concatenate([ids[device], ids[device ^ 1]], axis=0)
        reached = jnp.sum(
            jnp.where(
                (ids // PER_UNIT)[..., None] == new_units, jnp.arange(total_units) // U_DEV, 0
            ),
            axis=-1,
        )
        chosen = reached == (device ^ d)
        earlier = jnp.arange(pages_dev)[None, :] < jnp.arange(pages_dev)[:, None]
        ranks = jnp.sum((chosen[:, None, :] & earlier[None]).astype(jnp.int32), axis=-1)
        wants = jnp.arange(capacity, dtype=jnp.int32)[None, :, None]
        picked = chosen[:, None, :] & (ranks[:, None, :] == wants)
        late_ids = jnp.sum(jnp.where(picked, ids[:, None, :], 0), axis=-1)
        late_ids = late_ids.reshape(2 * capacity).astype(jnp.int32)
    flat_rows = hidden_states.reshape(requests * 2, D)
    if pairwise:
        flat_rows = after(flat_rows, cross_far)
    own_part = lax.dot_general(
        flat_rows, qkv_weight, (((1,), (1,)), ((), ())), preferred_element_type=jnp.float32
    ).astype(jnp.bfloat16)
    if pairwise:
        positions = context_lengths[:, None] + jnp.arange(2, dtype=jnp.int32)[None, :]
        cosine, sine = rope_tables(positions.reshape(2 * requests))
        rows, span = gather_line(own_part, devices)
        moved_a2 = send(after(piece(cross_far, 0), own_part, moved_a), a)
        moved_b2 = send(after(piece(cross_far, 1), own_part), b)
        rows, span = gather_more(after(rows, moved_a, moved_b), span, 2, devices)
        rows, span = gather_more(rows, span, 1, devices)
        turn = jnp.array([span.index(i) for i in range(devices)], jnp.int32)
        late = [(0, d * capacity + r) for r in range(capacity)]
        late += [(1, 3 * capacity + r) for r in range(capacity)]
        places = [key * capacity + r for key in (d, d + 1) for r in range(capacity)]
        queries, fresh, sent = rows_and_parts(
            own_units,
            turn,
            order,
            late_ids,
            context_lengths,
            rows,
            cosine,
            sine,
            cache_pages,
            cross_far,
            late,
        )
        parts = [send(sent, d)]
        chunk_c, chunk_d, chunk_2 = next_pack(
            order,
            [cache_pages, after(cross_far, rows), cross_near],
            capacity,
            [own(c) + passed(1, 2), own(d), own(near[0]) + passed(2, 1)],
        )
        moved_2 = send(chunk_2, near[0])
        moved_c = send(after(chunk_c, moved_a2, sent), c)

        def place(groups, sums, cache, attends, parts, finish):
            entries, sources = [], []
            for array, keys, first in groups:
                for n, key in enumerate(keys):
                    for r in range(capacity):
                        at = (r,) if array is cache_pages else first + n * capacity + r
                        entries.append((len(sources), at, (key * capacity + r,)))
                sources.append(array)
            return place_pages(
                table,
                order,
                own_lengths,
                fresh,
                queries if attends else None,
                sums,
                parts,
                places if parts else [],
                sources,
                entries,
                cache,
                finish,
            )

        new_cache, sums, _ = place(
            [(cache_pages, [0], 0), (cross_near, [1], 0), (moved_a, [a], 0), (moved_b, [b], 0)],
            None,
            None,
            True,
            [],
            False,
        )
        new_cache, sums, _ = place(
            [(moved_4, [near[1], near[1] + 1], 0), (moved_6, [near[2], near[2] + 1], 0)],
            sums,
            new_cache,
            True,
            [],
            False,
        )
        new_cache, sums, _ = place(
            [(moved_a2, [a + 1], 0), (moved_b2, [b + 1], 0), (moved_2, [near[0], near[0] + 1], 0)],
            sums,
            new_cache,
            True,
            [],
            False,
        )
        moved_d = send(after(chunk_d, moved_b2, sums[0], parts[0]), d)
        new_cache, sums, attended = place(
            [(moved_c, [c, c + 1], 0)], sums, new_cache, True, parts, True
        )
        attended = after(attended, moved_d)
        moved_d2 = send(after(piece(cross_far, 3), attended), d)
        new_cache, _, _ = place([(moved_d, [d], 0)], None, new_cache, False, [], False)
        new_cache, _, _ = place([(moved_d2, [d + 1], 0)], None, new_cache, False, [], False)
    else:
        own_requests, own_heads = own_units // KVH, own_units % KVH
        positions = own_lengths[:, None] + jnp.arange(2, dtype=jnp.int32)[None, :]
        cosine, sine = rope_tables(positions.reshape(2 * U_DEV))
        rows = lax.all_gather(own_part, "tp", axis=1, tiled=True)
        rows = rows.reshape(requests, 2, KVH, GROUP + 2, HD)
        rows = rows[own_requests, :, own_heads].astype(jnp.float32)
        turned = rotate(
            rows[:, :, : GROUP + 1],
            cosine.reshape(U_DEV, 2, 1, HD),
            sine.reshape(U_DEV, 2, 1, HD),
        )
        queries = turned[:, :, :GROUP].reshape(U_DEV, QROWS, HD)
        fresh = jnp.concatenate([turned[:, :, GROUP], rows[:, :, GROUP + 1]], axis=-1)
        fresh = fresh.reshape(2 * U_DEV, 2 * HD).astype(jnp.bfloat16).astype(jnp.float32)
        queries = queries.astype(jnp.bfloat16).astype(jnp.float32)
        entries = [(0, (w,), w) for w in range(pages_dev)]
        new_cache, sums, attended = place_pages(
            table,
            table,
            own_lengths,
            fresh,
            queries,
            None,
            [],
            [],
            [arrived],
            entries,
            None,
            True,
        )

    attended = attended.reshape(U_DEV, 2, GROUP * HD)
    if pairwise:
        heads, span = gather_line(attended, devices)
        heads, span = gather_more(heads, span, 2, devices)
        heads, span = gather_more(heads, span, 1, devices)
        holder = turn[(slot_index // U_DEV) ^ device]
        heads = heads.reshape(total_units, 2, GROUP * HD)[holder * U_DEV + slot_index % U_DEV]
    else:
        heads = lax.all_gather(attended, "tp", axis=0, tiled=True)[slot_index]
    logical = (
        heads.reshape(requests, KVH, 2, GROUP * HD)
        .transpose(0, 2, 1, 3)
        .reshape(requests * 2, HEADS * HD)
    )
    mixed_rows = lax.dot_general(
        logical, out_weight, (((1,), (1,)), ((), ())), preferred_element_type=jnp.float32
    )
    mixed_rows = mixed_rows.astype(jnp.bfloat16).reshape(requests, 2, out_weight.shape[0])
    return (mixed_rows, new_cache)


def solution(mesh):
    in_specs = (
        P("group", None, None),
        P("tp", None),
        P("tp", None),
        P(("group", "tp"), None, None),
        P("group"),
        P("group"),
        P("group"),
    )
    out_specs = (P("group", None, "tp"), P(("group", "tp"), None, None))
    return jax.shard_map(body, mesh=mesh, in_specs=in_specs, out_specs=out_specs, check_vma=False)
```

```python
import functools
import math

import jax
import jax.numpy as jnp
from jax import lax
from jax.experimental import pallas as pl
from jax.experimental.pallas import tpu as pltpu
from jax.sharding import PartitionSpec as P

D = 8192
HEADS = 64
KVH = 8
HD = 128
U_DEV = 4
MAXCTX = 2048
PAGE = 128
GROUP = HEADS // KVH
QROWS = 2 * GROUP
PER_UNIT = MAXCTX // PAGE
VMEM_LIMIT = 56 * 1024 * 1024
PLACE_LIMIT = 16 * 1024 * 1024

rope_base = 10000.0


def rope_tables(positions):
    half_dim = HD // 2
    frequency = rope_base ** (-(jnp.arange(half_dim, dtype=jnp.float32) * 2.0 / HD))
    angles = positions.astype(jnp.float32)[..., None] * frequency
    cosine = jnp.concatenate([jnp.cos(angles), jnp.cos(angles)], axis=-1)
    sine = jnp.concatenate([-jnp.sin(angles), jnp.sin(angles)], axis=-1)
    return cosine, sine


def rotate(values, cosine, sine):
    half_dim = HD // 2
    turned = jnp.concatenate([values[..., half_dim:], values[..., :half_dim]], axis=-1)
    return values * cosine + turned * sine


def any_spec():
    return pl.BlockSpec(memory_space=pl.ANY)


def smem_spec():
    return pl.BlockSpec(memory_space=pltpu.SMEM)


def vmem_spec():
    return pl.BlockSpec(memory_space=pltpu.VMEM)


def load_order(devices, capacity, relative, units_ref, old_ref, order_ref, slots, count):
    device = lax.axis_index("tp")
    total_units = units_ref.shape[0]
    pages_dev = old_ref.shape[0] // devices

    def clear(t, carry):
        count[t] = 0
        return carry

    def empty(t, carry):
        order_ref[t] = 0
        return carry

    def invert(q, carry):
        slots[units_ref[q]] = q
        return carry

    def assign(i, carry):
        unit = old_ref[device * pages_dev + i] // PER_UNIT
        target = slots[unit] // U_DEV
        if relative:
            target = target ^ device
        rank = count[target]
        count[target] = rank + 1
        order_ref[target * capacity + rank] = i
        return carry

    lax.fori_loop(0, devices, clear, 0, unroll=8)
    if devices * capacity > pages_dev:
        lax.fori_loop(0, devices * capacity, empty, 0, unroll=8)
    lax.fori_loop(0, total_units, invert, 0, unroll=8)
    lax.fori_loop(0, pages_dev, assign, 0, unroll=8)


def move_pages(outs_pages, capacity, order_ref, sources, outs, stage, load_sem, store_sem):
    loads, stores = [], []
    for source, key, r in sum(outs_pages, []):
        slot = len(loads)
        index = order_ref[key * capacity + r] if source == 0 else r
        copy = pltpu.make_async_copy(
            sources[source].at[index], stage.at[slot], load_sem.at[slot]
        )
        copy.start()
        loads.append(copy)
    slot = 0
    for n, pages in enumerate(outs_pages):
        count = len(pages)
        for copy in loads[slot : slot + count]:
            copy.wait()
        copy = pltpu.make_async_copy(stage.at[pl.ds(slot, count)], outs[n], store_sem.at[n])
        copy.start()
        stores.append(copy)
        slot += count
    for copy in stores:
        copy.wait()


def first_pack_kernel(
    devices, capacity, outs_pages, relative, units_ref, old_ref, pages_ref, *rest
):
    outs = rest[:-6]
    order_ref, slots, count, stage, load_sem, store_sem = rest[-6:]
    load_order(devices, capacity, relative, units_ref, old_ref, order_ref, slots, count)
    move_pages(
        outs_pages, capacity, order_ref, [pages_ref], outs, stage, load_sem, store_sem
    )


def next_pack_kernel(capacity, outs_pages, sources, order_ref, *rest):
    source_refs, outs = rest[:sources], rest[sources:-3]
    stage, load_sem, store_sem = rest[-3:]
    move_pages(
        outs_pages, capacity, order_ref, source_refs, outs, stage, load_sem, store_sem
    )


def pack_shapes(outs_pages, pages):
    total = sum(len(p) for p in outs_pages)
    shapes = [jax.ShapeDtypeStruct((len(p),) + pages.shape[1:], pages.dtype) for p in outs_pages]
    scratch = [
        pltpu.VMEM((total,) + pages.shape[1:], pages.dtype),
        pltpu.SemaphoreType.DMA((total,)),
        pltpu.SemaphoreType.DMA((len(outs_pages),)),
    ]
    return shapes, scratch


def first_pack(new_units, old_pages, pages, devices, capacity, outs_pages, relative):
    outs, scratch = pack_shapes(outs_pages, pages)
    result = pl.pallas_call(
        functools.partial(first_pack_kernel, devices, capacity, outs_pages, relative),
        out_shape=tuple(outs) + (jax.ShapeDtypeStruct((devices * capacity,), jnp.int32),),
        in_specs=[smem_spec(), smem_spec(), any_spec()],
        out_specs=tuple(any_spec() for _ in outs) + (smem_spec(),),
        scratch_shapes=[
            pltpu.SMEM(new_units.shape, jnp.int32),
            pltpu.SMEM((devices,), jnp.int32),
        ]
        + scratch,
        compiler_params=pltpu.CompilerParams(vmem_limit_bytes=VMEM_LIMIT),
        name="first_pack",
    )(new_units, old_pages, pages)
    return result[:-1], result[-1]


def next_pack(order, sources, capacity, outs_pages):
    outs, scratch = pack_shapes(outs_pages, sources[0])
    return pl.pallas_call(
        functools.partial(next_pack_kernel, capacity, outs_pages, len(sources)),
        out_shape=tuple(outs),
        in_specs=[smem_spec()] + [any_spec()] * len(sources),
        out_specs=tuple(any_spec() for _ in outs),
        scratch_shapes=scratch,
        compiler_params=pltpu.CompilerParams(vmem_limit_bytes=VMEM_LIMIT),
        name="next_pack",
    )(order, *sources)


def attend(query, keys, values, limit):
    scale = 1.0 / math.sqrt(HD)
    scores = (
        lax.dot_general(query, keys, (((1,), (1,)), ((), ())), preferred_element_type=jnp.float32)
        * scale
    )
    lane = lax.broadcasted_iota(jnp.int32, scores.shape, 1)
    weights = jnp.where(lane < limit, jnp.exp(scores), 0.0)
    total = jnp.sum(weights, axis=1, keepdims=True)
    weighted = jnp.dot(weights.astype(jnp.bfloat16), values, preferred_element_type=jnp.float32)
    return weighted, total


ALIGN = 16


def place_kernel(entries, started, attends, finish, late, *refs):
    refs = list(refs)
    table_ref, order_ref, length_ref, fresh_ref = refs[:4]
    refs = refs[4:]
    if attends:
        queries_ref = refs.pop(0)
        if started:
            weighted_in, total_in = refs.pop(0), refs.pop(0)
        part_ref = refs.pop(0) if late else None
    sources = 1 + max(source for source, _, _ in entries)
    source_refs, refs = refs[:sources], refs[sources:]
    if started:
        refs.pop(0)
    out_ref = refs.pop(0)
    if attends:
        weighted_ref, total_ref = refs.pop(0), refs.pop(0)
    attended_ref = refs.pop(0) if finish else None
    stage, load_sem, store_sem = refs
    if attends and started:
        weighted_ref[...] = weighted_in[...]
        total_ref[...] = total_in[...]
    loads = []
    for n, (source, index, _) in enumerate(entries):
        index = order_ref[index[0]] if isinstance(index, tuple) else index
        copy = pltpu.make_async_copy(
            source_refs[source].at[index], stage.at[n], load_sem.at[n]
        )
        copy.start()
        loads.append(copy)
    row = lax.broadcasted_iota(jnp.int32, (ALIGN, 2 * HD), 0)
    stores = []
    for n, (_, _, key) in enumerate(entries):
        w = table_ref[key[0]] if isinstance(key, tuple) else key
        unit, part = w // PER_UNIT, w % PER_UNIT
        length = length_ref[unit]
        loads[n].wait()
        for j in range(2):
            position = length + j

            @pl.when(position // PAGE == part)
            def _():
                inside = position % PAGE
                rows = pl.ds(pl.multiple_of(inside // ALIGN * ALIGN, ALIGN), ALIGN)
                block = stage[n, rows, :].astype(jnp.float32)
                token = fresh_ref[pl.ds(2 * unit + j, 1), :]
                block = jnp.where(row == inside % ALIGN, token, block)
                stage[n, rows, :] = block.astype(jnp.bfloat16)

        copy = pltpu.make_async_copy(stage.at[n], out_ref.at[w], store_sem.at[n])
        copy.start()
        stores.append(copy)
    if attends and not started:
        own_terms(queries_ref, fresh_ref, weighted_ref, total_ref)
    lane = lax.broadcasted_iota(jnp.int32, (QROWS, HD), 1)
    if late:
        sums = part_ref[len(late) * QROWS :, :].astype(jnp.float32)
    for n, at in enumerate(late):
        unit = table_ref[at] // PER_UNIT
        mine = (lane == 2 * n) | (lane == 2 * n + 1)
        total = jnp.sum(jnp.where(mine, sums, 0.0), axis=1, keepdims=True)
        weighted_ref[unit] += part_ref[n * QROWS : (n + 1) * QROWS, :].astype(jnp.float32)
        total_ref[unit] += jnp.broadcast_to(total, (QROWS, HD))
    group = 4
    for first in range(0, len(entries) if attends else 0, group):
        found = []
        for n in range(first, min(first + group, len(entries))):
            key = entries[n][2]
            w = table_ref[key[0]] if isinstance(key, tuple) else key
            unit, part = w // PER_UNIT, w % PER_UNIT
            weighted, total = attend(
                queries_ref[unit].astype(jnp.bfloat16),
                stage[n, :, :HD],
                stage[n, :, HD:],
                length_ref[unit] - part * PAGE,
            )
            found.append((unit, weighted, total))
        for unit, weighted, total in found:
            weighted_ref[unit] += weighted
            total_ref[unit] += jnp.broadcast_to(total, (QROWS, HD))
    if finish:
        attended_ref[...] = (weighted_ref[...] / total_ref[...]).astype(jnp.bfloat16)
    for copy in stores:
        copy.wait()


def own_terms(queries_ref, fresh_ref, weighted_ref, total_ref):
    scale = 1.0 / math.sqrt(HD)
    row = lax.broadcasted_iota(jnp.int32, (QROWS, 1), 0)
    for unit in range(U_DEV):
        query = queries_ref[unit]
        weighted = jnp.zeros((QROWS, HD), jnp.float32)
        total = jnp.zeros((QROWS, 1), jnp.float32)
        for j in range(2):
            at = 2 * unit + j
            key = fresh_ref[at : at + 1, :HD]
            value = fresh_ref[at : at + 1, HD:]
            score = jnp.sum(query * key, axis=1, keepdims=True) * scale
            weight = jnp.where(row >= j * GROUP, jnp.exp(score), 0.0)
            total = total + weight
            weighted = weighted + weight.astype(jnp.bfloat16).astype(jnp.float32) * value
        weighted_ref[unit] = weighted
        total_ref[unit] = jnp.broadcast_to(total, (QROWS, HD))


def place_pages(
    table, order, lengths, fresh, queries, sums, parts, late, sources, entries, cache, finish
):
    started, attends = cache is not None, queries is not None
    page_shape = sources[0].shape[1:]
    pages_dev = U_DEV * PER_UNIT
    args = [table, order, lengths, fresh]
    specs = [smem_spec()] * 3 + [vmem_spec()]
    if attends:
        vmem_args = [queries] + (list(sums) if started else []) + list(parts)
        args += vmem_args
        specs += [vmem_spec()] * len(vmem_args)
    args += list(sources)
    specs += [any_spec()] * len(sources)
    aliases = {}
    if started:
        aliases = {len(args): 0}
        args.append(cache)
        specs.append(any_spec())
    outs = [jax.ShapeDtypeStruct((pages_dev,) + page_shape, jnp.bfloat16)]
    out_specs = [any_spec()]
    if attends:
        outs += [jax.ShapeDtypeStruct((U_DEV, QROWS, HD), jnp.float32)] * 2
        out_specs += [vmem_spec()] * 2
    if finish:
        outs.append(jax.ShapeDtypeStruct((U_DEV, QROWS, HD), jnp.bfloat16))
        out_specs.append(vmem_spec())
    count = len(entries)
    result = pl.pallas_call(
        functools.partial(place_kernel, entries, started, attends, finish, late),
        out_shape=tuple(outs),
        in_specs=specs,
        out_specs=tuple(out_specs),
        input_output_aliases=aliases,
        scratch_shapes=[
            pltpu.VMEM((count,) + page_shape, jnp.bfloat16),
            pltpu.SemaphoreType.DMA((count,)),
            pltpu.SemaphoreType.DMA((count,)),
        ],
        compiler_params=pltpu.CompilerParams(vmem_limit_bytes=PLACE_LIMIT if started else VMEM_LIMIT),
        name="place_pages",
    )(*args)
    return result[0], result[1:3], result[3] if finish else None


def rows_kernel(
    late,
    units_ref,
    turn_ref,
    order_ref,
    ids_ref,
    lengths_ref,
    rows_ref,
    cosine_ref,
    sine_ref,
    pages_ref,
    passed_ref,
    queries_ref,
    fresh_ref,
    part_ref,
    stage,
    load_sem,
):
    device = lax.axis_index("tp")
    devices, _, width = rows_ref.shape
    pieces = (GROUP + 2) * HD // width
    half_dim = HD // 2
    row = lax.broadcasted_iota(jnp.int32, rows_ref.shape[1:], 0)
    lane = lax.broadcasted_iota(jnp.int32, (QROWS, HD), 1)

    def unit_rows(unit):
        request, head = unit // KVH, unit % KVH
        found = []
        for piece in range(pieces):
            place = turn_ref[(head * pieces + piece) ^ device]
            block = rows_ref[place].astype(jnp.float32)
            picked = [
                jnp.sum(jnp.where(row == 2 * request + j, block, 0.0), axis=0, keepdims=True)
                for j in range(2)
            ]
            for at in range(0, width, HD):
                found.append([line[:, at : at + HD] for line in picked])
        turned = []
        for j in range(2):
            heads = jnp.concatenate([head[j] for head in found[: GROUP + 1]], axis=0)
            swapped = jnp.concatenate([heads[:, half_dim:], heads[:, :half_dim]], axis=1)
            cosine = cosine_ref[pl.ds(2 * request + j, 1), :]
            sine = sine_ref[pl.ds(2 * request + j, 1), :]
            heads = heads * cosine + swapped * sine
            turned.append(heads.astype(jnp.bfloat16).astype(jnp.float32))
        return turned, [found[GROUP + 1][j] for j in range(2)]

    loads = []
    for slot, (source, at) in enumerate(late):
        page = pages_ref.at[order_ref[at]] if source == 0 else passed_ref.at[at]
        copy = pltpu.make_async_copy(page, stage.at[slot], load_sem.at[slot])
        copy.start()
        loads.append(copy)
    sums = jnp.zeros((QROWS, HD), jnp.float32)
    for slot in range(len(late)):
        page = ids_ref[slot]
        unit = page // PER_UNIT
        limit = lengths_ref[unit // KVH] - (page % PER_UNIT) * PAGE
        turned, _ = unit_rows(unit)
        query = jnp.concatenate([turned[0][:GROUP], turned[1][:GROUP]], axis=0)
        loads[slot].wait()
        weighted, total = attend(
            query.astype(jnp.bfloat16), stage[slot, :, :HD], stage[slot, :, HD:], limit
        )
        part_ref[slot * QROWS : (slot + 1) * QROWS, :] = weighted.astype(jnp.bfloat16)
        high = total.astype(jnp.bfloat16).astype(jnp.float32)
        sums = jnp.where(lane == 2 * slot, high, sums)
        sums = jnp.where(lane == 2 * slot + 1, total - high, sums)
    part_ref[len(late) * QROWS :, :] = sums.astype(jnp.bfloat16)
    for slot in range(U_DEV):
        turned, values = unit_rows(units_ref[slot])
        for j in range(2):
            at = 2 * slot + j
            queries_ref[slot, j * GROUP : (j + 1) * GROUP, :] = turned[j][:GROUP]
            fresh_ref[at : at + 1, :HD] = turned[j][GROUP:]
            fresh_ref[at : at + 1, HD:] = values[j]


def rows_and_parts(units, turn, order, ids, lengths, rows, cosine, sine, pages, passed, late):
    return pl.pallas_call(
        functools.partial(rows_kernel, late),
        out_shape=(
            jax.ShapeDtypeStruct((U_DEV, QROWS, HD), jnp.float32),
            jax.ShapeDtypeStruct((2 * U_DEV, 2 * HD), jnp.float32),
            jax.ShapeDtypeStruct(((len(late) + 1) * QROWS, HD), jnp.bfloat16),
        ),
        in_specs=[smem_spec()] * 5 + [vmem_spec()] * 3 + [any_spec()] * 2,
        out_specs=(vmem_spec(),) * 3,
        scratch_shapes=[
            pltpu.VMEM((len(late),) + pages.shape[1:], pages.dtype),
            pltpu.SemaphoreType.DMA((len(late),)),
        ],
        compiler_params=pltpu.CompilerParams(vmem_limit_bytes=VMEM_LIMIT),
        name="rows_and_parts",
    )(units, turn, order, ids, lengths, rows, cosine, sine, pages, passed)


def swap(values, key, devices):
    return lax.ppermute(values, "tp", [(i, i ^ key) for i in range(devices)])


def gather_line(values, devices):
    values = values[None]
    step = devices // 2
    keys = [step // 2, step, step + step // 2]
    found = [swap(values, k, devices) for k in keys]
    return jnp.concatenate([values] + found, axis=0), [0] + keys


def gather_more(values, span, step, devices):
    values = jnp.concatenate([values, swap(values, step, devices)], axis=0)
    return values, span + [s ^ step for s in span]


def after(value, *others):
    return lax.optimization_barrier((value,) + others)[0]


def body(hidden_states, qkv_weight, out_weight, cache_pages, context_lengths, new_units, old_pages):
    devices = lax.axis_size("tp")
    device = lax.axis_index("tp")
    requests = hidden_states.shape[0]
    pages_dev, page_rows, page_width = cache_pages.shape
    capacity = max(1, pages_dev // devices)
    total_units = new_units.shape[0]
    total_pages = old_pages.shape[0]
    pairwise = devices == 2 * KVH

    def own(*keys):
        return [(0, key, r) for key in keys for r in range(capacity)]

    def passed(source, piece):
        return [(source, 0, piece * capacity + r) for r in range(capacity)]

    def piece(chunk, n):
        return chunk[n * capacity : (n + 1) * capacity]

    def send(chunk, key):
        return swap(chunk, key, devices)

    if pairwise:
        half, quarter = devices // 2, devices // 4
        a, b = half, half + quarter
        c, d = a + 2, b + 2
        near = list(range(2, half, 2))
        (chunk_a, cross_near), order = first_pack(
            new_units,
            old_pages,
            cache_pages,
            devices,
            capacity,
            [own(a), own(1, *[k + 1 for k in near])],
            True,
        )
        moved_a, cross_near = send(chunk_a, a), send(cross_near, 1)
        chunk_4, chunk_6, chunk_b, cross_far = next_pack(
            order,
            [cache_pages, cross_near],
            capacity,
            [
                own(near[1]) + passed(1, 2),
                own(near[2]) + passed(1, 3),
                own(b),
                own(a + 1, b + 1, c + 1, d + 1),
            ],
        )
        moved_4, moved_6 = send(chunk_4, near[1]), send(chunk_6, near[2])
        moved_b, cross_far = send(chunk_b, b), send(cross_far, 1)
    else:
        (packed,), order = first_pack(
            new_units, old_pages, cache_pages, devices, capacity, [own(*range(devices))], False
        )
        arrived = lax.all_to_all(
            packed.reshape(devices, capacity, page_rows, page_width),
            "tp",
            split_axis=0,
            concat_axis=0,
            tiled=True,
        ).reshape(devices * capacity, page_rows, page_width)

    own_units = lax.dynamic_slice_in_dim(new_units, device * U_DEV, U_DEV)
    own_lengths = context_lengths[own_units // KVH]
    wanted = (
        own_units[:, None] * PER_UNIT + jnp.arange(PER_UNIT, dtype=jnp.int32)[None, :]
    ).reshape(pages_dev)
    source_pos = jnp.sum(
        jnp.where(
            wanted[:, None] == old_pages[None, :],
            jnp.arange(total_pages, dtype=jnp.int32)[None, :],
            0,
        ),
        axis=1,
    )
    source_dev = source_pos // pages_dev
    rank = jnp.sum(
        (
            (source_dev[:, None] == source_dev[None, :])
            & (source_pos[None, :] < source_pos[:, None])
        ).astype(jnp.int32),
        axis=1,
    )
    if pairwise:
        where = (source_dev ^ device) * capacity + rank
        spots = jnp.arange(devices * capacity, dtype=jnp.int32)
        slots = jnp.arange(pages_dev, dtype=jnp.int32)
        table = jnp.sum(jnp.where(where[None, :] == spots[:, None], slots[None, :], 0), axis=1)
    else:
        table = source_dev * capacity + rank

    flat_rows = hidden_states.reshape(requests * 2, D)
    if pairwise:
        flat_rows = after(flat_rows, cross_far)
    own_part = lax.dot_general(
        flat_rows, qkv_weight, (((1,), (1,)), ((), ())), preferred_element_type=jnp.float32
    ).astype(jnp.bfloat16)
    if pairwise:
        new_units, old_pages, _ = lax.optimization_barrier((new_units, old_pages, own_part))
    slot_index = jnp.sum(
        jnp.where(
            new_units[None, :] == jnp.arange(total_units, dtype=jnp.int32)[:, None],
            jnp.arange(total_units, dtype=jnp.int32)[None, :],
            0,
        ),
        axis=1,
    )
    if pairwise:
        ids = old_pages.reshape(devices, 1, pages_dev)
        ids = jnp.concatenate([ids[device], ids[device ^ 1]], axis=0)
        reached = jnp.sum(
            jnp.where(
                (ids // PER_UNIT)[..., None] == new_units, jnp.arange(total_units) // U_DEV, 0
            ),
            axis=-1,
        )
        chosen = reached == (device ^ d)
        earlier = jnp.arange(pages_dev)[None, :] < jnp.arange(pages_dev)[:, None]
        ranks = jnp.sum((chosen[:, None, :] & earlier[None]).astype(jnp.int32), axis=-1)
        wants = jnp.arange(capacity, dtype=jnp.int32)[None, :, None]
        picked = chosen[:, None, :] & (ranks[:, None, :] == wants)
        late_ids = jnp.sum(jnp.where(picked, ids[:, None, :], 0), axis=-1)
        late_ids = late_ids.reshape(2 * capacity).astype(jnp.int32)
    if pairwise:
        positions = context_lengths[:, None] + jnp.arange(2, dtype=jnp.int32)[None, :]
        cosine, sine = rope_tables(positions.reshape(2 * requests))
        rows, span = gather_line(own_part, devices)
        moved_a2 = send(after(piece(cross_far, 0), own_part, moved_a), a)
        moved_b2 = send(after(piece(cross_far, 1), own_part), b)
        rows, span = gather_more(after(rows, moved_a, moved_b), span, 2, devices)
        rows, span = gather_more(rows, span, 1, devices)
        turn = jnp.array([span.index(i) for i in range(devices)], jnp.int32)
        late = [(0, d * capacity + r) for r in range(capacity)]
        late += [(1, 3 * capacity + r) for r in range(capacity)]
        places = [key * capacity + r for key in (d, d + 1) for r in range(capacity)]
        queries, fresh, sent = rows_and_parts(
            own_units,
            turn,
            order,
            late_ids,
            context_lengths,
            rows,
            cosine,
            sine,
            cache_pages,
            cross_far,
            late,
        )
        parts = [send(sent, d)]
        chunk_c, chunk_d, chunk_2 = next_pack(
            order,
            [cache_pages, after(cross_far, rows), cross_near],
            capacity,
            [own(c) + passed(1, 2), own(d), own(near[0]) + passed(2, 1)],
        )
        moved_2 = send(chunk_2, near[0])
        moved_c = send(after(chunk_c, moved_a2, sent), c)

        def place(groups, sums, cache, attends, parts, finish):
            entries, sources = [], []
            for array, keys, first in groups:
                for n, key in enumerate(keys):
                    for r in range(capacity):
                        at = (r,) if array is cache_pages else first + n * capacity + r
                        entries.append((len(sources), at, (key * capacity + r,)))
                sources.append(array)
            return place_pages(
                table,
                order,
                own_lengths,
                fresh,
                queries if attends else None,
                sums,
                parts,
                places if parts else [],
                sources,
                entries,
                cache,
                finish,
            )

        new_cache, sums, _ = place(
            [(cache_pages, [0], 0), (cross_near, [1], 0), (moved_a, [a], 0), (moved_b, [b], 0)],
            None,
            None,
            True,
            [],
            False,
        )
        new_cache, sums, _ = place(
            [(moved_4, [near[1], near[1] + 1], 0), (moved_6, [near[2], near[2] + 1], 0)],
            sums,
            new_cache,
            True,
            [],
            False,
        )
        new_cache, sums, _ = place(
            [(moved_a2, [a + 1], 0), (moved_b2, [b + 1], 0), (moved_2, [near[0], near[0] + 1], 0)],
            sums,
            new_cache,
            True,
            [],
            False,
        )
        moved_d = send(after(chunk_d, moved_b2, sums[0], parts[0]), d)
        new_cache, sums, attended = place(
            [(moved_c, [c, c + 1], 0)], sums, new_cache, True, parts, True
        )
        attended = after(attended, moved_d)
        moved_d2 = send(after(piece(cross_far, 3), attended), d)
        new_cache, _, _ = place([(moved_d, [d], 0)], None, new_cache, False, [], False)
        new_cache, _, _ = place([(moved_d2, [d + 1], 0)], None, new_cache, False, [], False)
    else:
        own_requests, own_heads = own_units // KVH, own_units % KVH
        positions = own_lengths[:, None] + jnp.arange(2, dtype=jnp.int32)[None, :]
        cosine, sine = rope_tables(positions.reshape(2 * U_DEV))
        rows = lax.all_gather(own_part, "tp", axis=1, tiled=True)
        rows = rows.reshape(requests, 2, KVH, GROUP + 2, HD)
        rows = rows[own_requests, :, own_heads].astype(jnp.float32)
        turned = rotate(
            rows[:, :, : GROUP + 1],
            cosine.reshape(U_DEV, 2, 1, HD),
            sine.reshape(U_DEV, 2, 1, HD),
        )
        queries = turned[:, :, :GROUP].reshape(U_DEV, QROWS, HD)
        fresh = jnp.concatenate([turned[:, :, GROUP], rows[:, :, GROUP + 1]], axis=-1)
        fresh = fresh.reshape(2 * U_DEV, 2 * HD).astype(jnp.bfloat16).astype(jnp.float32)
        queries = queries.astype(jnp.bfloat16).astype(jnp.float32)
        entries = [(0, (w,), w) for w in range(pages_dev)]
        new_cache, sums, attended = place_pages(
            table,
            table,
            own_lengths,
            fresh,
            queries,
            None,
            [],
            [],
            [arrived],
            entries,
            None,
            True,
        )

    attended = attended.reshape(U_DEV, 2, GROUP * HD)
    if pairwise:
        heads, span = gather_line(attended, devices)
        heads, span = gather_more(heads, span, 2, devices)
        heads, span = gather_more(heads, span, 1, devices)
        holder = turn[(slot_index // U_DEV) ^ device]
        heads = heads.reshape(total_units, 2, GROUP * HD)[holder * U_DEV + slot_index % U_DEV]
    else:
        heads = lax.all_gather(attended, "tp", axis=0, tiled=True)[slot_index]
    logical = (
        heads.reshape(requests, KVH, 2, GROUP * HD)
        .transpose(0, 2, 1, 3)
        .reshape(requests * 2, HEADS * HD)
    )
    mixed_rows = lax.dot_general(
        logical, out_weight, (((1,), (1,)), ((), ())), preferred_element_type=jnp.float32
    )
    mixed_rows = mixed_rows.astype(jnp.bfloat16).reshape(requests, 2, out_weight.shape[0])
    return (mixed_rows, new_cache)


def solution(mesh):
    in_specs = (
        P("group", None, None),
        P("tp", None),
        P("tp", None),
        P(("group", "tp"), None, None),
        P("group"),
        P("group"),
        P("group"),
    )
    out_specs = (P("group", None, "tp"), P(("group", "tp"), None, None))
    return jax.shard_map(body, mesh=mesh, in_specs=in_specs, out_specs=out_specs, check_vma=False)
```
